32 devices in a mesh: slab: 16 (over z, y, x), grp: 2 (over core).
Axes of the slice: x: 2, y: 2, z: 4, core: 2. Of those that a mesh axis runs over, the one named last changes fastest.
Arguments:
- saturation: float32 [32, 64, 256], P(('slab', 'grp')), may hold values from 0.5 to 3
- inlet_mask: int32 [32, 64, 256], P(('slab', 'grp')), may hold values 0 or 1
- crystal_size: float32 [131072], P(('slab', 'grp')), may hold values from 0.5 to 2
- crystal_weight: float32 [131072], P(('slab', 'grp')), may hold values from 0.3 to 3
- crystal_cell: int32 [131072], P(('slab', 'grp')), may hold values from 0 to 32767
- live_count: int32 [32], P(('slab', 'grp')), may hold values from 1024 to 4096, as said below
- nucleus_cell: int32 [32, 4, 512], P(('slab', 'grp')), may hold values from 0 to 32767
- nucleus_count: int32 [32, 4, 512], P(('slab', 'grp')), may hold values from 1 to 8
- migrant_rows: int32 [32, 2, 512], P(('slab', 'grp')), may hold values from 0 to 4095, as said below
- migrant_count: int32 [32, 2], P(('slab', 'grp')), may hold values from 0 to 512
Outputs:
- saturation_out: float32 [32, 64, 256], P(('slab', 'grp'))
- size_out: float32 [131072], P(('slab', 'grp'))
- arrivals: float32 [32, 2, 2, 512], P(('slab', 'grp'))
The draws below stay inside these ranges and needn't reach their ends.
Inputs may be any that keep to these rules, and one draw needn't show every extreme that they name: `live_count`: about a quarter of the devices hold exactly 4096 live rows, the others a quarter to a third of that. `migrant_rows`: rows of the device's own parcels below its live count, all distinct; the list toward the lower slab lies in the lower half of the live rows, the other in the upper half.
All inputs are finite; a program needn't handle non-finite values. No bound on the sum of `inlet_mask` on one device may be relied on, other than what follows from the above.
Results may differ from the reference program's by a relative error of at most 0.00007.
Values sent between devices are 32-bit elements; how exact they have to be, the bound alone decides.
No kernel may reach another device: no remote copies, remote signals or barrier semaphores. Data moves between devices by JAX's collectives and lax.ppermute only.
A program may use at most 64 MiB of HBM per device.

```python
import math
import jax
import jax.numpy as jnp

PL = 1
NY = 64
NZ = 256
P_SIZE = 4096
MIG = 512
NEV = 512
STEPS = 2
SUBS = 2
DEVS = 32
NX = 32
N_SLAB = 16
N_GRP = 2


def live_counts(key):
    base = jax.random.randint(jax.random.fold_in(key, 11), (DEVS,), P_SIZE // 4, P_SIZE // 3 + 1)
    order = jax.random.permutation(jax.random.fold_in(key, 12), DEVS)
    return jnp.where(order < max(DEVS // 4, 1), P_SIZE, base).astype(jnp.int32)


def draw_live_count(key, part):
    return live_counts(key)


def draw_migrant_rows(key, part):
    totals = live_counts(key)[:, None]
    lower = totals // 2
    upper = totals - lower
    slots = jnp.arange(MIG).astype(jnp.int32)[None, :]
    lower_off = jax.random.randint(jax.random.fold_in(key, 13), (DEVS, MIG), 0, jnp.maximum(lower // MIG, 1))
    upper_off = jax.random.randint(jax.random.fold_in(key, 14), (DEVS, MIG), 0, jnp.maximum(upper // MIG, 1))
    toward_lower = slots * lower // MIG + lower_off
    toward_upper = lower + slots * upper // MIG + upper_off
    toward_upper = jnp.where(slots == MIG - 1, totals - 1, toward_upper)
    return jnp.stack([toward_lower, toward_upper], axis=1).astype(jnp.int32)


def draw_migrant_count(key, part):
    counts = jax.random.randint(jax.random.fold_in(key, 15), (DEVS, 2), 0, MIG + 1)
    order = jax.random.permutation(jax.random.fold_in(key, 16), DEVS)[:, None]
    return jnp.where(order < max(DEVS // 8, 1), MIG, counts).astype(jnp.int32)


def with_ends(array, key, low, top_value):
    spot = [jax.random.randint(jax.random.fold_in(key, axis), (), 0, length) for axis, length in enumerate(array.shape)]
    longest = array.shape.index(max(array.shape))
    beside = spot[:longest] + [(spot[longest] + 1) % array.shape[longest]] + spot[longest + 1:]
    return array.at[tuple(spot)].set(low).at[tuple(beside)].set(top_value)


def block_scale(rng, extent, split, least, largest):
    gain = 1.0
    for position, parts in split:
        steps = jax.random.uniform(jax.random.fold_in(jax.random.fold_in(rng, 6), position), (parts,), jnp.float32, least / len(split), largest / len(split))
        gain = gain * jnp.repeat(jnp.exp(steps), extent[position] // parts).reshape((-1,) + (1,) * (len(extent) - 1 - position))
    return gain


def setup_inputs(seed: int = 0) -> dict:
    seeds = jax.random.split(jax.random.key(seed), 11)
    return {
        "saturation": jnp.clip(0.5 + 2.5 * jax.random.uniform(seeds[0], (NX, NY, NZ), jnp.float32) ** block_scale(seeds[0], (NX, NY, NZ), ((0, 32),), -0.2, 0.2), 0.5, 3.0),
        "inlet_mask": with_ends((jax.random.randint(seeds[1], (NX, NY, NZ), 0, 16) < 1).astype(jnp.int32), jax.random.fold_in(seeds[1], 1), 0, 1),
        "crystal_size": jnp.clip(jnp.exp(math.log(2.0) - 1.3862944 * jax.random.uniform(seeds[2], (DEVS * P_SIZE,), jnp.float32) ** block_scale(seeds[2], (DEVS * P_SIZE,), ((0, 32),), -0.2, 0.2)), 0.5, 2.0),
        "crystal_weight": jnp.clip(jnp.exp(math.log(3.0) - 2.3025851 * jax.random.uniform(seeds[3], (DEVS * P_SIZE,), jnp.float32) ** block_scale(seeds[3], (DEVS * P_SIZE,), ((0, 32),), -0.2, 0.2)), 0.3, 3.0),
        "crystal_cell": with_ends(jax.random.randint(seeds[4], (DEVS * P_SIZE,), 0, N_GRP * PL * NY * NZ), jax.random.fold_in(seeds[4], 1), 0, (N_GRP * PL * NY * NZ) - 1).astype(jnp.int32),
        "live_count": draw_live_count(jax.random.fold_in(seeds[10], 71), 0),
        "nucleus_cell": with_ends(jax.random.randint(seeds[6], (DEVS, STEPS * SUBS, NEV), 0, N_GRP * PL * NY * NZ), jax.random.fold_in(seeds[6], 1), 0, (N_GRP * PL * NY * NZ) - 1).astype(jnp.int32),
        "nucleus_count": with_ends(jax.random.randint(seeds[7], (DEVS, STEPS * SUBS, NEV), 1, 9), jax.random.fold_in(seeds[7], 1), 1, 8).astype(jnp.int32),
        "migrant_rows": draw_migrant_rows(jax.random.fold_in(seeds[10], 71), 0),
        "migrant_count": draw_migrant_count(jax.random.fold_in(seeds[10], 71), 0),
    }


GROWTH = 0.08
VOLUME = 1.0
NUCLEATE = 0.02
DIFFUSE = 0.12
INLET = 4.0


def transport(padded_x, inlet_weight):
    field_mid = padded_x[1:-1]
    padded_yz = jnp.pad(field_mid, ((0, 0), (1, 1), (1, 1)))
    beside = padded_x[2:] + padded_x[:-2]
    beside = beside + padded_yz[:, 2:, 1:-1] + padded_yz[:, :-2, 1:-1]
    beside = beside + padded_yz[:, 1:-1, 2:] + padded_yz[:, 1:-1, :-2]
    field_mid = field_mid + DIFFUSE * (beside - 6.0 * field_mid)
    return field_mid + inlet_weight * (INLET - field_mid)


def reference(saturation, inlet_mask, crystal_size, crystal_weight, crystal_cell, live_count, nucleus_cell, nucleus_count, migrant_rows, migrant_count):
    devices = N_SLAB * N_GRP
    slab_cells = N_GRP * PL * NY * NZ
    slab_of = jnp.arange(devices).astype(jnp.int32) // N_GRP
    offsets = (slab_of * slab_cells).astype(jnp.int32)
    global_cell = (crystal_cell.reshape(devices, P_SIZE) + offsets[:, None]).reshape(-1).astype(jnp.int32)
    row_index = jnp.arange(P_SIZE).astype(jnp.int32)
    active = (row_index[None, :] < live_count[:, None]).astype(jnp.float32).reshape(-1)
    nucleus_global = (nucleus_cell + offsets[:, None, None]).astype(jnp.int32)
    inlet_weight = inlet_mask.astype(jnp.float32)
    crystal = crystal_size
    field = saturation
    for step_index in range(STEPS):
        for sub_index in range(SUBS):
            substep = step_index * SUBS + sub_index
            flat = field.reshape(-1)
            local_sat = flat[global_cell]
            enlarged = crystal + active * GROWTH * jax.nn.softplus(local_sat - 1.0)
            consumed = active * crystal_weight * VOLUME * (enlarged * enlarged * enlarged - crystal * crystal * crystal)
            event_cell = nucleus_global[:, substep, :].reshape(-1)
            event_mass = nucleus_count[:, substep, :].reshape(-1).astype(jnp.float32) * NUCLEATE * jax.nn.softplus(flat[event_cell] - 1.0)
            deposit = jnp.zeros_like(flat).at[global_cell].add(consumed).at[event_cell].add(event_mass)
            field = (flat - deposit).reshape(field.shape)
            crystal = enlarged
        field = transport(jnp.pad(field, ((1, 1), (0, 0), (0, 0))), inlet_weight)
    size_out = active * crystal
    rows = (migrant_rows + (jnp.arange(devices).astype(jnp.int32) * P_SIZE)[:, None, None]).astype(jnp.int32)
    sent = jnp.stack([size_out[rows], crystal_weight[rows]], axis=2)
    slot_live = (jnp.arange(MIG).astype(jnp.int32)[None, None, :] < migrant_count[:, :, None]).astype(jnp.float32)
    sent = (sent * slot_live[:, :, None, :]).reshape(N_SLAB, N_GRP, 2, 2, MIG)
    empty = jnp.zeros_like(sent[:1])
    from_lower = jnp.concatenate([empty, sent[:-1]], axis=0)[:, :, 1]
    from_upper = jnp.concatenate([sent[1:], empty], axis=0)[:, :, 0]
    arrivals = jnp.stack([from_lower, from_upper], axis=2).reshape(devices, 2, 2, MIG)
    return field, size_out, arrivals
```

```python
import functools

import jax
import jax.numpy as jnp
from jax import lax
from jax.experimental import pallas as pl
from jax.experimental.pallas import tpu as pltpu
from jax.sharding import PartitionSpec as P

STEPS = 2
SUBS = 2

GROWTH = 0.08
NUCLEATE = 0.02
DIFFUSE = 0.12
INLET = 4.0

LANES = 128
F32 = jnp.float32
BF16 = jnp.bfloat16
NT = (((1,), (1,)), ((), ()))
NN = (((1,), (0,)), ((), ()))


def softplus(x):
    return jnp.maximum(x, 0.0) + jnp.log1p(jnp.exp(-jnp.abs(x)))


def pieces(x):
    high = x.astype(BF16)
    return high, (x - high.astype(F32)).astype(BF16)


def hot(count, row):
    width = row.shape[1]
    index = lax.broadcasted_iota(jnp.int32, (count, width), 0)
    return jnp.where(index == row, 1.0, 0.0).astype(BF16)


def moments_kernel(away, size, weight, cell, live, event_cell, event_count, out, left, right, event_left):
    rows = size.shape[0]
    lines, places = out.shape[1:]
    plane = lax.axis_index("grp")
    plane = 1 - plane if away else plane
    first_line = plane * lines
    number = lax.broadcasted_iota(jnp.int32, size.shape, 0) * LANES + lax.broadcasted_iota(jnp.int32, size.shape, 1)
    sizes = size[...]
    zeroth = jnp.where(number < live[0], weight[...], 0.0)
    first = zeroth * sizes
    second = first * sizes
    parts = [part for moment in (zeroth, first, second) for part in pieces(moment)]
    parts = [part.astype(F32) for part in parts]
    cells = cell[...]
    line = cells // places - first_line
    place = cells % places
    for r in range(rows):
        where = pl.ds(r * LANES, LANES)
        hot_line = hot(lines, line[r : r + 1])
        for c, part in enumerate(parts):
            left[pl.ds(c * lines, lines), where] = hot_line * part[r : r + 1].astype(BF16)
        right[:, where] = hot(places, place[r : r + 1])
    sums = lax.dot_general(left[...], right[...], NT, preferred_element_type=F32)
    for c in range(3):
        out[c] = sums[2 * c * lines : (2 * c + 1) * lines] + sums[(2 * c + 1) * lines : (2 * c + 2) * lines]
    for k in range(STEPS * SUBS):
        cells = event_cell[0, pl.ds(k, 1), :]
        counts = event_count[0, pl.ds(k, 1), :].astype(F32).astype(BF16)
        hot_line = hot(lines, cells // places - first_line) * counts
        out[3 + k] = lax.dot_general(hot_line, hot(places, cells % places), NT, preferred_element_type=F32)


def moments(away, size, weight, cell, live, event_cell, event_count, plane_shape):
    parcels = size.shape[0] * size.shape[1]
    lines, places = plane_shape
    return pl.pallas_call(
        functools.partial(moments_kernel, away),
        out_shape=jax.ShapeDtypeStruct((3 + STEPS * SUBS, lines, places), F32),
        in_specs=[pl.BlockSpec(memory_space=pltpu.VMEM)] * 3
        + [pl.BlockSpec(memory_space=pltpu.SMEM)]
        + [pl.BlockSpec(memory_space=pltpu.VMEM)] * 2,
        out_specs=pl.BlockSpec(memory_space=pltpu.VMEM),
        scratch_shapes=[
            pltpu.VMEM((6 * lines, parcels), BF16),
            pltpu.VMEM((places, parcels), BF16),
            pltpu.VMEM((lines, event_cell.shape[2]), BF16),
        ],
        compiler_params=pltpu.CompilerParams(vmem_limit_bytes=32 << 20),
        cost_estimate=pl.CostEstimate(flops=2 * 6 * lines * parcels * places, bytes_accessed=1 << 19, transcendentals=0),
        name="moments_away" if away else "moments_home",
    )(size, weight, cell, live, event_cell, event_count)


def substep(field, zeroth, first, second, counts, grown):
    rate = softplus(field - 1.0)
    growth = GROWTH * rate
    taken = growth * (3.0 * second + growth * (3.0 * first + growth * zeroth))
    field = field - (taken + counts * (NUCLEATE * rate))
    second = second + growth * (2.0 * first + growth * zeroth)
    first = first + growth * zeroth
    return field, first, second, grown + growth


def first_kernel(field, home, away, out, state):
    total = [home[c] + away[c] for c in range(home.shape[0])]
    zeroth, first, second = total[:3]
    now, grown = field[0], jnp.zeros_like(field[0])
    for k in range(SUBS):
        now, first, second, grown = substep(now, zeroth, first, second, total[3 + k], grown)
    out[0] = now
    for c, value in enumerate([zeroth, first, second, grown] + total[3 + SUBS :]):
        state[c] = value


def moved(field):
    lines, places = field.shape
    line = lax.broadcasted_iota(jnp.int32, field.shape, 0)
    place = lax.broadcasted_iota(jnp.int32, field.shape, 1)
    total = jnp.where(line == 0, 0.0, pltpu.roll(field, 1, 0))
    total += jnp.where(line == lines - 1, 0.0, pltpu.roll(field, lines - 1, 0))
    total += jnp.where(place == 0, 0.0, pltpu.roll(field, 1, 1))
    total += jnp.where(place == places - 1, 0.0, pltpu.roll(field, places - 1, 1))
    return total


def transport(field, beside, other, inlet):
    around = beside + other + moved(field)
    field = field + DIFFUSE * (around - 6.0 * field)
    return field + inlet * (INLET - field)


def second_kernel(field, beside, other, inlet, state, out):
    now = transport(field[0], beside[0], other[0], inlet[0].astype(F32))
    zeroth, first, second, grown = (state[c] for c in range(4))
    for k in range(SUBS):
        now, first, second, grown = substep(now, zeroth, first, second, state[4 + k], grown)
    out[0] = now
    out[1] = grown


def third_kernel(planes, received, partner, inlet, out):
    lines = out.shape[1]
    out[0] = transport(planes[0], received[pl.ds(0, lines)], partner[0], inlet[0].astype(F32))


def migrants_kernel(size, weight, cell, rows, count, keep, send):
    side = lax.axis_index("grp")
    table_rows = size.shape[0]
    slots = rows.shape[2]
    places = 256
    sizes, weights, cells = size[...], weight[...], cell[...]
    table = []
    for values in (sizes, weights):
        rest = values
        for _ in range(3):
            part = rest.astype(BF16)
            rest = rest - part.astype(F32)
            table.append(part)
    table += [(cells // places).astype(F32).astype(BF16), (cells % places).astype(F32).astype(BF16)]
    table = jnp.concatenate(table, axis=1)
    slot = lax.broadcasted_iota(jnp.int32, (1, slots), 1)
    for out, j in ((keep, side), (send, 1 - side)):
        row = jnp.where(j == 0, rows[0, 0:1, :], rows[0, 1:2, :])
        valid = jnp.where(slot < count[0, j], 1.0, 0.0)
        hot_row = hot(table_rows, row // LANES)
        picked = lax.dot_general(table, hot_row, (((0,), (0,)), ((), ())), preferred_element_type=F32)
        hot_lane = hot(LANES, row % LANES).astype(F32)
        found = [
            jnp.sum(picked[c * LANES : (c + 1) * LANES] * hot_lane, axis=0, keepdims=True) for c in range(8)
        ]
        out[0:1] = (found[0] + found[1] + found[2]) * valid
        out[1:2] = (found[3] + found[4] + found[5]) * valid
        out[2:3] = found[6]
        out[3:4] = found[7]
        out[4:5] = valid
        out[5:8] = jnp.zeros((3, slots), F32)


def grown_at(stacked, line, place):
    lines = stacked.shape[0] // 2
    picked = lax.dot_general(stacked, hot(stacked.shape[1], place), NN, preferred_element_type=F32)
    picked = picked[:lines] + picked[lines:]
    index = lax.broadcasted_iota(jnp.int32, picked.shape, 0)
    return jnp.sum(jnp.where(index == line, picked, 0.0), axis=0, keepdims=True)


def both_planes(mine, partner):
    side = lax.axis_index("grp")
    low = jnp.where(side == 0, mine, partner)
    high = jnp.where(side == 0, partner, mine)
    whole = jnp.concatenate([low, high], axis=0)
    return jnp.concatenate(pieces(whole), axis=0)


def leaving_kernel(planes, partner, kept, taken, out):
    lines, places = planes.shape[1:]
    stacked = both_planes(planes[1], partner[1])
    out[pl.ds(0, lines)] = planes[0]
    at = lines
    for part in (kept, taken):
        grown = grown_at(stacked, part[2:3].astype(jnp.int32), part[3:4].astype(jnp.int32))
        sizes = part[0:1] + grown * part[4:5]
        for row in (sizes, part[1:2]):
            for first in range(0, row.shape[1], places):
                out[at : at + 1] = row[:, first : first + places]
                at += 1


def sizes_kernel(planes, partner, size, cell, live, out):
    places = planes.shape[2]
    stacked = both_planes(planes[1], partner[1])
    cells = cell[...]
    line = cells // places
    place = cells % places
    number = lax.broadcasted_iota(jnp.int32, size.shape, 0) * LANES + lax.broadcasted_iota(jnp.int32, size.shape, 1)
    sizes = size[...]
    active = number < live[0]
    group = 4
    for r in range(0, size.shape[0], group):
        lines_now = jnp.concatenate([line[r + i : r + i + 1] for i in range(group)], axis=1)
        places_now = jnp.concatenate([place[r + i : r + i + 1] for i in range(group)], axis=1)
        grown = grown_at(stacked, lines_now, places_now)
        for i in range(group):
            out[r + i : r + i + 1] = grown[:, i * LANES : (i + 1) * LANES]
    out[...] = jnp.where(active, sizes + out[...], 0.0)


def arrivals_kernel(mine, relayed, out):
    side = lax.axis_index("grp")
    places = mine.shape[1]
    slots = out.shape[3]
    parts = slots // places
    for v in range(2):
        for p in range(parts):
            where = pl.ds(p * places, places)
            own = mine[v * parts + p : v * parts + p + 1]
            other = relayed[v * parts + p : v * parts + p + 1]
            out[0, 0, v : v + 1, where] = jnp.where(side == 0, own, other)
            out[0, 1, v : v + 1, where] = jnp.where(side == 0, other, own)


VMEM = pl.BlockSpec(memory_space=pltpu.VMEM)
SMEM = pl.BlockSpec(memory_space=pltpu.SMEM)


def call(kernel, out_shape, *args, smem=(), name=None):
    return pl.pallas_call(
        kernel,
        out_shape=out_shape,
        in_specs=[SMEM if i in smem else VMEM for i in range(len(args))],
        out_specs=jax.tree.map(lambda _: VMEM, out_shape),
        compiler_params=pltpu.CompilerParams(vmem_limit_bytes=16 << 20),
        name=name,
    )(*args)


def local(
    saturation,
    inlet_mask,
    crystal_size,
    crystal_weight,
    crystal_cell,
    live_count,
    nucleus_cell,
    nucleus_count,
    migrant_rows,
    migrant_count,
):
    plane_shape = saturation.shape[1:]
    lines, places = plane_shape
    slots = migrant_rows.shape[2]
    parcels = crystal_size.shape[0]
    shape = lambda *dims: jax.ShapeDtypeStruct(dims, F32)
    size, weight, cell = (a.reshape(-1, LANES) for a in (crystal_size, crystal_weight, crystal_cell))
    swap = lambda value: lax.ppermute(value, "grp", [(0, 1), (1, 0)])
    slabs, grps = lax.axis_size("slab"), lax.axis_size("grp")
    outward = []
    for s in range(slabs - 1):
        outward.append((s * grps + 1, (s + 1) * grps))
        outward.append(((s + 1) * grps, s * grps + 1))
    across = lambda value: lax.ppermute(value, ("slab", "grp"), outward)

    away = moments(True, size, weight, cell, live_count, nucleus_cell, nucleus_count, plane_shape)
    away = swap(away)
    home = moments(False, size, weight, cell, live_count, nucleus_cell, nucleus_count, plane_shape)
    field, state = call(
        first_kernel, (shape(1, lines, places), shape(4 + SUBS, lines, places)), saturation, home, away, name="first"
    )
    beside = across(field)
    other = swap(field)
    kept, given = call(
        migrants_kernel, (shape(8, slots), shape(8, slots)), size, weight, cell, migrant_rows, migrant_count, smem=(4,), name="migrants"
    )
    taken = swap(given)
    planes = call(second_kernel, shape(2, lines, places), field, beside, other, inlet_mask, state, name="second")
    partner = swap(planes)
    leaving = call(
        leaving_kernel, shape(lines + 4 * slots // places, places), planes, partner, kept, taken, name="leaving"
    )
    received = across(leaving)
    size_out = call(
        sizes_kernel, shape(parcels // LANES, LANES), planes, partner, size, cell, live_count, smem=(4,), name="sizes"
    )
    part = 2 * slots // places
    relayed = swap(received[lines : lines + part])
    mine = received[lines + part :]
    field_out = call(third_kernel, shape(1, lines, places), planes, received, partner, inlet_mask, name="third")
    arrivals = call(arrivals_kernel, shape(1, 2, 2, slots), mine, relayed, name="arrivals")
    return (field_out, size_out.reshape(-1), arrivals)


def solution(mesh):
    in_specs = (
        P(("slab", "grp"), None, None),
        P(("slab", "grp"), None, None),
        P(("slab", "grp")),
        P(("slab", "grp")),
        P(("slab", "grp")),
        P(("slab", "grp")),
        P(("slab", "grp"), None, None),
        P(("slab", "grp"), None, None),
        P(("slab", "grp"), None, None),
        P(("slab", "grp"), None),
    )
    out_specs = (
        P(("slab", "grp"), None, None),
        P(("slab", "grp")),
        P(("slab", "grp"), None, None, None),
    )
    return jax.shard_map(local, mesh=mesh, in_specs=in_specs, out_specs=out_specs, check_vma=False)
```

```python
import functools

import jax
import jax.numpy as jnp
from jax import lax
from jax.experimental import pallas as pl
from jax.experimental.pallas import tpu as pltpu
from jax.sharding import PartitionSpec as P

STEPS = 2
SUBS = 2

GROWTH = 0.08
NUCLEATE = 0.02
DIFFUSE = 0.12
INLET = 4.0

LANES = 128
F32 = jnp.float32
BF16 = jnp.bfloat16
NT = (((1,), (1,)), ((), ()))
NN = (((1,), (0,)), ((), ()))
TN = (((0,), (0,)), ((), ()))


def softplus(x):
    return jnp.maximum(x, 0.0) + jnp.log1p(jnp.exp(-jnp.abs(x)))


def pieces(x):
    high = x.astype(BF16)
    return high, (x - high.astype(F32)).astype(BF16)


def hot(count, row):
    index = lax.broadcasted_iota(jnp.int32, (count, row.shape[1]), 0)
    return jnp.where(index == row, 1.0, 0.0).astype(BF16)


def row_numbers(shape):
    return lax.broadcasted_iota(jnp.int32, shape, 0) * LANES + lax.broadcasted_iota(jnp.int32, shape, 1)


def swapped():
    slab = lax.axis_index("slab")
    return (slab == 0) | (slab == lax.axis_size("slab") - 1)


def sending_side():
    grp = lax.axis_index("grp")
    return jnp.where(swapped(), 1 - grp, grp)


def has_beside():
    slab, grp = lax.axis_index("slab"), lax.axis_index("grp")
    return jnp.where(grp == 0, slab > 0, slab < lax.axis_size("slab") - 1)


def across_pairs(slabs):
    last = slabs - 1
    up_out = lambda s: 0 if s == 0 else 1
    down_out = lambda s: 1 if s == last else 0
    pairs = [(s * 2 + up_out(s), (s + 1) * 2) for s in range(last)]
    pairs += [((s + 1) * 2 + down_out(s + 1), s * 2 + 1) for s in range(last)]
    return pairs + [(1, 0), (last * 2, last * 2 + 1)]


def plane_moments(plane, size, weight, cell, plane_shape):
    lines, places = plane_shape
    sizes = size[...]
    zeroth = weight[...]
    first = zeroth * sizes
    parts = [part.astype(F32) for moment in (zeroth, first, first * sizes) for part in pieces(moment)]
    line = cell[...] // places - plane * lines
    place = cell[...] % places
    group = 4
    sums = jnp.zeros((len(parts) * lines, places), F32)
    for start in range(0, sizes.shape[0], group):
        left, right = [], []
        for r in range(start, start + group):
            hot_line = hot(lines, line[r : r + 1])
            left.append(jnp.concatenate([hot_line * part[r : r + 1].astype(BF16) for part in parts], axis=0))
            right.append(hot(places, place[r : r + 1]))
        left, right = jnp.concatenate(left, axis=1), jnp.concatenate(right, axis=1)
        sums = sums + lax.dot_general(left, right, NT, preferred_element_type=F32)
    return [sums[2 * c * lines : (2 * c + 1) * lines] + sums[(2 * c + 1) * lines : (2 * c + 2) * lines] for c in range(3)]


def plane_counts(plane, event_cell, event_count, k, plane_shape):
    lines, places = plane_shape
    cells = event_cell[0, pl.ds(k, 1), :]
    counts = event_count[0, pl.ds(k, 1), :].astype(F32).astype(BF16)
    left = hot(lines, cells // places - plane * lines) * counts
    return lax.dot_general(left, hot(places, cells % places), NT, preferred_element_type=F32)


def away_kernel(*refs):
    inputs, live, out, kept, active, sems = refs[:8], refs[8], refs[9], refs[10:18], *refs[18:]
    copies = [pltpu.make_async_copy(src, dst, sems.at[i]) for i, (src, dst) in enumerate(zip(inputs, kept))]
    for copy in copies:
        copy.start()
    for copy in copies[:6]:
        copy.wait()
    size, weight, cell, event_cell, event_count, field = kept[:6]
    active[...] = jnp.where(row_numbers(size.shape) < live[0], 1.0, 0.0)
    weight[...] = weight[...] * active[...]
    plane_shape = out.shape[1:]
    plane = 1 - sending_side()
    for c, moment in enumerate(plane_moments(plane, size, weight, cell, plane_shape)):
        out[c] = moment
    for k in range(SUBS):
        out[3 + k] = plane_counts(plane, event_cell, event_count, k, plane_shape)
    out[3 + SUBS] = field[0]
    for copy in copies[6:]:
        copy.wait()


def home_kernel(size, weight, cell, event_cell, event_count, out, late):
    plane_shape = out.shape[1:]
    plane = sending_side()
    for c, moment in enumerate(plane_moments(plane, size, weight, cell, plane_shape)):
        out[c] = moment
    for k in range(SUBS):
        out[3 + k] = plane_counts(plane, event_cell, event_count, k, plane_shape)
    grp = lax.axis_index("grp")
    for k in range(SUBS):
        late[k] = plane_counts(grp, event_cell, event_count, SUBS + k, plane_shape)
        late[SUBS + k] = plane_counts(1 - grp, event_cell, event_count, SUBS + k, plane_shape)


def substep(field, zeroth, first, second, counts, grown):
    rate = softplus(field - 1.0)
    growth = GROWTH * rate
    taken = growth * (3.0 * second + growth * (3.0 * first + growth * zeroth))
    field = field - (taken + counts * (NUCLEATE * rate))
    second = second + growth * (2.0 * first + growth * zeroth)
    first = first + growth * zeroth
    return field, first, second, grown + growth


def first_kernel(field, home, away, late, out, state):
    now = jnp.where(swapped(), away[3 + SUBS], field[0])
    zeroth, first, second = (home[c] + away[c] for c in range(3))
    grown = jnp.zeros_like(now)
    for k in range(SUBS):
        now, first, second, grown = substep(now, zeroth, first, second, home[3 + k] + away[3 + k], grown)
    out[0] = now
    for c, value in enumerate((now, zeroth, first, second, grown)):
        state[c] = value
    for k in range(SUBS):
        state[5 + k] = late[SUBS + k]


def moved(field):
    lines, places = field.shape
    line = lax.broadcasted_iota(jnp.int32, field.shape, 0)
    place = lax.broadcasted_iota(jnp.int32, field.shape, 1)
    total = jnp.where(line == 0, 0.0, pltpu.roll(field, 1, 0))
    total += jnp.where(line == lines - 1, 0.0, pltpu.roll(field, lines - 1, 0))
    total += jnp.where(place == 0, 0.0, pltpu.roll(field, 1, 1))
    total += jnp.where(place == places - 1, 0.0, pltpu.roll(field, places - 1, 1))
    return total


def transport(field, beside, other, inlet):
    around = jnp.where(has_beside(), beside, 0.0) + other + moved(field)
    field = field + DIFFUSE * (around - 6.0 * field)
    return field + inlet * (INLET - field)


def second_kernel(beside, mine, other, late, inlet, given, out):
    lines = beside.shape[1]
    state = [jnp.where(swapped(), other[c], mine[c]) for c in range(5)]
    partner_field = jnp.where(swapped(), mine[0], other[0])
    now, zeroth, first, second, grown = state
    now = transport(now, beside[0], partner_field, inlet[0].astype(F32))
    for k in range(SUBS):
        now, first, second, grown = substep(now, zeroth, first, second, late[k] + other[5 + k], grown)
    out[pl.ds(0, lines)] = now
    out[pl.ds(lines, lines)] = grown
    out[pl.ds(2 * lines, given.shape[0])] = given[...]


def third_kernel(planes, received, partner, inlet, out):
    lines = out.shape[1]
    here = pl.ds(0, lines)
    out[0] = transport(planes[here], received[here], partner[here], inlet[0].astype(F32))


def migrants_kernel(size, weight, cell, rows, count, keep, give, *, places):
    side = sending_side()
    table_rows = size.shape[0]
    slots = rows.shape[2]
    table = []
    for values in (size[...], weight[...]):
        rest = values
        for _ in range(3):
            part = rest.astype(BF16)
            rest = rest - part.astype(F32)
            table.append(part)
    cells = cell[...]
    table += [(cells // places).astype(F32).astype(BF16), (cells % places).astype(F32).astype(BF16)]
    table = jnp.concatenate(table, axis=1)
    slot = lax.broadcasted_iota(jnp.int32, (1, slots), 1)
    for out, j in ((keep, side), (give, 1 - side)):
        row = jnp.where(j == 0, rows[0, 0:1, :], rows[0, 1:2, :])
        used = jnp.where(j == 0, count[0:1, 0:1], count[0:1, 1:2])
        valid = jnp.where(slot < used, 1.0, 0.0)
        picked = lax.dot_general(table, hot(table_rows, row // LANES), TN, preferred_element_type=F32)
        hot_lane = hot(LANES, row % LANES).astype(F32)
        found = [jnp.sum(picked[c * LANES : (c + 1) * LANES] * hot_lane, axis=0, keepdims=True) for c in range(8)]
        sizes = (found[0] + found[1] + found[2]) * valid
        weights = (found[3] + found[4] + found[5]) * valid
        at = 0
        for value in (sizes, weights, found[6], found[7], valid):
            for start in range(0, slots, places):
                out[at : at + 1] = value[:, start : start + places]
                at += 1
        out[at:] = jnp.zeros((out.shape[0] - at, places), F32)


def grown_at(stacked, line, place):
    lines = stacked.shape[0] // 2
    picked = lax.dot_general(stacked, hot(stacked.shape[1], place), NN, preferred_element_type=F32)
    picked = picked[:lines] + picked[lines:]
    index = lax.broadcasted_iota(jnp.int32, picked.shape, 0)
    return jnp.sum(jnp.where(index == line, picked, 0.0), axis=0, keepdims=True)


def both_planes(planes, partner, lines):
    grp = lax.axis_index("grp")
    mine, other = planes[pl.ds(lines, lines)], partner[pl.ds(lines, lines)]
    low = jnp.where(grp == 0, mine, other)
    high = jnp.where(grp == 0, other, mine)
    return jnp.concatenate(pieces(jnp.concatenate([low, high], axis=0)), axis=0)


def leaving_kernel(planes, partner, kept, out, *, lines, parts):
    stacked = both_planes(planes, partner, lines)
    here = pl.ds(0, lines)
    out[here] = jnp.where(swapped(), partner[here], planes[here])
    grp = lax.axis_index("grp")
    taken = partner[pl.ds(2 * lines, kept.shape[0])]
    keeping = kept[...]
    at = lines
    for one, other in ((keeping, taken), (taken, keeping)):
        part = jnp.where(grp == 0, one, other)
        rows = [part[i : i + 1] for i in range(5 * parts)]
        line = jnp.concatenate(rows[2 * parts : 3 * parts], axis=1).astype(jnp.int32)
        place = jnp.concatenate(rows[3 * parts : 4 * parts], axis=1).astype(jnp.int32)
        grown = grown_at(stacked, line, place)
        places = part.shape[1]
        for p in range(parts):
            out[at + p : at + p + 1] = rows[p] + grown[:, p * places : (p + 1) * places] * rows[4 * parts + p]
            out[at + parts + p : at + parts + p + 1] = rows[parts + p]
        at += 2 * parts


def sizes_kernel(planes, partner, size, cell, active, out, *, lines):
    places = planes.shape[1]
    stacked = both_planes(planes, partner, lines)
    cells = cell[...]
    line = cells // places
    place = cells % places
    group = 4
    found = []
    for start in range(0, size.shape[0], group):
        each = range(start, start + group)
        grown = grown_at(
            stacked,
            jnp.concatenate([line[r : r + 1] for r in each], axis=1),
            jnp.concatenate([place[r : r + 1] for r in each], axis=1),
        )
        found += [grown[:, i * LANES : (i + 1) * LANES] for i in range(group)]
    grown = jnp.concatenate(found, axis=0)
    out[...] = active[...] * (size[...] + grown)


def arrivals_kernel(received, relayed, out, *, lines, parts):
    slab, grp = lax.axis_index("slab"), lax.axis_index("grp")
    rows = 2 * parts
    pick = lambda block: jnp.where(grp == 0, block[:rows], block[rows:])
    mine = pick(received[pl.ds(lines, 2 * rows)])
    other = pick(relayed[...])
    lower = jnp.where(slab > 0, jnp.where(grp == 0, mine, other), 0.0)
    upper = jnp.where(slab < lax.axis_size("slab") - 1, jnp.where(grp == 0, other, mine), 0.0)
    places = mine.shape[1]
    for side, value in enumerate((lower, upper)):
        for v in range(2):
            for p in range(parts):
                at = v * parts + p
                out[0, side, v : v + 1, pl.ds(p * places, places)] = value[at : at + 1]


VMEM = pl.BlockSpec(memory_space=pltpu.VMEM)
SMEM = pl.BlockSpec(memory_space=pltpu.SMEM)
HBM = pl.BlockSpec(memory_space=pltpu.HBM)


def shape(*dims):
    return jax.ShapeDtypeStruct(dims, F32)


def call(kernel, out_shape, *args, name, cost=0, limit=16, scratch=(), specs=None):
    return pl.pallas_call(
        kernel,
        out_shape=out_shape,
        in_specs=specs or [VMEM] * len(args),
        out_specs=jax.tree.map(lambda _: VMEM, out_shape),
        scratch_shapes=scratch,
        compiler_params=pltpu.CompilerParams(vmem_limit_bytes=limit << 20),
        cost_estimate=pl.CostEstimate(flops=cost, bytes_accessed=0, transcendentals=0) if cost else None,
        name=name,
    )(*args)


def local(
    saturation,
    inlet_mask,
    crystal_size,
    crystal_weight,
    crystal_cell,
    live_count,
    nucleus_cell,
    nucleus_count,
    migrant_rows,
    migrant_count,
):
    lines, places = saturation.shape[1:]
    slots = migrant_rows.shape[2]
    parts = slots // places
    swap = lambda value: lax.ppermute(value, "grp", [(0, 1), (1, 0)])
    pairs = across_pairs(lax.axis_size("slab"))
    across = lambda value: lax.ppermute(value, ("slab", "grp"), pairs)

    inputs = [a.reshape(-1, LANES) for a in (crystal_size, crystal_weight, crystal_cell)]
    inputs += [nucleus_cell, nucleus_count, saturation, inlet_mask, migrant_rows]
    away, size, weight, cell, event_cell, event_count, field, inlet, rows, active = call(
        away_kernel,
        [shape(4 + SUBS, lines, places)]
        + [jax.ShapeDtypeStruct(a.shape, a.dtype) for a in inputs]
        + [shape(*inputs[0].shape)],
        *[pltpu.with_memory_space_constraint(a, pltpu.HBM) for a in inputs],
        live_count,
        specs=[HBM] * 8 + [SMEM],
        scratch=[pltpu.SemaphoreType.DMA((len(inputs),))],
        name="away",
    )
    away = swap(away)
    home, late = call(
        home_kernel,
        (shape(3 + SUBS, lines, places), shape(2 * SUBS, lines, places)),
        size, weight, cell, event_cell, event_count, cost=1 << 30, name="home",
    )
    front, mine = call(
        first_kernel, (shape(1, lines, places), shape(5 + SUBS, lines, places)), field, home, away, late, name="first"
    )
    beside = across(front)
    other = swap(mine)
    info = (shape(16, places), shape(16, places))
    kept, given = call(
        functools.partial(migrants_kernel, places=places), info, size, weight, cell, rows, migrant_count,
        cost=1 << 30, name="migrants",
    )
    planes = call(
        second_kernel, shape(2 * lines + 16, places), beside, mine, other, late, inlet, given, name="second"
    )
    partner = swap(planes)
    leaving = call(
        functools.partial(leaving_kernel, lines=lines, parts=parts),
        shape(lines + 4 * parts, places), planes, partner, kept, name="leaving",
    )
    received = across(leaving)
    size_out = call(
        functools.partial(sizes_kernel, lines=lines), shape(*size.shape), planes, partner, size, cell, active,
        cost=1 << 31, name="sizes",
    )
    relayed = swap(received[lines:])
    field_out = call(third_kernel, shape(1, lines, places), planes, received, partner, inlet, cost=1 << 28, name="third")
    arrivals = call(
        functools.partial(arrivals_kernel, lines=lines, parts=parts), shape(1, 2, 2, slots), received, relayed, name="arrivals"
    )
    return (field_out, size_out.reshape(-1), arrivals)


def solution(mesh):
    in_specs = (
        P(("slab", "grp"), None, None),
        P(("slab", "grp"), None, None),
        P(("slab", "grp")),
        P(("slab", "grp")),
        P(("slab", "grp")),
        P(("slab", "grp")),
        P(("slab", "grp"), None, None),
        P(("slab", "grp"), None, None),
        P(("slab", "grp"), None, None),
        P(("slab", "grp"), None),
    )
    out_specs = (
        P(("slab", "grp"), None, None),
        P(("slab", "grp")),
        P(("slab", "grp"), None, None, None),
    )
    return jax.shard_map(local, mesh=mesh, in_specs=in_specs, out_specs=out_specs, check_vma=False)
```

```python
import functools

import jax
import jax.numpy as jnp
from jax import lax
from jax.experimental import pallas as pl
from jax.experimental.pallas import tpu as pltpu
from jax.sharding import PartitionSpec as P

STEPS = 2
SUBS = 2

GROWTH = 0.08
NUCLEATE = 0.02
DIFFUSE = 0.12
INLET = 4.0

LANES = 128
F32 = jnp.float32
BF16 = jnp.bfloat16
NT = (((1,), (1,)), ((), ()))
NN = (((1,), (0,)), ((), ()))
TN = (((0,), (0,)), ((), ()))


def softplus(x):
    return jnp.maximum(x, 0.0) + jnp.log1p(jnp.exp(-jnp.abs(x)))


def pieces(x):
    high = x.astype(BF16)
    return high, (x - high.astype(F32)).astype(BF16)


def hot(count, row):
    index = lax.broadcasted_iota(jnp.int32, (count, row.shape[1]), 0)
    return jnp.where(index == row, 1.0, 0.0).astype(BF16)


def row_numbers(shape):
    return lax.broadcasted_iota(jnp.int32, shape, 0) * LANES + lax.broadcasted_iota(jnp.int32, shape, 1)


def ends():
    slab = lax.axis_index("slab")
    return (slab == 0) | (slab == lax.axis_size("slab") - 1)


def sends_other():
    return ends() | (lax.axis_index("slab") % 2 == 0)


def receives_other():
    return (lax.axis_index("slab") % 2 == 0) & ~ends()


def sending_side():
    grp = lax.axis_index("grp")
    return jnp.where(sends_other(), 1 - grp, grp)


def receiving_side():
    grp = lax.axis_index("grp")
    return jnp.where(receives_other(), 1 - grp, grp)


def has_beside(side):
    slab = lax.axis_index("slab")
    return jnp.where(side == 0, slab > 0, slab < lax.axis_size("slab") - 1)


def across_pairs(slabs):
    last = slabs - 1
    up_out = lambda s: 0 if s == 0 else s % 2
    up_in = lambda s: 1 if s == 0 else s % 2
    down_out = lambda s: 1 if s == last else 1 - s % 2
    down_in = lambda s: 0 if s == last else 1 - s % 2
    pairs = [(s * 2 + up_out(s), (s + 1) * 2 + down_in(s + 1)) for s in range(last)]
    pairs += [((s + 1) * 2 + down_out(s + 1), s * 2 + up_in(s)) for s in range(last)]
    return pairs + [(1, 0), (last * 2, last * 2 + 1)]


def plane_moments(plane, size, weight, cell, plane_shape):
    lines, places = plane_shape
    sizes = size[...]
    zeroth = weight[...]
    first = zeroth * sizes
    parts = [part.astype(F32) for moment in (zeroth, first, first * sizes) for part in pieces(moment)]
    line = cell[...] // places - plane * lines
    place = cell[...] % places
    group = 4
    sums = jnp.zeros((len(parts) * lines, places), F32)
    for start in range(0, sizes.shape[0], group):
        left, right = [], []
        for r in range(start, start + group):
            hot_line = hot(lines, line[r : r + 1])
            left.append(jnp.concatenate([hot_line * part[r : r + 1].astype(BF16) for part in parts], axis=0))
            right.append(hot(places, place[r : r + 1]))
        left, right = jnp.concatenate(left, axis=1), jnp.concatenate(right, axis=1)
        sums = sums + lax.dot_general(left, right, NT, preferred_element_type=F32)
    return [sums[2 * c * lines : (2 * c + 1) * lines] + sums[(2 * c + 1) * lines : (2 * c + 2) * lines] for c in range(3)]


def plane_counts(plane, event_cell, event_count, k, plane_shape):
    lines, places = plane_shape
    cells = event_cell[0, pl.ds(k, 1), :]
    counts = event_count[0, pl.ds(k, 1), :].astype(F32).astype(BF16)
    left = hot(lines, cells // places - plane * lines) * counts
    return lax.dot_general(left, hot(places, cells % places), NT, preferred_element_type=F32)


def away_kernel(*refs):
    inputs, live, out, kept, active, sems = refs[:8], refs[8], refs[9], refs[10:18], *refs[18:]
    copies = [pltpu.make_async_copy(src, dst, sems.at[i]) for i, (src, dst) in enumerate(zip(inputs, kept))]
    for copy in copies:
        copy.start()
    for copy in copies[:6]:
        copy.wait()
    size, weight, cell, event_cell, event_count, field = kept[:6]
    active[...] = jnp.where(row_numbers(size.shape) < live[0], 1.0, 0.0)
    weight[...] = weight[...] * active[...]
    plane_shape = out.shape[1:]
    plane = 1 - sending_side()
    for c, moment in enumerate(plane_moments(plane, size, weight, cell, plane_shape)):
        out[c] = moment
    for k in range(SUBS):
        out[3 + k] = plane_counts(plane, event_cell, event_count, k, plane_shape)
    out[3 + SUBS] = field[0]
    for copy in copies[6:]:
        copy.wait()


def home_kernel(size, weight, cell, event_cell, event_count, inlet, out, late):
    plane_shape = out.shape[1:]
    plane = sending_side()
    for c, moment in enumerate(plane_moments(plane, size, weight, cell, plane_shape)):
        out[c] = moment
    for k in range(SUBS):
        out[3 + k] = plane_counts(plane, event_cell, event_count, k, plane_shape)
    later = receiving_side()
    for k in range(SUBS):
        out[3 + SUBS + k] = plane_counts(1 - later, event_cell, event_count, SUBS + k, plane_shape)
        late[k] = plane_counts(later, event_cell, event_count, SUBS + k, plane_shape)
    out[3 + 2 * SUBS] = inlet[0].astype(F32)


def substep(field, zeroth, first, second, counts, grown):
    rate = softplus(field - 1.0)
    growth = GROWTH * rate
    taken = growth * (3.0 * second + growth * (3.0 * first + growth * zeroth))
    field = field - (taken + counts * (NUCLEATE * rate))
    second = second + growth * (2.0 * first + growth * zeroth)
    first = first + growth * zeroth
    return field, first, second, grown + growth


def first_substeps(field, one, other):
    zeroth, first, second = (one[c] + other[c] for c in range(3))
    grown = jnp.zeros_like(field)
    for k in range(SUBS):
        field, first, second, grown = substep(field, zeroth, first, second, one[3 + k] + other[3 + k], grown)
    return field, zeroth, first, second, grown


def front_kernel(field, home, away, out):
    start = jnp.where(sends_other(), away[3 + SUBS], field[0])
    out[0] = first_substeps(start, home, away)[0]


def state_kernel(field, home, away, sent, partner_home, late, inlet, out):
    other = sends_other()
    near = first_substeps(jnp.where(other, away[3 + SUBS], field[0]), home, away)
    far = first_substeps(jnp.where(other, field[0], away[3 + SUBS]), partner_home, sent)
    for c in range(5):
        out[c] = jnp.where(ends(), far[c], near[c])
    out[5] = jnp.where(ends(), near[0], far[0])
    for k in range(SUBS):
        out[6 + k] = late[k] + partner_home[3 + SUBS + k]
    out[6 + SUBS] = jnp.where(receives_other(), partner_home[3 + 2 * SUBS], inlet[0].astype(F32))


def moved(field):
    lines, places = field.shape
    line = lax.broadcasted_iota(jnp.int32, field.shape, 0)
    place = lax.broadcasted_iota(jnp.int32, field.shape, 1)
    total = jnp.where(line == 0, 0.0, pltpu.roll(field, 1, 0))
    total += jnp.where(line == lines - 1, 0.0, pltpu.roll(field, lines - 1, 0))
    total += jnp.where(place == 0, 0.0, pltpu.roll(field, 1, 1))
    total += jnp.where(place == places - 1, 0.0, pltpu.roll(field, places - 1, 1))
    return total


def transport(field, beside, other, inlet, side):
    around = jnp.where(has_beside(side), beside, 0.0) + other + moved(field)
    field = field + DIFFUSE * (around - 6.0 * field)
    return field + inlet * (INLET - field)


def second_kernel(beside, state, given, out):
    lines = beside.shape[1]
    now, zeroth, first, second, grown = (state[c] for c in range(5))
    now = transport(now, beside[0], state[5], state[6 + SUBS], receiving_side())
    for k in range(SUBS):
        now, first, second, grown = substep(now, zeroth, first, second, state[6 + k], grown)
    out[pl.ds(0, lines)] = now
    out[pl.ds(lines, lines)] = grown
    out[pl.ds(2 * lines, given.shape[0])] = given[...]


def migrants_kernel(size, weight, cell, rows, count, keep, give, *, places):
    side = sending_side()
    table_rows = size.shape[0]
    slots = rows.shape[2]
    table = []
    for values in (size[...], weight[...]):
        rest = values
        for _ in range(3):
            part = rest.astype(BF16)
            rest = rest - part.astype(F32)
            table.append(part)
    cells = cell[...]
    table += [(cells // places).astype(F32).astype(BF16), (cells % places).astype(F32).astype(BF16)]
    table = jnp.concatenate(table, axis=1)
    slot = lax.broadcasted_iota(jnp.int32, (1, slots), 1)
    for out, j in ((keep, side), (give, 1 - side)):
        row = jnp.where(j == 0, rows[0, 0:1, :], rows[0, 1:2, :])
        used = jnp.where(j == 0, count[0:1, 0:1], count[0:1, 1:2])
        valid = jnp.where(slot < used, 1.0, 0.0)
        picked = lax.dot_general(table, hot(table_rows, row // LANES), TN, preferred_element_type=F32)
        hot_lane = hot(LANES, row % LANES).astype(F32)
        found = [jnp.sum(picked[c * LANES : (c + 1) * LANES] * hot_lane, axis=0, keepdims=True) for c in range(8)]
        sizes = (found[0] + found[1] + found[2]) * valid
        weights = (found[3] + found[4] + found[5]) * valid
        at = 0
        for value in (sizes, weights, found[6], found[7], valid):
            for start in range(0, slots, places):
                out[at : at + 1] = value[:, start : start + places]
                at += 1
        out[at:] = jnp.zeros((out.shape[0] - at, places), F32)


def grown_at(stacked, line, place):
    lines = stacked.shape[0] // 2
    picked = lax.dot_general(stacked, hot(stacked.shape[1], place), NN, preferred_element_type=F32)
    picked = picked[:lines] + picked[lines:]
    index = lax.broadcasted_iota(jnp.int32, picked.shape, 0)
    return jnp.sum(jnp.where(index == line, picked, 0.0), axis=0, keepdims=True)


def both_planes(planes, partner, lines):
    mine, other = planes[pl.ds(lines, lines)], partner[pl.ds(lines, lines)]
    first = receiving_side() == 0
    low = jnp.where(first, mine, other)
    high = jnp.where(first, other, mine)
    return jnp.concatenate(pieces(jnp.concatenate([low, high], axis=0)), axis=0)


def leaving_kernel(planes, partner, kept, out, *, lines, parts):
    stacked = both_planes(planes, partner, lines)
    here = pl.ds(0, lines)
    out[here] = jnp.where(ends(), partner[here], planes[here])
    grp = lax.axis_index("grp")
    taken = partner[pl.ds(2 * lines, kept.shape[0])]
    keeping = kept[...]
    at = lines
    for one, other in ((keeping, taken), (taken, keeping)):
        part = jnp.where(grp == 0, one, other)
        rows = [part[i : i + 1] for i in range(5 * parts)]
        line = jnp.concatenate(rows[2 * parts : 3 * parts], axis=1).astype(jnp.int32)
        place = jnp.concatenate(rows[3 * parts : 4 * parts], axis=1).astype(jnp.int32)
        grown = grown_at(stacked, line, place)
        places = part.shape[1]
        for p in range(parts):
            out[at + p : at + p + 1] = rows[p] + grown[:, p * places : (p + 1) * places] * rows[4 * parts + p]
            out[at + parts + p : at + parts + p + 1] = rows[parts + p]
        at += 2 * parts


def sizes_kernel(planes, partner, size, cell, active, out, *, lines):
    places = planes.shape[1]
    stacked = both_planes(planes, partner, lines)
    cells = cell[...]
    line = cells // places
    place = cells % places
    group = 4
    found = []
    for start in range(0, size.shape[0], group):
        each = range(start, start + group)
        grown = grown_at(
            stacked,
            jnp.concatenate([line[r : r + 1] for r in each], axis=1),
            jnp.concatenate([place[r : r + 1] for r in each], axis=1),
        )
        found += [grown[:, i * LANES : (i + 1) * LANES] for i in range(group)]
    grown = jnp.concatenate(found, axis=0)
    out[...] = active[...] * (size[...] + grown)


def last_kernel(planes, partner, received, relayed, inlet, field_out, arrivals_out, *, lines, parts):
    slab, grp = lax.axis_index("slab"), lax.axis_index("grp")
    here = pl.ds(0, lines)
    other = receives_other()
    field = jnp.where(other, partner[here], planes[here])
    beyond = jnp.where(other, planes[here], partner[here])
    beside = jnp.where(other, relayed[here], received[here])
    field_out[0] = transport(field, beside, beyond, inlet[0].astype(F32), grp)
    rows = 2 * parts
    pick = lambda block: jnp.where(grp == 0, block[lines : lines + rows], block[lines + rows : lines + 2 * rows])
    mine, theirs = pick(received), pick(relayed)
    from_lower = receiving_side() == 0
    lower = jnp.where(slab > 0, jnp.where(from_lower, mine, theirs), 0.0)
    upper = jnp.where(slab < lax.axis_size("slab") - 1, jnp.where(from_lower, theirs, mine), 0.0)
    places = mine.shape[1]
    for side, value in enumerate((lower, upper)):
        for v in range(2):
            for p in range(parts):
                at = v * parts + p
                arrivals_out[0, side, v : v + 1, pl.ds(p * places, places)] = value[at : at + 1]


VMEM = pl.BlockSpec(memory_space=pltpu.VMEM)
SMEM = pl.BlockSpec(memory_space=pltpu.SMEM)
HBM = pl.BlockSpec(memory_space=pltpu.HBM)


def shape(*dims):
    return jax.ShapeDtypeStruct(dims, F32)


def call(kernel, out_shape, *args, name, cost=0, limit=16, scratch=(), specs=None):
    return pl.pallas_call(
        kernel,
        out_shape=out_shape,
        in_specs=specs or [VMEM] * len(args),
        out_specs=jax.tree.map(lambda _: VMEM, out_shape),
        scratch_shapes=scratch,
        compiler_params=pltpu.CompilerParams(vmem_limit_bytes=limit << 20),
        cost_estimate=pl.CostEstimate(flops=cost, bytes_accessed=0, transcendentals=0) if cost else None,
        name=name,
    )(*args)


def local(
    saturation,
    inlet_mask,
    crystal_size,
    crystal_weight,
    crystal_cell,
    live_count,
    nucleus_cell,
    nucleus_count,
    migrant_rows,
    migrant_count,
):
    lines, places = saturation.shape[1:]
    slots = migrant_rows.shape[2]
    parts = slots // places
    swap = lambda value: lax.ppermute(value, "grp", [(0, 1), (1, 0)])
    pairs = across_pairs(lax.axis_size("slab"))
    across = lambda value: lax.ppermute(value, ("slab", "grp"), pairs)

    inputs = [a.reshape(-1, LANES) for a in (crystal_size, crystal_weight, crystal_cell)]
    inputs += [nucleus_cell, nucleus_count, saturation, inlet_mask, migrant_rows]
    sent, size, weight, cell, event_cell, event_count, field, inlet, rows, active = call(
        away_kernel,
        [shape(4 + SUBS, lines, places)]
        + [jax.ShapeDtypeStruct(a.shape, a.dtype) for a in inputs]
        + [shape(*inputs[0].shape)],
        *[pltpu.with_memory_space_constraint(a, pltpu.HBM) for a in inputs],
        live_count,
        specs=[HBM] * 8 + [SMEM],
        scratch=[pltpu.SemaphoreType.DMA((len(inputs),))],
        name="away",
    )
    away = swap(sent)
    home, late = call(
        home_kernel,
        (shape(4 + 2 * SUBS, lines, places), shape(SUBS, lines, places)),
        size, weight, cell, event_cell, event_count, inlet, cost=1 << 30, name="home",
    )
    front = call(front_kernel, shape(1, lines, places), field, home, away, name="front")
    front, late_home = lax.optimization_barrier((front, home))
    partner_home = swap(late_home)
    beside = across(front)
    state = call(
        state_kernel, shape(7 + SUBS, lines, places), field, home, away, sent, partner_home, late, inlet,
        cost=1 << 28, name="state",
    )
    info = (shape(16, places), shape(16, places))
    kept, given = call(
        functools.partial(migrants_kernel, places=places), info, size, weight, cell, rows, migrant_count,
        cost=1 << 33, name="migrants",
    )
    planes = call(
        second_kernel, shape(2 * lines + 16, places), beside, state, given, name="second"
    )
    partner = swap(planes)
    leaving = call(
        functools.partial(leaving_kernel, lines=lines, parts=parts),
        shape(lines + 4 * parts, places), planes, partner, kept, name="leaving",
    )
    received = across(leaving)
    size_out = call(
        functools.partial(sizes_kernel, lines=lines), shape(*size.shape), planes, partner, size, cell, active,
        cost=1 << 31, name="sizes",
    )
    received, size_out = lax.optimization_barrier((received, size_out))
    relayed = swap(received)
    field_out, arrivals = call(
        functools.partial(last_kernel, lines=lines, parts=parts),
        (shape(1, lines, places), shape(1, 2, 2, slots)), planes, partner, received, relayed, inlet, name="last",
    )
    return (field_out, size_out.reshape(-1), arrivals)


def solution(mesh):
    in_specs = (
        P(("slab", "grp"), None, None),
        P(("slab", "grp"), None, None),
        P(("slab", "grp")),
        P(("slab", "grp")),
        P(("slab", "grp")),
        P(("slab", "grp")),
        P(("slab", "grp"), None, None),
        P(("slab", "grp"), None, None),
        P(("slab", "grp"), None, None),
        P(("slab", "grp"), None),
    )
    out_specs = (
        P(("slab", "grp"), None, None),
        P(("slab", "grp")),
        P(("slab", "grp"), None, None, None),
    )
    return jax.shard_map(local, mesh=mesh, in_specs=in_specs, out_specs=out_specs, check_vma=False)
```

```python
import functools

import jax
import jax.numpy as jnp
from jax import lax
from jax.experimental import pallas as pl
from jax.experimental.pallas import tpu as pltpu
from jax.sharding import PartitionSpec as P

STEPS = 2
SUBS = 2

GROWTH = 0.08
NUCLEATE = 0.02
DIFFUSE = 0.12
INLET = 4.0

LANES = 128
F32 = jnp.float32
BF16 = jnp.bfloat16
NT = (((1,), (1,)), ((), ()))
NN = (((1,), (0,)), ((), ()))
TN = (((0,), (0,)), ((), ()))


def softplus(x):
    return jnp.maximum(x, 0.0) + jnp.log1p(jnp.exp(-jnp.abs(x)))


def pieces(x):
    high = x.astype(BF16)
    return high, (x - high.astype(F32)).astype(BF16)


def hot(count, row):
    index = lax.broadcasted_iota(jnp.int32, (count, row.shape[1]), 0)
    return jnp.where(index == row, 1.0, 0.0).astype(BF16)


def row_numbers(shape):
    return lax.broadcasted_iota(jnp.int32, shape, 0) * LANES + lax.broadcasted_iota(jnp.int32, shape, 1)


def ends():
    slab = lax.axis_index("slab")
    return (slab == 0) | (slab == lax.axis_size("slab") - 1)


def sends_other():
    return ends() | (lax.axis_index("slab") % 2 == 0)


def receives_other():
    return (lax.axis_index("slab") % 2 == 0) & ~ends()


def sending_side():
    grp = lax.axis_index("grp")
    return jnp.where(sends_other(), 1 - grp, grp)


def receiving_side():
    grp = lax.axis_index("grp")
    return jnp.where(receives_other(), 1 - grp, grp)


def has_beside(side):
    slab = lax.axis_index("slab")
    return jnp.where(side == 0, slab > 0, slab < lax.axis_size("slab") - 1)


def across_pairs(slabs):
    last = slabs - 1
    up_out = lambda s: 0 if s == 0 else s % 2
    up_in = lambda s: 1 if s == 0 else s % 2
    down_out = lambda s: 1 if s == last else 1 - s % 2
    down_in = lambda s: 0 if s == last else 1 - s % 2
    pairs = [(s * 2 + up_out(s), (s + 1) * 2 + down_in(s + 1)) for s in range(last)]
    pairs += [((s + 1) * 2 + down_out(s + 1), s * 2 + up_in(s)) for s in range(last)]
    return pairs + [(1, 0), (last * 2, last * 2 + 1)]


def plane_moments(plane, sizes, weights, cells, plane_shape):
    lines, places = plane_shape
    first = weights * sizes
    parts = [part.astype(F32) for moment in (weights, first, first * sizes) for part in pieces(moment)]
    line = cells // places - plane * lines
    place = cells % places
    group = 4
    sums = jnp.zeros((len(parts) * lines, places), F32)
    for start in range(0, sizes.shape[0], group):
        left, right = [], []
        for r in range(start, start + group):
            hot_line = hot(lines, line[r : r + 1])
            left.append(jnp.concatenate([hot_line * part[r : r + 1].astype(BF16) for part in parts], axis=0))
            right.append(hot(places, place[r : r + 1]))
        left, right = jnp.concatenate(left, axis=1), jnp.concatenate(right, axis=1)
        sums = sums + lax.dot_general(left, right, NT, preferred_element_type=F32)
    return [sums[2 * c * lines : (2 * c + 1) * lines] + sums[(2 * c + 1) * lines : (2 * c + 2) * lines] for c in range(3)]


def plane_counts(plane, cells, counts, plane_shape):
    lines, places = plane_shape
    left = hot(lines, cells // places - plane * lines) * counts.astype(BF16)
    return lax.dot_general(left, hot(places, cells % places), NT, preferred_element_type=F32)


def own_events(event_cell, event_count, k):
    row = pl.ds(k, 1)
    return event_cell[0, row, :], event_count[0, row, :].astype(F32)


def sections(parcel_rows, event_rows, field_rows):
    sizes = [parcel_rows] * 3 + [event_rows] * 2 + [field_rows] * 2
    starts = [sum(sizes[:i]) for i in range(len(sizes) + 1)]
    return [pl.ds(start, size) for start, size in zip(starts, sizes)], starts[-1]


def packed_events(packed, spans, k, width):
    per = width // LANES
    rows = [packed[pl.ds(span.start + k * per + j, 1)] for span in spans for j in range(per)]
    cells, counts = jnp.concatenate(rows[:per], axis=1), jnp.concatenate(rows[per:], axis=1)
    return cells.astype(jnp.int32), counts


def load_kernel(*refs):
    inputs, live, out, kept, active, sems = refs[:8], refs[8], refs[9], refs[10:18], *refs[18:]
    copies = [pltpu.make_async_copy(src, dst, sems.at[i]) for i, (src, dst) in enumerate(zip(inputs, kept))]
    for copy in copies:
        copy.start()
    for copy in copies:
        copy.wait()
    size, weight, cell, event_cell, event_count, field = kept[:6]
    active[...] = jnp.where(row_numbers(size.shape) < live[0], 1.0, 0.0)
    weight[...] = weight[...] * active[...]
    events, width = event_cell.shape[1:]
    per = width // LANES
    spans, _ = sections(size.shape[0], events * per, field.shape[1])
    out[spans[0]] = size[...]
    out[spans[1]] = weight[...]
    out[spans[2]] = cell[...].astype(F32)
    for span, array in ((spans[3], event_cell), (spans[4], event_count)):
        values = array[0].astype(F32)
        for k in range(events):
            for j in range(per):
                out[pl.ds(span.start + k * per + j, 1)] = values[k : k + 1, j * LANES : (j + 1) * LANES]
    for j in range(2):
        out[spans[5 + j]] = field[0, :, pl.ds(j * LANES, LANES)]


def home_kernel(size, weight, cell, event_cell, event_count, out):
    plane_shape = out.shape[1:]
    plane = sending_side()
    for c, moment in enumerate(plane_moments(plane, size[...], weight[...], cell[...], plane_shape)):
        out[c] = moment
    for k in range(SUBS):
        out[3 + k] = plane_counts(plane, *own_events(event_cell, event_count, k), plane_shape)


def substep(field, zeroth, first, second, counts, grown):
    rate = softplus(field - 1.0)
    growth = GROWTH * rate
    taken = growth * (3.0 * second + growth * (3.0 * first + growth * zeroth))
    field = field - (taken + counts * (NUCLEATE * rate))
    second = second + growth * (2.0 * first + growth * zeroth)
    first = first + growth * zeroth
    return field, first, second, grown + growth


def front_kernel(field, home, packed, out, state, *, parcel_rows, events):
    plane_shape = out.shape[1:]
    plane = sending_side()
    spans, _ = sections(parcel_rows, events[0] * events[1] // LANES, plane_shape[0])
    cells = packed[spans[2]].astype(jnp.int32)
    zeroth, first, second = plane_moments(plane, packed[spans[0]], packed[spans[1]], cells, plane_shape)
    zeroth, first, second = zeroth + home[0], first + home[1], second + home[2]
    theirs = jnp.concatenate([packed[spans[5]], packed[spans[6]]], axis=1)
    now = jnp.where(sends_other(), theirs, field[0])
    grown = jnp.zeros_like(now)
    for k in range(SUBS):
        counts = home[3 + k] + plane_counts(plane, *packed_events(packed, spans[3:5], k, events[1]), plane_shape)
        now, first, second, grown = substep(now, zeroth, first, second, counts, grown)
    out[0] = now
    for c, value in enumerate((now, zeroth, first, second, grown)):
        state[c] = value


def late_kernel(state, packed, event_cell, event_count, inlet, out, late, *, parcel_rows):
    plane_shape = out.shape[1:]
    events, width = event_cell.shape[1:]
    spans, _ = sections(parcel_rows, events * width // LANES, plane_shape[0])
    plane = receiving_side()
    for c in range(5):
        out[c] = state[c]
    out[5] = inlet[0].astype(F32)
    for k in range(SUBS):
        mine = plane_counts(plane, *own_events(event_cell, event_count, SUBS + k), plane_shape)
        late[k] = mine + plane_counts(plane, *packed_events(packed, spans[3:5], SUBS + k, width), plane_shape)


def moved(field):
    lines, places = field.shape
    line = lax.broadcasted_iota(jnp.int32, field.shape, 0)
    place = lax.broadcasted_iota(jnp.int32, field.shape, 1)
    total = jnp.where(line == 0, 0.0, pltpu.roll(field, 1, 0))
    total += jnp.where(line == lines - 1, 0.0, pltpu.roll(field, lines - 1, 0))
    total += jnp.where(place == 0, 0.0, pltpu.roll(field, 1, 1))
    total += jnp.where(place == places - 1, 0.0, pltpu.roll(field, places - 1, 1))
    return total


def transport(field, beside, other, inlet, side):
    around = jnp.where(has_beside(side), beside, 0.0) + other + moved(field)
    field = field + DIFFUSE * (around - 6.0 * field)
    return field + inlet * (INLET - field)


def second_kernel(beside, mine, other, late, given, out):
    lines = beside.shape[1]
    now, zeroth, first, second, grown = (jnp.where(ends(), other[c], mine[c]) for c in range(5))
    partner_field = jnp.where(ends(), mine[0], other[0])
    inlet = jnp.where(receives_other(), other[5], mine[5])
    now = transport(now, beside[0], partner_field, inlet, receiving_side())
    for k in range(SUBS):
        now, first, second, grown = substep(now, zeroth, first, second, late[k], grown)
    out[pl.ds(0, lines)] = now
    out[pl.ds(lines, lines)] = grown
    out[pl.ds(2 * lines, given.shape[0])] = given[...]


def migrants_kernel(size, weight, cell, rows, count, keep, give, *, places):
    side = sending_side()
    table_rows = size.shape[0]
    slots = rows.shape[2]
    table = []
    for values in (size[...], weight[...]):
        rest = values
        for _ in range(3):
            part = rest.astype(BF16)
            rest = rest - part.astype(F32)
            table.append(part)
    cells = cell[...]
    table += [(cells // places).astype(F32).astype(BF16), (cells % places).astype(F32).astype(BF16)]
    table = jnp.concatenate(table, axis=1)
    slot = lax.broadcasted_iota(jnp.int32, (1, slots), 1)
    for out, j in ((keep, side), (give, 1 - side)):
        row = jnp.where(j == 0, rows[0, 0:1, :], rows[0, 1:2, :])
        used = jnp.where(j == 0, count[0:1, 0:1], count[0:1, 1:2])
        valid = jnp.where(slot < used, 1.0, 0.0)
        picked = lax.dot_general(table, hot(table_rows, row // LANES), TN, preferred_element_type=F32)
        hot_lane = hot(LANES, row % LANES).astype(F32)
        found = [jnp.sum(picked[c * LANES : (c + 1) * LANES] * hot_lane, axis=0, keepdims=True) for c in range(8)]
        sizes = (found[0] + found[1] + found[2]) * valid
        weights = (found[3] + found[4] + found[5]) * valid
        at = 0
        for value in (sizes, weights, found[6], found[7], valid):
            for start in range(0, slots, places):
                out[at : at + 1] = value[:, start : start + places]
                at += 1
        out[at:] = jnp.zeros((out.shape[0] - at, places), F32)


def grown_at(stacked, line, place):
    lines = stacked.shape[0] // 2
    picked = lax.dot_general(stacked, hot(stacked.shape[1], place), NN, preferred_element_type=F32)
    picked = picked[:lines] + picked[lines:]
    index = lax.broadcasted_iota(jnp.int32, picked.shape, 0)
    return jnp.sum(jnp.where(index == line, picked, 0.0), axis=0, keepdims=True)


def both_planes(planes, partner, lines):
    mine, other = planes[pl.ds(lines, lines)], partner[pl.ds(lines, lines)]
    first = receiving_side() == 0
    low = jnp.where(first, mine, other)
    high = jnp.where(first, other, mine)
    return jnp.concatenate(pieces(jnp.concatenate([low, high], axis=0)), axis=0)


def leaving_kernel(planes, partner, kept, out, *, lines, parts):
    stacked = both_planes(planes, partner, lines)
    here = pl.ds(0, lines)
    out[here] = jnp.where(ends(), partner[here], planes[here])
    grp = lax.axis_index("grp")
    taken = partner[pl.ds(2 * lines, kept.shape[0])]
    keeping = kept[...]
    blocks = [jnp.where(grp == 0, one, other) for one, other in ((keeping, taken), (taken, keeping))]
    pick = lambda c: [block[i : i + 1] for block in blocks for i in range(c * parts, (c + 1) * parts)]
    sizes, weights, valid = pick(0), pick(1), pick(4)
    line = jnp.concatenate(pick(2), axis=1).astype(jnp.int32)
    place = jnp.concatenate(pick(3), axis=1).astype(jnp.int32)
    grown = grown_at(stacked, line, place)
    places = planes.shape[1]
    for j in range(2):
        at = lines + 2 * parts * j
        for p in range(parts):
            i = j * parts + p
            out[at + p : at + p + 1] = sizes[i] + grown[:, i * places : (i + 1) * places] * valid[i]
            out[at + parts + p : at + parts + p + 1] = weights[i]


def sizes_kernel(planes, partner, size, cell, active, out, *, lines):
    places = planes.shape[1]
    stacked = both_planes(planes, partner, lines)
    cells = cell[...]
    line = cells // places
    place = cells % places
    group = 4
    found = []
    for start in range(0, size.shape[0], group):
        each = range(start, start + group)
        grown = grown_at(
            stacked,
            jnp.concatenate([line[r : r + 1] for r in each], axis=1),
            jnp.concatenate([place[r : r + 1] for r in each], axis=1),
        )
        found += [grown[:, i * LANES : (i + 1) * LANES] for i in range(group)]
    grown = jnp.concatenate(found, axis=0)
    out[...] = active[...] * (size[...] + grown)


def rest_kernel(planes, partner, inlet, out):
    lines = inlet.shape[1]
    here = pl.ds(0, lines)
    other = receives_other()
    field = jnp.where(other, partner[here], planes[here])
    beyond = jnp.where(other, planes[here], partner[here])
    keep = 1.0 - inlet[0].astype(F32)
    field = field + DIFFUSE * (beyond + moved(field) - 6.0 * field)
    out[0] = keep * field + (1.0 - keep) * INLET
    out[1] = jnp.where(has_beside(lax.axis_index("grp")), DIFFUSE * keep, 0.0)


def last_kernel(rest, received, relayed, field_out, arrivals_out, *, lines, parts):
    slab, grp = lax.axis_index("slab"), lax.axis_index("grp")
    here = pl.ds(0, lines)
    field_out[0] = rest[0] + rest[1] * jnp.where(receives_other(), relayed[here], received[here])
    rows = 2 * parts
    pick = lambda block: jnp.where(grp == 0, block[lines : lines + rows], block[lines + rows : lines + 2 * rows])
    mine, theirs = pick(received), pick(relayed)
    from_lower = receiving_side() == 0
    lower = jnp.where(slab > 0, jnp.where(from_lower, mine, theirs), 0.0)
    upper = jnp.where(slab < lax.axis_size("slab") - 1, jnp.where(from_lower, theirs, mine), 0.0)
    places = mine.shape[1]
    for side, value in enumerate((lower, upper)):
        for v in range(2):
            for p in range(parts):
                at = v * parts + p
                arrivals_out[0, side, v : v + 1, pl.ds(p * places, places)] = value[at : at + 1]


VMEM = pl.BlockSpec(memory_space=pltpu.VMEM)
SMEM = pl.BlockSpec(memory_space=pltpu.SMEM)
HBM = pl.BlockSpec(memory_space=pltpu.HBM)


def shape(*dims):
    return jax.ShapeDtypeStruct(dims, F32)


def call(kernel, out_shape, *args, name, cost=0, limit=16, scratch=(), specs=None):
    return pl.pallas_call(
        kernel,
        out_shape=out_shape,
        in_specs=specs or [VMEM] * len(args),
        out_specs=jax.tree.map(lambda _: VMEM, out_shape),
        scratch_shapes=scratch,
        compiler_params=pltpu.CompilerParams(vmem_limit_bytes=limit << 20),
        cost_estimate=pl.CostEstimate(flops=cost, bytes_accessed=0, transcendentals=0) if cost else None,
        name=name,
    )(*args)


def local(
    saturation,
    inlet_mask,
    crystal_size,
    crystal_weight,
    crystal_cell,
    live_count,
    nucleus_cell,
    nucleus_count,
    migrant_rows,
    migrant_count,
):
    lines, places = saturation.shape[1:]
    slots = migrant_rows.shape[2]
    parts = slots // places
    swap = lambda value: lax.ppermute(value, "grp", [(0, 1), (1, 0)])
    pairs = across_pairs(lax.axis_size("slab"))
    across = lambda value: lax.ppermute(value, ("slab", "grp"), pairs)

    hbm = lambda a: pltpu.with_memory_space_constraint(a, pltpu.HBM)
    like = lambda a: jax.ShapeDtypeStruct(a.shape, a.dtype)
    inputs = [a.reshape(-1, LANES) for a in (crystal_size, crystal_weight, crystal_cell)]
    inputs += [nucleus_cell, nucleus_count, saturation, inlet_mask, migrant_rows]
    parcel_rows, events = inputs[0].shape[0], nucleus_cell.shape[1:]
    _, packed_rows = sections(parcel_rows, events[0] * events[1] // LANES, lines)
    packed, size, weight, cell, event_cell, event_count, field, inlet, rows, active = call(
        load_kernel,
        [shape(packed_rows, LANES)] + [like(a) for a in inputs] + [shape(*inputs[0].shape)],
        *[hbm(a) for a in inputs],
        live_count,
        specs=[HBM] * 8 + [SMEM],
        scratch=[pltpu.SemaphoreType.DMA((len(inputs),))],
        name="load",
    )
    packed = swap(packed)
    home = call(
        home_kernel, shape(3 + SUBS, lines, places), size, weight, cell, event_cell, event_count,
        cost=1 << 30, name="home",
    )
    front, state = call(
        functools.partial(front_kernel, parcel_rows=parcel_rows, events=events),
        (shape(1, lines, places), shape(5, lines, places)), field, home, packed, name="front",
    )
    beside = across(front)
    _, state = lax.optimization_barrier((front, state))
    mine, late = call(
        functools.partial(late_kernel, parcel_rows=parcel_rows), (shape(6, lines, places), shape(SUBS, lines, places)),
        state, packed, event_cell, event_count, inlet, cost=1 << 28, name="late",
    )
    other = swap(mine)
    info = (shape(16, places), shape(16, places))
    kept, given = call(
        functools.partial(migrants_kernel, places=places), info, size, weight, cell, rows, migrant_count,
        cost=1 << 33, name="migrants",
    )
    planes = call(
        second_kernel, shape(2 * lines + 16, places), beside, mine, other, late, given, name="second"
    )
    partner = swap(planes)
    leaving = call(
        functools.partial(leaving_kernel, lines=lines, parts=parts),
        shape(lines + 4 * parts, places), planes, partner, kept, name="leaving",
    )
    received = across(leaving)
    size_out = call(
        functools.partial(sizes_kernel, lines=lines), shape(*size.shape), planes, partner, size, cell, active,
        cost=1 << 31, name="sizes",
    )
    received, size_out = lax.optimization_barrier((received, size_out))
    relayed = swap(received)
    rest = call(rest_kernel, shape(2, lines, places), planes, partner, inlet, cost=1 << 28, name="rest")
    field_out, arrivals = call(
        functools.partial(last_kernel, lines=lines, parts=parts),
        (shape(1, lines, places), shape(1, 2, 2, slots)), rest, received, relayed, name="last",
    )
    return (field_out, size_out.reshape(-1), arrivals)


def solution(mesh):
    in_specs = (
        P(("slab", "grp"), None, None),
        P(("slab", "grp"), None, None),
        P(("slab", "grp")),
        P(("slab", "grp")),
        P(("slab", "grp")),
        P(("slab", "grp")),
        P(("slab", "grp"), None, None),
        P(("slab", "grp"), None, None),
        P(("slab", "grp"), None, None),
        P(("slab", "grp"), None),
    )
    out_specs = (
        P(("slab", "grp"), None, None),
        P(("slab", "grp")),
        P(("slab", "grp"), None, None, None),
    )
    return jax.shard_map(local, mesh=mesh, in_specs=in_specs, out_specs=out_specs, check_vma=False)
```

```python
import functools

import jax
import jax.numpy as jnp
from jax import lax
from jax.experimental import pallas as pl
from jax.experimental.pallas import tpu as pltpu
from jax.sharding import PartitionSpec as P

STEPS = 2
SUBS = 2

GROWTH = 0.08
NUCLEATE = 0.02
DIFFUSE = 0.12
INLET = 4.0

LANES = 128
F32 = jnp.float32
BF16 = jnp.bfloat16
NT = (((1,), (1,)), ((), ()))
NN = (((1,), (0,)), ((), ()))
TN = (((0,), (0,)), ((), ()))


def softplus(x):
    return jnp.maximum(x, 0.0) + jnp.log1p(jnp.exp(-jnp.abs(x)))


def pieces(x):
    high = x.astype(BF16)
    return high, (x - high.astype(F32)).astype(BF16)


def hot(count, row):
    index = lax.broadcasted_iota(jnp.int32, (count, row.shape[1]), 0)
    return jnp.where(index == row, 1.0, 0.0).astype(BF16)


def row_numbers(shape):
    return lax.broadcasted_iota(jnp.int32, shape, 0) * LANES + lax.broadcasted_iota(jnp.int32, shape, 1)


def ends():
    slab = lax.axis_index("slab")
    return (slab == 0) | (slab == lax.axis_size("slab") - 1)


def sends_other():
    return ends() | (lax.axis_index("slab") % 2 == 0)


def receives_other():
    return (lax.axis_index("slab") % 2 == 0) & ~ends()


def sending_side():
    grp = lax.axis_index("grp")
    return jnp.where(sends_other(), 1 - grp, grp)


def receiving_side():
    grp = lax.axis_index("grp")
    return jnp.where(receives_other(), 1 - grp, grp)


def has_beside(side):
    slab = lax.axis_index("slab")
    return jnp.where(side == 0, slab > 0, slab < lax.axis_size("slab") - 1)


def across_pairs(slabs, second):
    last, first_out = slabs - 1, 1 if second else 0
    up_out = lambda s: first_out if s == 0 else s % 2
    up_in = lambda s: 1 - first_out if s == 0 else s % 2
    down_out = lambda s: 1 - first_out if s == last else 1 - s % 2
    down_in = lambda s: first_out if s == last else 1 - s % 2
    pairs = [(s * 2 + up_out(s), (s + 1) * 2 + down_in(s + 1)) for s in range(last)]
    pairs += [((s + 1) * 2 + down_out(s + 1), s * 2 + up_in(s)) for s in range(last)]
    closing = [(1 - first_out, first_out), (last * 2 + first_out, last * 2 + 1 - first_out)]
    return pairs + closing


def plane_moments(plane, sizes, weights, cells, plane_shape):
    lines, places = plane_shape
    first = weights * sizes
    parts = [part.astype(F32) for moment in (weights, first, first * sizes) for part in pieces(moment)]
    line = cells // places - plane * lines
    place = cells % places
    group = 4
    sums = jnp.zeros((len(parts) * lines, places), F32)
    for start in range(0, sizes.shape[0], group):
        left, right = [], []
        for r in range(start, start + group):
            hot_line = hot(lines, line[r : r + 1])
            left.append(jnp.concatenate([hot_line * part[r : r + 1].astype(BF16) for part in parts], axis=0))
            right.append(hot(places, place[r : r + 1]))
        left, right = jnp.concatenate(left, axis=1), jnp.concatenate(right, axis=1)
        sums = sums + lax.dot_general(left, right, NT, preferred_element_type=F32)
    return [sums[2 * c * lines : (2 * c + 1) * lines] + sums[(2 * c + 1) * lines : (2 * c + 2) * lines] for c in range(3)]


def plane_counts(plane, cells, counts, plane_shape):
    lines, places = plane_shape
    left = hot(lines, cells // places - plane * lines) * counts.astype(BF16)
    return lax.dot_general(left, hot(places, cells % places), NT, preferred_element_type=F32)


def own_events(event_cell, event_count, k):
    row = pl.ds(k, 1)
    return event_cell[0, row, :], event_count[0, row, :].astype(F32)


def sections(parcel_rows, event_rows, field_rows):
    sizes = [parcel_rows] * 3 + [event_rows] * 2 + [field_rows] * 2
    starts = [sum(sizes[:i]) for i in range(len(sizes) + 1)]
    return [pl.ds(start, size) for start, size in zip(starts, sizes)], starts[-1]


def packed_events(packed, spans, k, width):
    per = width // LANES
    rows = [packed[pl.ds(span.start + k * per + j, 1)] for span in spans for j in range(per)]
    cells, counts = jnp.concatenate(rows[:per], axis=1), jnp.concatenate(rows[per:], axis=1)
    return cells.astype(jnp.int32), counts


def load_kernel(*refs):
    inputs, live, out, kept, active, sems = refs[:9], refs[9], refs[10], refs[11:20], *refs[20:]
    copies = [pltpu.make_async_copy(src, dst, sems.at[i]) for i, (src, dst) in enumerate(zip(inputs, kept))]
    for copy in copies:
        copy.start()
    for copy in copies:
        copy.wait()
    size, weight, cell, event_cell, event_count, field = kept[:6]
    active[...] = jnp.where(row_numbers(size.shape) < live[0], 1.0, 0.0)
    weight[...] = weight[...] * active[...]
    events, width = event_cell.shape[1:]
    per = width // LANES
    spans, _ = sections(size.shape[0], events * per, field.shape[1])
    out[spans[0]] = size[...]
    out[spans[1]] = weight[...]
    out[spans[2]] = cell[...].astype(F32)
    for span, array in ((spans[3], event_cell), (spans[4], event_count)):
        values = array[0].astype(F32)
        for k in range(events):
            for j in range(per):
                out[pl.ds(span.start + k * per + j, 1)] = values[k : k + 1, j * LANES : (j + 1) * LANES]
    for j in range(2):
        out[spans[5 + j]] = field[0, :, pl.ds(j * LANES, LANES)]


def home_kernel(size, weight, cell, event_cell, event_count, out):
    plane_shape = out.shape[1:]
    plane = sending_side()
    for c, moment in enumerate(plane_moments(plane, size[...], weight[...], cell[...], plane_shape)):
        out[c] = moment
    for k in range(SUBS):
        out[3 + k] = plane_counts(plane, *own_events(event_cell, event_count, k), plane_shape)


def substep(field, zeroth, first, second, counts, grown):
    rate = softplus(field - 1.0)
    growth = GROWTH * rate
    taken = growth * (3.0 * second + growth * (3.0 * first + growth * zeroth))
    field = field - (taken + counts * (NUCLEATE * rate))
    second = second + growth * (2.0 * first + growth * zeroth)
    first = first + growth * zeroth
    return field, first, second, grown + growth


def front_kernel(field, home, packed, out, state, *, parcel_rows, events):
    plane_shape = out.shape[1:]
    plane = sending_side()
    spans, _ = sections(parcel_rows, events[0] * events[1] // LANES, plane_shape[0])
    cells = packed[spans[2]].astype(jnp.int32)
    zeroth, first, second = plane_moments(plane, packed[spans[0]], packed[spans[1]], cells, plane_shape)
    zeroth, first, second = zeroth + home[0], first + home[1], second + home[2]
    theirs = jnp.concatenate([packed[spans[5]], packed[spans[6]]], axis=1)
    now = jnp.where(sends_other(), theirs, field[0])
    grown = jnp.zeros_like(now)
    for k in range(SUBS):
        counts = home[3 + k] + plane_counts(plane, *packed_events(packed, spans[3:5], k, events[1]), plane_shape)
        now, first, second, grown = substep(now, zeroth, first, second, counts, grown)
    out[0] = now
    for c, value in enumerate((now, zeroth, first, second, grown)):
        state[c] = value


def late_kernel(state, packed, event_cell, event_count, inlet, out, late, *, parcel_rows):
    plane_shape = out.shape[1:]
    events = event_cell.shape[1:]
    spans, _ = sections(parcel_rows, events[0] * events[1] // LANES, plane_shape[0])
    plane = receiving_side()
    for c in range(5):
        out[c] = state[c]
    out[5] = inlet[0].astype(F32)
    for k in range(SUBS):
        mine = plane_counts(plane, *own_events(event_cell, event_count, SUBS + k), plane_shape)
        late[k] = mine + plane_counts(plane, *packed_events(packed, spans[3:5], SUBS + k, events[1]), plane_shape)


def moved(field):
    lines, places = field.shape
    line = lax.broadcasted_iota(jnp.int32, field.shape, 0)
    place = lax.broadcasted_iota(jnp.int32, field.shape, 1)
    total = jnp.where(line == 0, 0.0, pltpu.roll(field, 1, 0))
    total += jnp.where(line == lines - 1, 0.0, pltpu.roll(field, lines - 1, 0))
    total += jnp.where(place == 0, 0.0, pltpu.roll(field, 1, 1))
    total += jnp.where(place == places - 1, 0.0, pltpu.roll(field, places - 1, 1))
    return total


def transport(field, beside, other, inlet, side):
    around = jnp.where(has_beside(side), beside, 0.0) + other + moved(field)
    field = field + DIFFUSE * (around - 6.0 * field)
    return field + inlet * (INLET - field)


def second_kernel(beside, mine, other, late, info, their_info, front, total, out, *, parts):
    lines = beside.shape[1]
    now, zeroth, first, second, grown = (jnp.where(ends(), other[c], mine[c]) for c in range(5))
    partner_field = jnp.where(ends(), mine[0], other[0])
    inlet = jnp.where(receives_other(), other[5], mine[5])
    now = transport(now, beside[0], partner_field, inlet, receiving_side())
    for k in range(SUBS):
        now, first, second, grown = substep(now, zeroth, first, second, late[k], grown)
    front[0] = now
    total[0] = grown
    half = info.shape[0] // 2
    rows = by_owner(info[pl.ds(half, half)], their_info[pl.ds(0, half)], parts)
    for i, value in enumerate(plane_growth(grown, rows, parts)):
        out[i : i + 1] = value
    out[2 * parts :] = jnp.zeros((out.shape[0] - 2 * parts, out.shape[1]), F32)


def migrants_kernel(size, weight, cell, rows, count, out, *, places):
    side = receiving_side()
    table_rows = size.shape[0]
    slots = rows.shape[2]
    table, nothing = [], jnp.zeros(size.shape, BF16)
    for values in (size[...], weight[...]):
        stack, rest = [], values
        for _ in range(3):
            part = rest.astype(BF16)
            rest = rest - part.astype(F32)
            stack.append(part)
        table.append(jnp.concatenate(stack, axis=0))
    cells = cell[...]
    for values in (cells // places, cells % places):
        table.append(jnp.concatenate([values.astype(F32).astype(BF16), nothing, nothing], axis=0))
    table = jnp.concatenate(table, axis=1)
    slot = lax.broadcasted_iota(jnp.int32, (1, slots), 1)
    half = out.shape[0] // 2
    for block, j in ((0, side), (half, 1 - side)):
        row = jnp.where(j == 0, rows[0, 0:1, :], rows[0, 1:2, :])
        used = jnp.where(j == 0, count[0:1, 0:1], count[0:1, 1:2])
        valid = jnp.where(slot < used, 1.0, 0.0)
        hot_row = jnp.concatenate([hot(table_rows, row // LANES)] * 3, axis=0)
        picked = lax.dot_general(table, hot_row, TN, preferred_element_type=F32)
        hot_lane = hot(LANES, row % LANES).astype(F32)
        found = [jnp.sum(picked[c * LANES : (c + 1) * LANES] * hot_lane, axis=0, keepdims=True) for c in range(4)]
        sizes, weights = found[0] * valid, found[1] * valid
        at = block
        for value in (sizes, weights, found[2], found[3], valid):
            for start in range(0, slots, places):
                out[at : at + 1] = value[:, start : start + places]
                at += 1
        out[at : block + half] = jnp.zeros((block + half - at, places), F32)


def grown_at(stacked, line, place):
    lines = stacked.shape[0] // 2
    picked = lax.dot_general(stacked, hot(stacked.shape[1], place), NN, preferred_element_type=F32)
    picked = picked[:lines] + picked[lines:]
    index = lax.broadcasted_iota(jnp.int32, picked.shape, 0)
    return jnp.sum(jnp.where(index == line, picked, 0.0), axis=0, keepdims=True)


def both_planes(mine, other):
    first = receiving_side() == 0
    low = jnp.where(first, mine, other)
    high = jnp.where(first, other, mine)
    return jnp.concatenate(pieces(jnp.concatenate([low, high], axis=0)), axis=0)


def by_owner(mine, partners, parts):
    first = lax.axis_index("grp") == 0
    blocks = [jnp.where(first, one, other) for one, other in ((mine, partners), (partners, mine))]
    return lambda c: [block[i : i + 1] for block in blocks for i in range(c * parts, (c + 1) * parts)]


def plane_growth(grown, rows, parts):
    lines, places = grown.shape
    stacked = jnp.concatenate(pieces(grown), axis=0)
    line = jnp.concatenate(rows(2), axis=1).astype(jnp.int32) - receiving_side() * lines
    found = grown_at(stacked, line, jnp.concatenate(rows(3), axis=1).astype(jnp.int32))
    valid = rows(4)
    return [found[:, i * places : (i + 1) * places] * valid[i] for i in range(2 * parts)]


def own_kernel(total, info, their_info, out, *, parts):
    half = info.shape[0] // 2
    rows = by_owner(info[pl.ds(0, half)], their_info[pl.ds(half, half)], parts)
    found = plane_growth(total[0], rows, parts)
    sizes, weights = rows(0), rows(1)
    for i in range(2 * parts):
        at = (i // parts) * 2 * parts + i % parts
        out[at : at + 1] = sizes[i] + found[i]
        out[at + parts : at + parts + 1] = weights[i]


def leaving_kernel(front, own, theirs, out, *, parts):
    lines = front.shape[1]
    out[pl.ds(0, lines)] = front[0]
    for j in range(2):
        at = 2 * parts * j
        out[lines + at : lines + at + parts] = own[at : at + parts] + theirs[j * parts : (j + 1) * parts]
        out[lines + at + parts : lines + at + 2 * parts] = own[at + parts : at + 2 * parts]


def sizes_kernel(total, their_total, size, cell, active, out):
    places = total.shape[2]
    stacked = both_planes(total[0], their_total[0])
    cells = cell[...]
    line = cells // places
    place = cells % places
    group = 4
    found = []
    for start in range(0, size.shape[0], group):
        each = range(start, start + group)
        grown = grown_at(
            stacked,
            jnp.concatenate([line[r : r + 1] for r in each], axis=1),
            jnp.concatenate([place[r : r + 1] for r in each], axis=1),
        )
        found += [grown[:, i * LANES : (i + 1) * LANES] for i in range(group)]
    grown = jnp.concatenate(found, axis=0)
    out[...] = active[...] * (size[...] + grown)


def rest_kernel(front, their_front, inlet, out):
    other = receives_other()
    field = jnp.where(other, their_front[0], front[0])
    beyond = jnp.where(other, front[0], their_front[0])
    keep = 1.0 - inlet[0].astype(F32)
    field = field + DIFFUSE * (beyond + moved(field) - 6.0 * field)
    out[0] = keep * field + (1.0 - keep) * INLET
    out[1] = jnp.where(has_beside(lax.axis_index("grp")), DIFFUSE * keep, 0.0)


def last_kernel(rest, received, relayed, field_out, arrivals_out, *, lines, parts):
    slab, grp = lax.axis_index("slab"), lax.axis_index("grp")
    here = pl.ds(0, lines)
    field_out[0] = rest[0] + rest[1] * jnp.where(sends_other(), relayed[here], received[here])
    rows = 2 * parts
    pick = lambda block: jnp.where(grp == 0, block[lines : lines + rows], block[lines + rows : lines + 2 * rows])
    mine, theirs = pick(received), pick(relayed)
    from_lower = sending_side() == 0
    lower = jnp.where(slab > 0, jnp.where(from_lower, mine, theirs), 0.0)
    upper = jnp.where(slab < lax.axis_size("slab") - 1, jnp.where(from_lower, theirs, mine), 0.0)
    places = mine.shape[1]
    for side, value in enumerate((lower, upper)):
        for v in range(2):
            for p in range(parts):
                at = v * parts + p
                arrivals_out[0, side, v : v + 1, pl.ds(p * places, places)] = value[at : at + 1]


VMEM = pl.BlockSpec(memory_space=pltpu.VMEM)
SMEM = pl.BlockSpec(memory_space=pltpu.SMEM)
HBM = pl.BlockSpec(memory_space=pltpu.HBM)


def shape(*dims):
    return jax.ShapeDtypeStruct(dims, F32)


def call(kernel, out_shape, *args, name, cost=0, limit=16, scratch=(), specs=None):
    return pl.pallas_call(
        kernel,
        out_shape=out_shape,
        in_specs=specs or [VMEM] * len(args),
        out_specs=jax.tree.map(lambda _: VMEM, out_shape),
        scratch_shapes=scratch,
        compiler_params=pltpu.CompilerParams(vmem_limit_bytes=limit << 20),
        cost_estimate=pl.CostEstimate(flops=cost, bytes_accessed=0, transcendentals=0) if cost else None,
        name=name,
    )(*args)


def local(
    saturation,
    inlet_mask,
    crystal_size,
    crystal_weight,
    crystal_cell,
    live_count,
    nucleus_cell,
    nucleus_count,
    migrant_rows,
    migrant_count,
):
    lines, places = saturation.shape[1:]
    slots = migrant_rows.shape[2]
    parts = slots // places
    swap = lambda value: lax.ppermute(value, "grp", [(0, 1), (1, 0)])
    slabs = lax.axis_size("slab")
    across = lambda value, second: lax.ppermute(value, ("slab", "grp"), across_pairs(slabs, second))

    hbm = lambda a: pltpu.with_memory_space_constraint(a, pltpu.HBM)
    like = lambda a: jax.ShapeDtypeStruct(a.shape, a.dtype)
    inputs = [a.reshape(-1, LANES) for a in (crystal_size, crystal_weight, crystal_cell)]
    inputs += [nucleus_cell, nucleus_count, saturation, inlet_mask, migrant_rows, migrant_count]
    parcel_rows, events = inputs[0].shape[0], nucleus_cell.shape[1:]
    _, packed_rows = sections(parcel_rows, events[0] * events[1] // LANES, lines)
    packed, size, weight, cell, event_cell, event_count, field, inlet, rows, count, active = call(
        load_kernel,
        [shape(packed_rows, LANES)] + [like(a) for a in inputs] + [shape(*inputs[0].shape)],
        *[hbm(a) for a in inputs],
        live_count,
        specs=[HBM] * 9 + [SMEM],
        scratch=[pltpu.SemaphoreType.DMA((len(inputs),))],
        name="load",
    )
    packed = swap(packed)
    home = call(
        home_kernel, shape(3 + SUBS, lines, places), size, weight, cell, event_cell, event_count,
        cost=1 << 30, name="home",
    )
    front, state = call(
        functools.partial(front_kernel, parcel_rows=parcel_rows, events=events),
        (shape(1, lines, places), shape(5, lines, places)), field, home, packed, name="front",
    )
    beside = across(front, False)
    _, state = lax.optimization_barrier((front, state))
    mine, late = call(
        functools.partial(late_kernel, parcel_rows=parcel_rows), (shape(6, lines, places), shape(SUBS, lines, places)),
        state, packed, event_cell, event_count, inlet, cost=1 << 28, name="late",
    )
    other = swap(mine)
    info = call(
        functools.partial(migrants_kernel, places=places), shape(32, places), size, weight, cell, rows, count,
        cost=1 << 33, name="migrants",
    )
    their_info = swap(info)
    front, total, given = call(
        functools.partial(second_kernel, parts=parts),
        (shape(1, lines, places), shape(1, lines, places), shape(8, places)),
        beside, mine, other, late, info, their_info, name="second",
    )
    theirs = swap(given)
    own = call(
        functools.partial(own_kernel, parts=parts), shape(4 * parts, places), total, info, their_info,
        cost=1 << 28, name="own",
    )
    leaving = call(
        functools.partial(leaving_kernel, parts=parts), shape(lines + 4 * parts, places), front, own, theirs, name="leaving"
    )
    received = across(leaving, True)
    _, later = lax.optimization_barrier((leaving, total))
    their_total, their_front = swap(later), swap(front)
    size_out = call(
        sizes_kernel, shape(*size.shape), total, their_total, size, cell, active, cost=1 << 26, name="sizes",
    )
    received, size_out = lax.optimization_barrier((received, size_out))
    relayed = swap(received)
    rest = call(rest_kernel, shape(2, lines, places), front, their_front, inlet, cost=1 << 28, name="rest")
    field_out, arrivals = call(
        functools.partial(last_kernel, lines=lines, parts=parts),
        (shape(1, lines, places), shape(1, 2, 2, slots)), rest, received, relayed, name="last",
    )
    return (field_out, size_out.reshape(-1), arrivals)


def solution(mesh):
    in_specs = (
        P(("slab", "grp"), None, None),
        P(("slab", "grp"), None, None),
        P(("slab", "grp")),
        P(("slab", "grp")),
        P(("slab", "grp")),
        P(("slab", "grp")),
        P(("slab", "grp"), None, None),
        P(("slab", "grp"), None, None),
        P(("slab", "grp"), None, None),
        P(("slab", "grp"), None),
    )
    out_specs = (
        P(("slab", "grp"), None, None),
        P(("slab", "grp")),
        P(("slab", "grp"), None, None, None),
    )
    return jax.shard_map(local, mesh=mesh, in_specs=in_specs, out_specs=out_specs, check_vma=False)
```

```python
import functools

import jax
import jax.numpy as jnp
from jax import lax
from jax.experimental import pallas as pl
from jax.experimental.pallas import tpu as pltpu
from jax.sharding import PartitionSpec as P

STEPS = 2
SUBS = 2

GROWTH = 0.08
NUCLEATE = 0.02
DIFFUSE = 0.12
INLET = 4.0

LANES = 128
F32 = jnp.float32
BF16 = jnp.bfloat16
NT = (((1,), (1,)), ((), ()))
NN = (((1,), (0,)), ((), ()))
TN = (((0,), (0,)), ((), ()))


def softplus(x):
    return jnp.maximum(x, 0.0) + jnp.log(1.0 + jnp.exp(-jnp.abs(x)))


def pieces(x):
    high = x.astype(BF16)
    return high, (x - high.astype(F32)).astype(BF16)


def hot(count, row):
    index = lax.broadcasted_iota(jnp.int32, (count, row.shape[1]), 0)
    return jnp.where(index == row, 1.0, 0.0).astype(BF16)


def row_numbers(shape):
    return lax.broadcasted_iota(jnp.int32, shape, 0) * LANES + lax.broadcasted_iota(jnp.int32, shape, 1)


def ends():
    slab = lax.axis_index("slab")
    return (slab == 0) | (slab == lax.axis_size("slab") - 1)


def sends_other():
    return ends() | (lax.axis_index("slab") % 2 == 0)


def receives_other():
    return (lax.axis_index("slab") % 2 == 0) & ~ends()


def sending_side():
    grp = lax.axis_index("grp")
    return jnp.where(sends_other(), 1 - grp, grp)


def receiving_side():
    grp = lax.axis_index("grp")
    return jnp.where(receives_other(), 1 - grp, grp)


def has_beside(side):
    slab = lax.axis_index("slab")
    return jnp.where(side == 0, slab > 0, slab < lax.axis_size("slab") - 1)


def across_pairs(slabs, second):
    last, first_out = slabs - 1, 1 if second else 0
    up_out = lambda s: first_out if s == 0 else s % 2
    up_in = lambda s: 1 - first_out if s == 0 else s % 2
    down_out = lambda s: 1 - first_out if s == last else 1 - s % 2
    down_in = lambda s: first_out if s == last else 1 - s % 2
    pairs = [(s * 2 + up_out(s), (s + 1) * 2 + down_in(s + 1)) for s in range(last)]
    pairs += [((s + 1) * 2 + down_out(s + 1), s * 2 + up_in(s)) for s in range(last)]
    closing = [(1 - first_out, first_out), (last * 2 + first_out, last * 2 + 1 - first_out)]
    return pairs + closing


def plane_moments(plane, sizes, weights, cells, plane_shape):
    lines, places = plane_shape
    first = weights * sizes
    parts = [part.astype(F32) for moment in (weights, first, first * sizes) for part in pieces(moment)]
    line = cells // places - plane * lines
    place = cells % places
    group = 4
    sums = jnp.zeros((len(parts) * lines, places), F32)
    for start in range(0, sizes.shape[0], group):
        left, right = [], []
        for r in range(start, start + group):
            hot_line = hot(lines, line[r : r + 1])
            left.append(jnp.concatenate([hot_line * part[r : r + 1].astype(BF16) for part in parts], axis=0))
            right.append(hot(places, place[r : r + 1]))
        left, right = jnp.concatenate(left, axis=1), jnp.concatenate(right, axis=1)
        sums = sums + lax.dot_general(left, right, NT, preferred_element_type=F32)
    return [sums[2 * c * lines : (2 * c + 1) * lines] + sums[(2 * c + 1) * lines : (2 * c + 2) * lines] for c in range(3)]


def plane_counts(plane, cells, counts, plane_shape):
    lines, places = plane_shape
    left = hot(lines, cells // places - plane * lines) * counts.astype(BF16)
    return lax.dot_general(left, hot(places, cells % places), NT, preferred_element_type=F32)


def own_events(event_cell, event_count, k):
    row = pl.ds(k, 1)
    return event_cell[0, row, :], event_count[0, row, :].astype(F32)


def own_counts(event_cell, event_count, out):
    for k in range(SUBS):
        out[k] = plane_counts(sending_side(), *own_events(event_cell, event_count, k), out.shape[1:])


def sections(parcel_rows, event_rows, field_rows):
    sizes = [parcel_rows] * 3 + [event_rows] * 2 + [field_rows] * 2
    starts = [sum(sizes[:i]) for i in range(len(sizes) + 1)]
    return [pl.ds(start, size) for start, size in zip(starts, sizes)], starts[-1]


def packed_events(packed, spans, k, width):
    per = width // LANES
    rows = [packed[pl.ds(span.start + k * per + j, 1)] for span in spans for j in range(per)]
    cells, counts = jnp.concatenate(rows[:per], axis=1), jnp.concatenate(rows[per:], axis=1)
    return cells.astype(jnp.int32), counts


def load_kernel(*refs):
    inputs, live, out, kept, active, counts, sems = refs[:9], refs[9], refs[10], refs[11:20], *refs[20:]
    copies = [pltpu.make_async_copy(src, dst, sems.at[i]) for i, (src, dst) in enumerate(zip(inputs, kept))]
    for copy in copies:
        copy.start()
    for copy in copies:
        copy.wait()
    size, weight, cell, event_cell, event_count, field = kept[:6]
    active[...] = jnp.where(row_numbers(size.shape) < live[0], 1.0, 0.0)
    weight[...] = weight[...] * active[...]
    events, width = event_cell.shape[1:]
    per = width // LANES
    spans, _ = sections(size.shape[0], events * per, field.shape[1])
    out[spans[0]] = size[...]
    out[spans[1]] = weight[...]
    out[spans[2]] = cell[...].astype(F32)
    for span, array in ((spans[3], event_cell), (spans[4], event_count)):
        values = array[0].astype(F32)
        for k in range(events):
            for j in range(per):
                out[pl.ds(span.start + k * per + j, 1)] = values[k : k + 1, j * LANES : (j + 1) * LANES]
    for j in range(2):
        out[spans[5 + j]] = field[0, :, pl.ds(j * LANES, LANES)]

    @pl.when(lax.axis_index("grp") == 1)
    def _():
        own_counts(event_cell, event_count, counts)


def home_kernel(size, weight, cell, event_cell, event_count, counted, out, counts):
    grp = lax.axis_index("grp")

    def own_moments():
        for c, moment in enumerate(plane_moments(sending_side(), size[...], weight[...], cell[...], out.shape[1:])):
            out[c] = moment

    @pl.when(grp == 0)
    def _():
        own_moments()
        own_counts(event_cell, event_count, counts)

    @pl.when(grp == 1)
    def _():
        own_moments()
        counts[...] = counted[...]


def substep(field, zeroth, first, second, counts, grown):
    rate = softplus(field - 1.0)
    growth = GROWTH * rate
    taken = growth * (3.0 * second + growth * (3.0 * first + growth * zeroth))
    field = field - (taken + counts * (NUCLEATE * rate))
    second = second + growth * (2.0 * first + growth * zeroth)
    first = first + growth * zeroth
    return field, first, second, grown + growth


def front_kernel(field, home, home_counts, packed, out, state, *, parcel_rows, events):
    plane_shape = out.shape[1:]
    plane = sending_side()
    spans, _ = sections(parcel_rows, events[0] * events[1] // LANES, plane_shape[0])
    cells = packed[spans[2]].astype(jnp.int32)
    zeroth, first, second = plane_moments(plane, packed[spans[0]], packed[spans[1]], cells, plane_shape)
    zeroth, first, second = zeroth + home[0], first + home[1], second + home[2]
    theirs = jnp.concatenate([packed[spans[5]], packed[spans[6]]], axis=1)
    now = jnp.where(sends_other(), theirs, field[0])
    grown = jnp.zeros_like(now)
    for k in range(SUBS):
        counts = home_counts[k] + plane_counts(plane, *packed_events(packed, spans[3:5], k, events[1]), plane_shape)
        now, first, second, grown = substep(now, zeroth, first, second, counts, grown)
    out[0] = now
    for c, value in enumerate((now, zeroth, first, second, grown)):
        state[c] = value


def pack_kernel(state, inlet, out):
    for c in range(5):
        out[c] = state[c]
    out[5] = inlet[0].astype(F32)


def late_kernel(packed, event_cell, event_count, late, *, parcel_rows):
    plane_shape = late.shape[1:]
    events, width = event_cell.shape[1:]
    spans, _ = sections(parcel_rows, events * width // LANES, plane_shape[0])
    for k in range(SUBS):
        mine = own_events(event_cell, event_count, SUBS + k)
        theirs = packed_events(packed, spans[3:5], SUBS + k, width)
        both = [jnp.concatenate(pair, axis=1) for pair in zip(mine, theirs)]
        late[k] = plane_counts(receiving_side(), *both, plane_shape)


def moved(field):
    lines, places = field.shape
    line = lax.broadcasted_iota(jnp.int32, field.shape, 0)
    place = lax.broadcasted_iota(jnp.int32, field.shape, 1)
    total = jnp.where(line == 0, 0.0, pltpu.roll(field, 1, 0))
    total += jnp.where(line == lines - 1, 0.0, pltpu.roll(field, lines - 1, 0))
    total += jnp.where(place == 0, 0.0, pltpu.roll(field, 1, 1))
    total += jnp.where(place == places - 1, 0.0, pltpu.roll(field, places - 1, 1))
    return total


def split_transport(field, other, inlet, side):
    keep = 1.0 - inlet
    field = field + DIFFUSE * (other + moved(field) - 6.0 * field)
    return keep * field + inlet * INLET, jnp.where(has_beside(side), DIFFUSE * keep, 0.0)


def ready_kernel(mine, other, info, their_info, out, hot_place, lists, *, parts):
    now, zeroth, first, second, grown = (jnp.where(ends(), other[c], mine[c]) for c in range(5))
    partner_field = jnp.where(ends(), mine[0], other[0])
    inlet = jnp.where(receives_other(), other[5], mine[5])
    base, slope = split_transport(now, partner_field, inlet, receiving_side())
    for c, value in enumerate((base, slope, zeroth, first, second, grown)):
        out[c] = value
    half = info.shape[0] // 2
    rows = by_owner(info[pl.ds(half, half)], their_info[pl.ds(0, half)], parts)
    lists[0:1] = jnp.concatenate(rows(2), axis=1) - (receiving_side() * base.shape[0]).astype(F32)
    lists[1:2] = jnp.concatenate(rows(4), axis=1)
    hot_place[...] = hot(base.shape[1], jnp.concatenate(rows(3), axis=1).astype(jnp.int32))


def second_kernel(beside, ready, late, hot_place, lists, front, total, out, *, parts):
    base, slope, zeroth, first, second, grown = (ready[c] for c in range(6))
    now = base + slope * beside[0]
    for k in range(SUBS):
        now, first, second, grown = substep(now, zeroth, first, second, late[k], grown)
    front[0] = now
    total[0] = grown
    stacked = jnp.concatenate(pieces(grown), axis=0)
    found = picked_growth(stacked, hot_place[...], lists[0:1].astype(jnp.int32)) * lists[1:2]
    places = now.shape[1]
    for i in range(2 * parts):
        out[i : i + 1] = found[:, i * places : (i + 1) * places]
    out[2 * parts :] = jnp.zeros((out.shape[0] - 2 * parts, places), F32)


def migrants_kernel(size, weight, cell, rows, count, out, *, places):
    side = receiving_side()
    table_rows = size.shape[0]
    slots = rows.shape[2]
    table, nothing = [], jnp.zeros(size.shape, BF16)
    for values in (size[...], weight[...]):
        stack, rest = [], values
        for _ in range(3):
            part = rest.astype(BF16)
            rest = rest - part.astype(F32)
            stack.append(part)
        table.append(jnp.concatenate(stack, axis=0))
    cells = cell[...]
    for values in (cells // places, cells % places):
        table.append(jnp.concatenate([values.astype(F32).astype(BF16), nothing, nothing], axis=0))
    table = jnp.concatenate(table, axis=1)
    slot = lax.broadcasted_iota(jnp.int32, (1, slots), 1)
    half = out.shape[0] // 2
    for block, j in ((0, side), (half, 1 - side)):
        row = jnp.where(j == 0, rows[0, 0:1, :], rows[0, 1:2, :])
        used = jnp.where(j == 0, count[0:1, 0:1], count[0:1, 1:2])
        valid = jnp.where(slot < used, 1.0, 0.0)
        hot_row = jnp.concatenate([hot(table_rows, row // LANES)] * 3, axis=0)
        picked = lax.dot_general(table, hot_row, TN, preferred_element_type=F32)
        hot_lane = hot(LANES, row % LANES).astype(F32)
        found = [jnp.sum(picked[c * LANES : (c + 1) * LANES] * hot_lane, axis=0, keepdims=True) for c in range(4)]
        sizes, weights = found[0] * valid, found[1] * valid
        at = block
        for value in (sizes, weights, found[2], found[3], valid):
            for start in range(0, slots, places):
                out[at : at + 1] = value[:, start : start + places]
                at += 1
        out[at : block + half] = jnp.zeros((block + half - at, places), F32)


def picked_growth(stacked, hot_place, line):
    lines = stacked.shape[0] // 2
    picked = lax.dot_general(stacked, hot_place, NN, preferred_element_type=F32)
    picked = picked[:lines] + picked[lines:]
    index = lax.broadcasted_iota(jnp.int32, picked.shape, 0)
    return jnp.sum(jnp.where(index == line, picked, 0.0), axis=0, keepdims=True)


def grown_at(stacked, line, place):
    return picked_growth(stacked, hot(stacked.shape[1], place), line)


def both_planes(mine, other):
    first = receiving_side() == 0
    low = jnp.where(first, mine, other)
    high = jnp.where(first, other, mine)
    return jnp.concatenate(pieces(jnp.concatenate([low, high], axis=0)), axis=0)


def by_owner(mine, partners, parts):
    first = lax.axis_index("grp") == 0
    blocks = [jnp.where(first, one, other) for one, other in ((mine, partners), (partners, mine))]
    return lambda c: [block[i : i + 1] for block in blocks for i in range(c * parts, (c + 1) * parts)]


def plane_growth(grown, rows, parts):
    lines, places = grown.shape
    stacked = jnp.concatenate(pieces(grown), axis=0)
    line = jnp.concatenate(rows(2), axis=1).astype(jnp.int32) - receiving_side() * lines
    found = grown_at(stacked, line, jnp.concatenate(rows(3), axis=1).astype(jnp.int32))
    valid = rows(4)
    return [found[:, i * places : (i + 1) * places] * valid[i] for i in range(2 * parts)]


def own_kernel(total, info, their_info, out, *, parts):
    half = info.shape[0] // 2
    rows = by_owner(info[pl.ds(0, half)], their_info[pl.ds(half, half)], parts)
    found = plane_growth(total[0], rows, parts)
    sizes, weights = rows(0), rows(1)
    for i in range(2 * parts):
        at = (i // parts) * 2 * parts + i % parts
        out[at : at + 1] = sizes[i] + found[i]
        out[at + parts : at + parts + 1] = weights[i]


def leaving_kernel(front, own, theirs, out, *, parts):
    lines = front.shape[1]
    out[pl.ds(0, lines)] = front[0]
    for j in range(2):
        at = 2 * parts * j
        out[lines + at : lines + at + parts] = own[at : at + parts] + theirs[j * parts : (j + 1) * parts]
        out[lines + at + parts : lines + at + 2 * parts] = own[at + parts : at + 2 * parts]


def sizes_kernel(total, their_total, size, cell, active, out):
    places = total.shape[2]
    stacked = both_planes(total[0], their_total[0])
    cells = cell[...]
    line = cells // places
    place = cells % places
    group = 4
    found = []
    for start in range(0, size.shape[0], group):
        each = range(start, start + group)
        grown = grown_at(
            stacked,
            jnp.concatenate([line[r : r + 1] for r in each], axis=1),
            jnp.concatenate([place[r : r + 1] for r in each], axis=1),
        )
        found += [grown[:, i * LANES : (i + 1) * LANES] for i in range(group)]
    grown = jnp.concatenate(found, axis=0)
    out[...] = active[...] * (size[...] + grown)


def rest_kernel(front, their_front, inlet, out):
    other = receives_other()
    field = jnp.where(other, their_front[0], front[0])
    beyond = jnp.where(other, front[0], their_front[0])
    out[0], out[1] = split_transport(field, beyond, inlet[0].astype(F32), lax.axis_index("grp"))


def last_kernel(rest, received, relayed, field_out, arrivals_out, *, lines, parts):
    slab, grp = lax.axis_index("slab"), lax.axis_index("grp")
    here = pl.ds(0, lines)
    field_out[0] = rest[0] + rest[1] * jnp.where(sends_other(), relayed[here], received[here])
    rows = 2 * parts
    pick = lambda block: jnp.where(grp == 0, block[lines : lines + rows], block[lines + rows : lines + 2 * rows])
    mine, theirs = pick(received), pick(relayed)
    from_lower = sending_side() == 0
    lower = jnp.where(slab > 0, jnp.where(from_lower, mine, theirs), 0.0)
    upper = jnp.where(slab < lax.axis_size("slab") - 1, jnp.where(from_lower, theirs, mine), 0.0)
    places = mine.shape[1]
    for side, value in enumerate((lower, upper)):
        for v in range(2):
            for p in range(parts):
                at = v * parts + p
                arrivals_out[0, side, v : v + 1, pl.ds(p * places, places)] = value[at : at + 1]


VMEM = pl.BlockSpec(memory_space=pltpu.VMEM)
SMEM = pl.BlockSpec(memory_space=pltpu.SMEM)
HBM = pl.BlockSpec(memory_space=pltpu.HBM)


def shape(*dims):
    return jax.ShapeDtypeStruct(dims, F32)


def call(kernel, out_shape, *args, name, cost=0, limit=16, scratch=(), specs=None):
    return pl.pallas_call(
        kernel,
        out_shape=out_shape,
        in_specs=specs or [VMEM] * len(args),
        out_specs=jax.tree.map(lambda _: VMEM, out_shape),
        scratch_shapes=scratch,
        compiler_params=pltpu.CompilerParams(vmem_limit_bytes=limit << 20),
        cost_estimate=pl.CostEstimate(flops=cost, bytes_accessed=0, transcendentals=0) if cost else None,
        name=name,
    )(*args)


def local(
    saturation,
    inlet_mask,
    crystal_size,
    crystal_weight,
    crystal_cell,
    live_count,
    nucleus_cell,
    nucleus_count,
    migrant_rows,
    migrant_count,
):
    lines, places = saturation.shape[1:]
    slots = migrant_rows.shape[2]
    parts = slots // places
    swap = lambda value: lax.ppermute(value, "grp", [(0, 1), (1, 0)])
    slabs = lax.axis_size("slab")
    across = lambda value, second: lax.ppermute(value, ("slab", "grp"), across_pairs(slabs, second))

    hbm = lambda a: pltpu.with_memory_space_constraint(a, pltpu.HBM)
    like = lambda a: jax.ShapeDtypeStruct(a.shape, a.dtype)
    inputs = [a.reshape(-1, LANES) for a in (crystal_size, crystal_weight, crystal_cell)]
    inputs += [nucleus_cell, nucleus_count, saturation, inlet_mask, migrant_rows, migrant_count]
    parcel_rows, events = inputs[0].shape[0], nucleus_cell.shape[1:]
    _, packed_rows = sections(parcel_rows, events[0] * events[1] // LANES, lines)
    packed, size, weight, cell, event_cell, event_count, field, inlet, rows, count, active, counted = call(
        load_kernel,
        [shape(packed_rows, LANES)]
        + [like(a) for a in inputs]
        + [shape(*inputs[0].shape), shape(SUBS, lines, places)],
        *[hbm(a) for a in inputs],
        live_count,
        specs=[HBM] * 9 + [SMEM],
        scratch=[pltpu.SemaphoreType.DMA((len(inputs),))],
        name="load",
    )
    packed = swap(packed)
    home, counts = call(
        home_kernel, (shape(3, lines, places), shape(SUBS, lines, places)),
        size, weight, cell, event_cell, event_count, counted,
        cost=1 << 30, name="home",
    )
    front, state = call(
        functools.partial(front_kernel, parcel_rows=parcel_rows, events=events),
        (shape(1, lines, places), shape(5, lines, places)), field, home, counts, packed, name="front",
    )
    beside = across(front, False)
    _, state = lax.optimization_barrier((front, state))
    mine = call(pack_kernel, shape(6, lines, places), state, inlet, cost=1 << 28, name="pack")
    other = swap(mine)
    info = call(
        functools.partial(migrants_kernel, places=places), shape(32, places), size, weight, cell, rows, count,
        cost=1 << 33, name="migrants",
    )
    their_info = swap(info)
    late = call(
        functools.partial(late_kernel, parcel_rows=parcel_rows), shape(SUBS, lines, places),
        packed, event_cell, event_count, cost=1 << 28, name="late",
    )
    info, late = lax.optimization_barrier((info, late))
    ready, hot_place, lists = call(
        functools.partial(ready_kernel, parts=parts),
        (shape(6, lines, places), jax.ShapeDtypeStruct((places, 2 * slots), BF16), shape(8, 2 * slots)),
        mine, other, info, their_info, cost=1 << 26, name="ready",
    )
    front, total, given = call(
        functools.partial(second_kernel, parts=parts),
        (shape(1, lines, places), shape(1, lines, places), shape(8, places)),
        beside, ready, late, hot_place, lists, name="second",
    )
    theirs = swap(given)
    own = call(
        functools.partial(own_kernel, parts=parts), shape(4 * parts, places), total, info, their_info,
        cost=1 << 28, name="own",
    )
    leaving = call(
        functools.partial(leaving_kernel, parts=parts), shape(lines + 4 * parts, places), front, own, theirs, name="leaving"
    )
    received = across(leaving, True)
    _, later = lax.optimization_barrier((leaving, total))
    their_total, their_front = swap(later), swap(front)
    size_out = call(
        sizes_kernel, shape(*size.shape), total, their_total, size, cell, active, cost=1 << 26, name="sizes",
    )
    received, size_out = lax.optimization_barrier((received, size_out))
    relayed = swap(received)
    rest = call(rest_kernel, shape(2, lines, places), front, their_front, inlet, cost=1 << 28, name="rest")
    field_out, arrivals = call(
        functools.partial(last_kernel, lines=lines, parts=parts),
        (shape(1, lines, places), shape(1, 2, 2, slots)), rest, received, relayed, name="last",
    )
    return (field_out, size_out.reshape(-1), arrivals)


def solution(mesh):
    in_specs = (
        P(("slab", "grp"), None, None),
        P(("slab", "grp"), None, None),
        P(("slab", "grp")),
        P(("slab", "grp")),
        P(("slab", "grp")),
        P(("slab", "grp")),
        P(("slab", "grp"), None, None),
        P(("slab", "grp"), None, None),
        P(("slab", "grp"), None, None),
        P(("slab", "grp"), None),
    )
    out_specs = (
        P(("slab", "grp"), None, None),
        P(("slab", "grp")),
        P(("slab", "grp"), None, None, None),
    )
    return jax.shard_map(local, mesh=mesh, in_specs=in_specs, out_specs=out_specs, check_vma=False)
```

```python
import functools

import jax
import jax.numpy as jnp
from jax import lax
from jax.experimental import pallas as pl
from jax.experimental.pallas import tpu as pltpu
from jax.sharding import PartitionSpec as P

STEPS = 2
SUBS = 2

GROWTH = 0.08
NUCLEATE = 0.02
DIFFUSE = 0.12
INLET = 4.0

LANES = 128
F32 = jnp.float32
BF16 = jnp.bfloat16
NT = (((1,), (1,)), ((), ()))
NN = (((1,), (0,)), ((), ()))
TN = (((0,), (0,)), ((), ()))


def softplus(x):
    return jnp.maximum(x, 0.0) + jnp.log(1.0 + jnp.exp(-jnp.abs(x)))


def pieces(x):
    high = x.astype(BF16)
    return high, (x - high.astype(F32)).astype(BF16)


def hot(count, row):
    index = lax.broadcasted_iota(jnp.int32, (count, row.shape[1]), 0)
    return jnp.where(index == row, 1.0, 0.0).astype(BF16)


def row_numbers(shape):
    return lax.broadcasted_iota(jnp.int32, shape, 0) * LANES + lax.broadcasted_iota(jnp.int32, shape, 1)


def ends():
    slab = lax.axis_index("slab")
    return (slab == 0) | (slab == lax.axis_size("slab") - 1)


def sends_other():
    return ends() | (lax.axis_index("slab") % 2 == 0)


def receives_other():
    return (lax.axis_index("slab") % 2 == 0) & ~ends()


def sending_side():
    grp = lax.axis_index("grp")
    return jnp.where(sends_other(), 1 - grp, grp)


def receiving_side():
    grp = lax.axis_index("grp")
    return jnp.where(receives_other(), 1 - grp, grp)


def has_beside(side):
    slab = lax.axis_index("slab")
    return jnp.where(side == 0, slab > 0, slab < lax.axis_size("slab") - 1)


def across_pairs(slabs, second):
    last, first_out = slabs - 1, 1 if second else 0
    up_out = lambda s: first_out if s == 0 else s % 2
    up_in = lambda s: 1 - first_out if s == 0 else s % 2
    down_out = lambda s: 1 - first_out if s == last else 1 - s % 2
    down_in = lambda s: first_out if s == last else 1 - s % 2
    pairs = [(s * 2 + up_out(s), (s + 1) * 2 + down_in(s + 1)) for s in range(last)]
    pairs += [((s + 1) * 2 + down_out(s + 1), s * 2 + up_in(s)) for s in range(last)]
    closing = [(1 - first_out, first_out), (last * 2 + first_out, last * 2 + 1 - first_out)]
    return pairs + closing


def plane_moments(plane, sizes, weights, cells, plane_shape):
    lines, places = plane_shape
    first = weights * sizes
    parts = [part.astype(F32) for moment in (weights, first, first * sizes) for part in pieces(moment)]
    line = cells // places - plane * lines
    place = cells % places
    group = 4
    sums = jnp.zeros((len(parts) * lines, places), F32)
    for start in range(0, sizes.shape[0], group):
        left, right = [], []
        for r in range(start, start + group):
            hot_line = hot(lines, line[r : r + 1])
            left.append(jnp.concatenate([hot_line * part[r : r + 1].astype(BF16) for part in parts], axis=0))
            right.append(hot(places, place[r : r + 1]))
        left, right = jnp.concatenate(left, axis=1), jnp.concatenate(right, axis=1)
        sums = sums + lax.dot_general(left, right, NT, preferred_element_type=F32)
    return [sums[2 * c * lines : (2 * c + 1) * lines] + sums[(2 * c + 1) * lines : (2 * c + 2) * lines] for c in range(3)]


def plane_counts(plane, cells, counts, plane_shape):
    lines, places = plane_shape
    left = hot(lines, cells // places - plane * lines) * counts.astype(BF16)
    return lax.dot_general(left, hot(places, cells % places), NT, preferred_element_type=F32)


def own_events(event_cell, event_count, k):
    row = pl.ds(k, 1)
    return event_cell[0, row, :], event_count[0, row, :].astype(F32)


def own_counts(event_cell, event_count, out):
    for k in range(SUBS):
        out[k] = plane_counts(sending_side(), *own_events(event_cell, event_count, k), out.shape[1:])


def sections(parcel_rows, event_rows, field_rows):
    sizes = [parcel_rows] * 3 + [event_rows] * 2 + [field_rows] * 2
    starts = [sum(sizes[:i]) for i in range(len(sizes) + 1)]
    return [pl.ds(start, size) for start, size in zip(starts, sizes)], starts[-1]


def packed_events(packed, spans, k, width):
    per = width // LANES
    rows = [packed[pl.ds(span.start + k * per + j, 1)] for span in spans for j in range(per)]
    cells, counts = jnp.concatenate(rows[:per], axis=1), jnp.concatenate(rows[per:], axis=1)
    return cells.astype(jnp.int32), counts


def load_kernel(*refs):
    inputs, live, out, kept, active, counts, sems = refs[:9], refs[9], refs[10], refs[11:20], *refs[20:]
    copies = [pltpu.make_async_copy(src, dst, sems.at[i]) for i, (src, dst) in enumerate(zip(inputs, kept))]
    for copy in copies:
        copy.start()
    for copy in copies:
        copy.wait()
    size, weight, cell, event_cell, event_count, field = kept[:6]
    active[...] = jnp.where(row_numbers(size.shape) < live[0], 1.0, 0.0)
    weight[...] = weight[...] * active[...]
    events, width = event_cell.shape[1:]
    per = width // LANES
    spans, _ = sections(size.shape[0], events * per, field.shape[1])
    out[spans[0]] = size[...]
    out[spans[1]] = weight[...]
    out[spans[2]] = cell[...].astype(F32)
    for span, array in ((spans[3], event_cell), (spans[4], event_count)):
        values = array[0].astype(F32)
        for k in range(events):
            for j in range(per):
                out[pl.ds(span.start + k * per + j, 1)] = values[k : k + 1, j * LANES : (j + 1) * LANES]
    for j in range(2):
        out[spans[5 + j]] = field[0, :, pl.ds(j * LANES, LANES)]

    @pl.when(lax.axis_index("grp") == 1)
    def _():
        own_counts(event_cell, event_count, counts)


def home_kernel(size, weight, cell, event_cell, event_count, counted, out, counts):
    grp = lax.axis_index("grp")

    def own_moments():
        for c, moment in enumerate(plane_moments(sending_side(), size[...], weight[...], cell[...], out.shape[1:])):
            out[c] = moment

    @pl.when(grp == 0)
    def _():
        own_moments()
        own_counts(event_cell, event_count, counts)

    @pl.when(grp == 1)
    def _():
        own_moments()
        counts[...] = counted[...]


def substep(field, zeroth, first, second, counts, grown):
    rate = softplus(field - 1.0)
    growth = GROWTH * rate
    taken = growth * (3.0 * second + growth * (3.0 * first + growth * zeroth))
    field = field - (taken + counts * (NUCLEATE * rate))
    second = second + growth * (2.0 * first + growth * zeroth)
    first = first + growth * zeroth
    return field, first, second, grown + growth


def front_kernel(field, home, home_counts, packed, out, state, *, parcel_rows, events):
    plane_shape = out.shape[1:]
    plane = sending_side()
    spans, _ = sections(parcel_rows, events[0] * events[1] // LANES, plane_shape[0])
    cells = packed[spans[2]].astype(jnp.int32)
    zeroth, first, second = plane_moments(plane, packed[spans[0]], packed[spans[1]], cells, plane_shape)
    zeroth, first, second = zeroth + home[0], first + home[1], second + home[2]
    theirs = jnp.concatenate([packed[spans[5]], packed[spans[6]]], axis=1)
    now = jnp.where(sends_other(), theirs, field[0])
    grown = jnp.zeros_like(now)
    for k in range(SUBS):
        counts = home_counts[k] + plane_counts(plane, *packed_events(packed, spans[3:5], k, events[1]), plane_shape)
        now, first, second, grown = substep(now, zeroth, first, second, counts, grown)
    out[0] = now
    for c, value in enumerate((now, zeroth, first, second, grown)):
        state[c] = value


def pack_kernel(state, inlet, out):
    for c in range(5):
        out[c] = state[c]
    out[5] = inlet[0].astype(F32)


def late_kernel(packed, event_cell, event_count, late, *, parcel_rows):
    plane_shape = late.shape[1:]
    events, width = event_cell.shape[1:]
    spans, _ = sections(parcel_rows, events * width // LANES, plane_shape[0])
    for k in range(SUBS):
        mine = own_events(event_cell, event_count, SUBS + k)
        theirs = packed_events(packed, spans[3:5], SUBS + k, width)
        both = [jnp.concatenate(pair, axis=1) for pair in zip(mine, theirs)]
        late[k] = plane_counts(receiving_side(), *both, plane_shape)


def moved(field):
    lines, places = field.shape
    line = lax.broadcasted_iota(jnp.int32, field.shape, 0)
    place = lax.broadcasted_iota(jnp.int32, field.shape, 1)
    total = jnp.where(line == 0, 0.0, pltpu.roll(field, 1, 0))
    total += jnp.where(line == lines - 1, 0.0, pltpu.roll(field, lines - 1, 0))
    total += jnp.where(place == 0, 0.0, pltpu.roll(field, 1, 1))
    total += jnp.where(place == places - 1, 0.0, pltpu.roll(field, places - 1, 1))
    return total


def split_transport(field, other, inlet, side):
    keep = 1.0 - inlet
    field = field + DIFFUSE * (other + moved(field) - 6.0 * field)
    return keep * field + inlet * INLET, jnp.where(has_beside(side), DIFFUSE * keep, 0.0)


def ready_kernel(mine, other, info, their_info, out, hot_place, lists, *, parts):
    now, zeroth, first, second, grown = (jnp.where(ends(), other[c], mine[c]) for c in range(5))
    partner_field = jnp.where(ends(), mine[0], other[0])
    inlet = jnp.where(receives_other(), other[5], mine[5])
    base, slope = split_transport(now, partner_field, inlet, receiving_side())
    for c, value in enumerate((base, slope, zeroth, first, second, grown)):
        out[c] = value
    half = info.shape[0] // 2
    rows = by_owner(info[pl.ds(half, half)], their_info[pl.ds(0, half)], parts)
    lists[0:1] = jnp.concatenate(rows(2), axis=1) - (receiving_side() * base.shape[0]).astype(F32)
    lists[1:2] = jnp.concatenate(rows(4), axis=1)
    hot_place[...] = hot(base.shape[1], jnp.concatenate(rows(3), axis=1).astype(jnp.int32))


def second_substeps(beside, ready, late):
    base, slope, zeroth, first, second, grown = (ready[c] for c in range(6))
    now = base + slope * beside[0]
    for k in range(SUBS):
        now, first, second, grown = substep(now, zeroth, first, second, late[k], grown)
    return now, grown


def second_kernel(beside, ready, late, hot_place, lists, out, *, parts):
    _, grown = second_substeps(beside, ready, late)
    stacked = jnp.concatenate(pieces(grown), axis=0)
    found = picked_growth(stacked, hot_place[...], lists[0:1].astype(jnp.int32)) * lists[1:2]
    places = grown.shape[1]
    for i in range(2 * parts):
        out[i : i + 1] = found[:, i * places : (i + 1) * places]
    out[2 * parts :] = jnp.zeros((out.shape[0] - 2 * parts, places), F32)


def migrants_kernel(size, weight, cell, rows, count, out, *, places):
    side = receiving_side()
    table_rows = size.shape[0]
    slots = rows.shape[2]
    table, nothing = [], jnp.zeros(size.shape, BF16)
    for values in (size[...], weight[...]):
        stack, rest = [], values
        for _ in range(3):
            part = rest.astype(BF16)
            rest = rest - part.astype(F32)
            stack.append(part)
        table.append(jnp.concatenate(stack, axis=0))
    cells = cell[...]
    for values in (cells // places, cells % places):
        table.append(jnp.concatenate([values.astype(F32).astype(BF16), nothing, nothing], axis=0))
    table = jnp.concatenate(table, axis=1)
    slot = lax.broadcasted_iota(jnp.int32, (1, slots), 1)
    half = out.shape[0] // 2
    for block, j in ((0, side), (half, 1 - side)):
        row = jnp.where(j == 0, rows[0, 0:1, :], rows[0, 1:2, :])
        used = jnp.where(j == 0, count[0:1, 0:1], count[0:1, 1:2])
        valid = jnp.where(slot < used, 1.0, 0.0)
        hot_row = jnp.concatenate([hot(table_rows, row // LANES)] * 3, axis=0)
        picked = lax.dot_general(table, hot_row, TN, preferred_element_type=F32)
        hot_lane = hot(LANES, row % LANES).astype(F32)
        found = [jnp.sum(picked[c * LANES : (c + 1) * LANES] * hot_lane, axis=0, keepdims=True) for c in range(4)]
        sizes, weights = found[0] * valid, found[1] * valid
        at = block
        for value in (sizes, weights, found[2], found[3], valid):
            for start in range(0, slots, places):
                out[at : at + 1] = value[:, start : start + places]
                at += 1
        out[at : block + half] = jnp.zeros((block + half - at, places), F32)


def picked_growth(stacked, hot_place, line):
    lines = stacked.shape[0] // 2
    picked = lax.dot_general(stacked, hot_place, NN, preferred_element_type=F32)
    picked = picked[:lines] + picked[lines:]
    index = lax.broadcasted_iota(jnp.int32, picked.shape, 0)
    return jnp.sum(jnp.where(index == line, picked, 0.0), axis=0, keepdims=True)


def grown_at(stacked, line, place):
    return picked_growth(stacked, hot(stacked.shape[1], place), line)


def both_planes(mine, other):
    first = receiving_side() == 0
    low = jnp.where(first, mine, other)
    high = jnp.where(first, other, mine)
    return jnp.concatenate(pieces(jnp.concatenate([low, high], axis=0)), axis=0)


def by_owner(mine, partners, parts):
    first = lax.axis_index("grp") == 0
    blocks = [jnp.where(first, one, other) for one, other in ((mine, partners), (partners, mine))]
    return lambda c: [block[i : i + 1] for block in blocks for i in range(c * parts, (c + 1) * parts)]


def plane_growth(grown, rows, parts):
    lines, places = grown.shape
    stacked = jnp.concatenate(pieces(grown), axis=0)
    line = jnp.concatenate(rows(2), axis=1).astype(jnp.int32) - receiving_side() * lines
    found = grown_at(stacked, line, jnp.concatenate(rows(3), axis=1).astype(jnp.int32))
    valid = rows(4)
    return [found[:, i * places : (i + 1) * places] * valid[i] for i in range(2 * parts)]


def own_kernel(beside, ready, late, info, their_info, out, front, total, *, parts):
    front[0], total[0] = second_substeps(beside, ready, late)
    half = info.shape[0] // 2
    rows = by_owner(info[pl.ds(0, half)], their_info[pl.ds(half, half)], parts)
    found = plane_growth(total[0], rows, parts)
    sizes, weights = rows(0), rows(1)
    for i in range(2 * parts):
        at = (i // parts) * 2 * parts + i % parts
        out[at : at + 1] = sizes[i] + found[i]
        out[at + parts : at + parts + 1] = weights[i]


def leaving_kernel(front, own, theirs, out, *, parts):
    lines = front.shape[1]
    out[pl.ds(0, lines)] = front[0]
    for j in range(2):
        at = 2 * parts * j
        out[lines + at : lines + at + parts] = own[at : at + parts] + theirs[j * parts : (j + 1) * parts]
        out[lines + at + parts : lines + at + 2 * parts] = own[at + parts : at + 2 * parts]


def sizes_kernel(total, their_total, size, cell, active, out):
    places = total.shape[2]
    stacked = both_planes(total[0], their_total[0])
    cells = cell[...]
    line = cells // places
    place = cells % places
    group = 4
    found = []
    for start in range(0, size.shape[0], group):
        each = range(start, start + group)
        grown = grown_at(
            stacked,
            jnp.concatenate([line[r : r + 1] for r in each], axis=1),
            jnp.concatenate([place[r : r + 1] for r in each], axis=1),
        )
        found += [grown[:, i * LANES : (i + 1) * LANES] for i in range(group)]
    grown = jnp.concatenate(found, axis=0)
    out[...] = active[...] * (size[...] + grown)


def rest_kernel(front, their_front, inlet, out):
    other = receives_other()
    field = jnp.where(other, their_front[0], front[0])
    beyond = jnp.where(other, front[0], their_front[0])
    out[0], out[1] = split_transport(field, beyond, inlet[0].astype(F32), lax.axis_index("grp"))


def last_kernel(rest, received, relayed, field_out, arrivals_out, *, lines, parts):
    slab, grp = lax.axis_index("slab"), lax.axis_index("grp")
    here = pl.ds(0, lines)
    field_out[0] = rest[0] + rest[1] * jnp.where(sends_other(), relayed[here], received[here])
    rows = 2 * parts
    pick = lambda block: jnp.where(grp == 0, block[lines : lines + rows], block[lines + rows : lines + 2 * rows])
    mine, theirs = pick(received), pick(relayed)
    from_lower = sending_side() == 0
    lower = jnp.where(slab > 0, jnp.where(from_lower, mine, theirs), 0.0)
    upper = jnp.where(slab < lax.axis_size("slab") - 1, jnp.where(from_lower, theirs, mine), 0.0)
    places = mine.shape[1]
    for side, value in enumerate((lower, upper)):
        for v in range(2):
            for p in range(parts):
                at = v * parts + p
                arrivals_out[0, side, v : v + 1, pl.ds(p * places, places)] = value[at : at + 1]


VMEM = pl.BlockSpec(memory_space=pltpu.VMEM)
SMEM = pl.BlockSpec(memory_space=pltpu.SMEM)
HBM = pl.BlockSpec(memory_space=pltpu.HBM)


def shape(*dims):
    return jax.ShapeDtypeStruct(dims, F32)


def call(kernel, out_shape, *args, name, cost=0, limit=16, scratch=(), specs=None):
    return pl.pallas_call(
        kernel,
        out_shape=out_shape,
        in_specs=specs or [VMEM] * len(args),
        out_specs=jax.tree.map(lambda _: VMEM, out_shape),
        scratch_shapes=scratch,
        compiler_params=pltpu.CompilerParams(vmem_limit_bytes=limit << 20),
        cost_estimate=pl.CostEstimate(flops=cost, bytes_accessed=0, transcendentals=0) if cost else None,
        name=name,
    )(*args)


def local(
    saturation,
    inlet_mask,
    crystal_size,
    crystal_weight,
    crystal_cell,
    live_count,
    nucleus_cell,
    nucleus_count,
    migrant_rows,
    migrant_count,
):
    lines, places = saturation.shape[1:]
    slots = migrant_rows.shape[2]
    parts = slots // places
    swap = lambda value: lax.ppermute(value, "grp", [(0, 1), (1, 0)])
    slabs = lax.axis_size("slab")
    across = lambda value, second: lax.ppermute(value, ("slab", "grp"), across_pairs(slabs, second))

    hbm = lambda a: pltpu.with_memory_space_constraint(a, pltpu.HBM)
    like = lambda a: jax.ShapeDtypeStruct(a.shape, a.dtype)
    inputs = [a.reshape(-1, LANES) for a in (crystal_size, crystal_weight, crystal_cell)]
    inputs += [nucleus_cell, nucleus_count, saturation, inlet_mask, migrant_rows, migrant_count]
    parcel_rows, events = inputs[0].shape[0], nucleus_cell.shape[1:]
    _, packed_rows = sections(parcel_rows, events[0] * events[1] // LANES, lines)
    packed, size, weight, cell, event_cell, event_count, field, inlet, rows, count, active, counted = call(
        load_kernel,
        [shape(packed_rows, LANES)]
        + [like(a) for a in inputs]
        + [shape(*inputs[0].shape), shape(SUBS, lines, places)],
        *[hbm(a) for a in inputs],
        live_count,
        specs=[HBM] * 9 + [SMEM],
        scratch=[pltpu.SemaphoreType.DMA((len(inputs),))],
        name="load",
    )
    packed = swap(packed)
    home, counts = call(
        home_kernel, (shape(3, lines, places), shape(SUBS, lines, places)),
        size, weight, cell, event_cell, event_count, counted,
        cost=1 << 30, name="home",
    )
    front, state = call(
        functools.partial(front_kernel, parcel_rows=parcel_rows, events=events),
        (shape(1, lines, places), shape(5, lines, places)), field, home, counts, packed, name="front",
    )
    beside = across(front, False)
    _, state = lax.optimization_barrier((front, state))
    mine = call(pack_kernel, shape(6, lines, places), state, inlet, cost=1 << 28, name="pack")
    other = swap(mine)
    info = call(
        functools.partial(migrants_kernel, places=places), shape(32, places), size, weight, cell, rows, count,
        cost=1 << 33, name="migrants",
    )
    their_info = swap(info)
    late = call(
        functools.partial(late_kernel, parcel_rows=parcel_rows), shape(SUBS, lines, places),
        packed, event_cell, event_count, cost=1 << 28, name="late",
    )
    info, late = lax.optimization_barrier((info, late))
    ready, hot_place, lists = call(
        functools.partial(ready_kernel, parts=parts),
        (shape(6, lines, places), jax.ShapeDtypeStruct((places, 2 * slots), BF16), shape(8, 2 * slots)),
        mine, other, info, their_info, cost=1 << 26, name="ready",
    )
    given = call(
        functools.partial(second_kernel, parts=parts), shape(8, places), beside, ready, late, hot_place, lists,
        name="second",
    )
    theirs = swap(given)
    own, front, total = call(
        functools.partial(own_kernel, parts=parts),
        (shape(4 * parts, places), shape(1, lines, places), shape(1, lines, places)),
        beside, ready, late, info, their_info, cost=1 << 28, name="own",
    )
    leaving = call(
        functools.partial(leaving_kernel, parts=parts), shape(lines + 4 * parts, places), front, own, theirs, name="leaving"
    )
    received = across(leaving, True)
    _, later = lax.optimization_barrier((leaving, total))
    their_total, their_front = swap(later), swap(front)
    size_out = call(
        sizes_kernel, shape(*size.shape), total, their_total, size, cell, active, cost=1 << 26, name="sizes",
    )
    received, size_out = lax.optimization_barrier((received, size_out))
    relayed = swap(received)
    rest = call(rest_kernel, shape(2, lines, places), front, their_front, inlet, cost=1 << 28, name="rest")
    field_out, arrivals = call(
        functools.partial(last_kernel, lines=lines, parts=parts),
        (shape(1, lines, places), shape(1, 2, 2, slots)), rest, received, relayed, name="last",
    )
    return (field_out, size_out.reshape(-1), arrivals)


def solution(mesh):
    in_specs = (
        P(("slab", "grp"), None, None),
        P(("slab", "grp"), None, None),
        P(("slab", "grp")),
        P(("slab", "grp")),
        P(("slab", "grp")),
        P(("slab", "grp")),
        P(("slab", "grp"), None, None),
        P(("slab", "grp"), None, None),
        P(("slab", "grp"), None, None),
        P(("slab", "grp"), None),
    )
    out_specs = (
        P(("slab", "grp"), None, None),
        P(("slab", "grp")),
        P(("slab", "grp"), None, None, None),
    )
    return jax.shard_map(local, mesh=mesh, in_specs=in_specs, out_specs=out_specs, check_vma=False)
```

```python
import functools

import jax
import jax.numpy as jnp
from jax import lax
from jax.experimental import pallas as pl
from jax.experimental.pallas import tpu as pltpu
from jax.sharding import PartitionSpec as P

STEPS = 2
SUBS = 2

GROWTH = 0.08
NUCLEATE = 0.02
DIFFUSE = 0.12
INLET = 4.0

LANES = 128
F32 = jnp.float32
BF16 = jnp.bfloat16
NT = (((1,), (1,)), ((), ()))
NN = (((1,), (0,)), ((), ()))
TN = (((0,), (0,)), ((), ()))


def softplus(x):
    return jnp.maximum(x, 0.0) + jnp.log(1.0 + jnp.exp(-jnp.abs(x)))


def pieces(x):
    high = x.astype(BF16)
    return high, (x - high.astype(F32)).astype(BF16)


def hot(count, row):
    index = lax.broadcasted_iota(jnp.int32, (count, row.shape[1]), 0)
    return jnp.where(index == row, 1.0, 0.0).astype(BF16)


def row_numbers(shape):
    return lax.broadcasted_iota(jnp.int32, shape, 0) * LANES + lax.broadcasted_iota(jnp.int32, shape, 1)


def ends():
    slab = lax.axis_index("slab")
    return (slab == 0) | (slab == lax.axis_size("slab") - 1)


def sends_other():
    return ends() | (lax.axis_index("slab") % 2 == 0)


def receives_other():
    return (lax.axis_index("slab") % 2 == 0) & ~ends()


def sending_side():
    grp = lax.axis_index("grp")
    return jnp.where(sends_other(), 1 - grp, grp)


def receiving_side():
    grp = lax.axis_index("grp")
    return jnp.where(receives_other(), 1 - grp, grp)


def has_beside(side):
    slab = lax.axis_index("slab")
    return jnp.where(side == 0, slab > 0, slab < lax.axis_size("slab") - 1)


def across_pairs(slabs, second):
    last, first_out = slabs - 1, 1 if second else 0
    up_out = lambda s: first_out if s == 0 else s % 2
    up_in = lambda s: 1 - first_out if s == 0 else s % 2
    down_out = lambda s: 1 - first_out if s == last else 1 - s % 2
    down_in = lambda s: first_out if s == last else 1 - s % 2
    pairs = [(s * 2 + up_out(s), (s + 1) * 2 + down_in(s + 1)) for s in range(last)]
    pairs += [((s + 1) * 2 + down_out(s + 1), s * 2 + up_in(s)) for s in range(last)]
    closing = [(1 - first_out, first_out), (last * 2 + first_out, last * 2 + 1 - first_out)]
    return pairs + closing


def plane_moments(plane, sizes, weights, cells, plane_shape):
    lines, places = plane_shape
    first = weights * sizes
    parts = [part.astype(F32) for moment in (weights, first, first * sizes) for part in pieces(moment)]
    line = cells // places - plane * lines
    place = cells % places
    group = 4
    sums = jnp.zeros((len(parts) * lines, places), F32)
    for start in range(0, sizes.shape[0], group):
        left, right = [], []
        for r in range(start, start + group):
            hot_line = hot(lines, line[r : r + 1])
            left.append(jnp.concatenate([hot_line * part[r : r + 1].astype(BF16) for part in parts], axis=0))
            right.append(hot(places, place[r : r + 1]))
        left, right = jnp.concatenate(left, axis=1), jnp.concatenate(right, axis=1)
        sums = sums + lax.dot_general(left, right, NT, preferred_element_type=F32)
    return [sums[2 * c * lines : (2 * c + 1) * lines] + sums[(2 * c + 1) * lines : (2 * c + 2) * lines] for c in range(3)]


def plane_counts(plane, cells, counts, plane_shape):
    lines, places = plane_shape
    left = hot(lines, cells // places - plane * lines) * counts.astype(BF16)
    return lax.dot_general(left, hot(places, cells % places), NT, preferred_element_type=F32)


def own_events(event_cell, event_count, k):
    row = pl.ds(k, 1)
    return event_cell[0, row, :], event_count[0, row, :].astype(F32)


def own_counts(event_cell, event_count, out):
    for k in range(SUBS):
        out[k] = plane_counts(sending_side(), *own_events(event_cell, event_count, k), out.shape[1:])


def sections(parcel_rows, event_rows, field_rows):
    sizes = [parcel_rows] * 3 + [event_rows] * 2 + [field_rows] * 2
    starts = [sum(sizes[:i]) for i in range(len(sizes) + 1)]
    return [pl.ds(start, size) for start, size in zip(starts, sizes)], starts[-1]


def packed_events(packed, spans, k, width):
    per = width // LANES
    rows = [packed[pl.ds(span.start + k * per + j, 1)] for span in spans for j in range(per)]
    cells, counts = jnp.concatenate(rows[:per], axis=1), jnp.concatenate(rows[per:], axis=1)
    return cells.astype(jnp.int32), counts


def load_kernel(*refs):
    inputs, live, out, kept, active, counts, sems = refs[:6], refs[6], refs[7], refs[8:14], *refs[14:]
    copies = [pltpu.make_async_copy(src, dst, sems.at[i]) for i, (src, dst) in enumerate(zip(inputs, kept))]
    for copy in copies:
        copy.start()
    for copy in copies:
        copy.wait()
    size, weight, cell, event_cell, event_count, field = kept[:6]
    active[...] = jnp.where(row_numbers(size.shape) < live[0], 1.0, 0.0)
    weight[...] = weight[...] * active[...]
    events, width = event_cell.shape[1:]
    per = width // LANES
    spans, _ = sections(size.shape[0], events * per, field.shape[1])
    out[spans[0]] = size[...]
    out[spans[1]] = weight[...]
    out[spans[2]] = cell[...].astype(F32)
    for span, array in ((spans[3], event_cell), (spans[4], event_count)):
        values = array[0].astype(F32)
        for k in range(events):
            for j in range(per):
                out[pl.ds(span.start + k * per + j, 1)] = values[k : k + 1, j * LANES : (j + 1) * LANES]
    for j in range(2):
        out[spans[5 + j]] = field[0, :, pl.ds(j * LANES, LANES)]

    @pl.when(lax.axis_index("grp") == 1)
    def _():
        own_counts(event_cell, event_count, counts)


def home_kernel(size, weight, cell, event_cell, event_count, counted, inlet, rows, count, out, counts, *rest):
    kept, sems = rest[:3], rest[3]
    copies = [pltpu.make_async_copy(src, dst, sems.at[i]) for i, (src, dst) in enumerate(zip((inlet, rows, count), kept))]
    for copy in copies:
        copy.start()
    grp = lax.axis_index("grp")

    def own_moments():
        for c, moment in enumerate(plane_moments(sending_side(), size[...], weight[...], cell[...], out.shape[1:])):
            out[c] = moment

    @pl.when(grp == 0)
    def _():
        own_moments()
        own_counts(event_cell, event_count, counts)

    @pl.when(grp == 1)
    def _():
        own_moments()
        counts[...] = counted[...]

    for copy in copies:
        copy.wait()


def substep(field, zeroth, first, second, counts, grown):
    rate = softplus(field - 1.0)
    growth = GROWTH * rate
    taken = growth * (3.0 * second + growth * (3.0 * first + growth * zeroth))
    field = field - (taken + counts * (NUCLEATE * rate))
    second = second + growth * (2.0 * first + growth * zeroth)
    first = first + growth * zeroth
    return field, first, second, grown + growth


def front_kernel(field, home, home_counts, packed, out, state, *, parcel_rows, events):
    plane_shape = out.shape[1:]
    plane = sending_side()
    spans, _ = sections(parcel_rows, events[0] * events[1] // LANES, plane_shape[0])
    cells = packed[spans[2]].astype(jnp.int32)
    zeroth, first, second = plane_moments(plane, packed[spans[0]], packed[spans[1]], cells, plane_shape)
    zeroth, first, second = zeroth + home[0], first + home[1], second + home[2]
    theirs = jnp.concatenate([packed[spans[5]], packed[spans[6]]], axis=1)
    now = jnp.where(sends_other(), theirs, field[0])
    grown = jnp.zeros_like(now)
    for k in range(SUBS):
        counts = home_counts[k] + plane_counts(plane, *packed_events(packed, spans[3:5], k, events[1]), plane_shape)
        now, first, second, grown = substep(now, zeroth, first, second, counts, grown)
    out[0] = now
    for c, value in enumerate((now, zeroth, first, second, grown)):
        state[c] = value


def pack_kernel(state, inlet, out):
    for c in range(5):
        out[c] = state[c]
    out[5] = inlet[0].astype(F32)


def late_kernel(packed, event_cell, event_count, late, *, parcel_rows):
    plane_shape = late.shape[1:]
    events, width = event_cell.shape[1:]
    spans, _ = sections(parcel_rows, events * width // LANES, plane_shape[0])
    for k in range(SUBS):
        mine = own_events(event_cell, event_count, SUBS + k)
        theirs = packed_events(packed, spans[3:5], SUBS + k, width)
        both = [jnp.concatenate(pair, axis=1) for pair in zip(mine, theirs)]
        late[k] = plane_counts(receiving_side(), *both, plane_shape)


def moved(field):
    lines, places = field.shape
    line = lax.broadcasted_iota(jnp.int32, field.shape, 0)
    place = lax.broadcasted_iota(jnp.int32, field.shape, 1)
    total = jnp.where(line == 0, 0.0, pltpu.roll(field, 1, 0))
    total += jnp.where(line == lines - 1, 0.0, pltpu.roll(field, lines - 1, 0))
    total += jnp.where(place == 0, 0.0, pltpu.roll(field, 1, 1))
    total += jnp.where(place == places - 1, 0.0, pltpu.roll(field, places - 1, 1))
    return total


def split_transport(field, other, inlet, side):
    keep = 1.0 - inlet
    field = field + DIFFUSE * (other + moved(field) - 6.0 * field)
    return keep * field + inlet * INLET, jnp.where(has_beside(side), DIFFUSE * keep, 0.0)


def ready_kernel(mine, other, info, their_info, out, hot_place, lists, *, parts):
    now, zeroth, first, second, grown = (jnp.where(ends(), other[c], mine[c]) for c in range(5))
    partner_field = jnp.where(ends(), mine[0], other[0])
    inlet = jnp.where(receives_other(), other[5], mine[5])
    base, slope = split_transport(now, partner_field, inlet, receiving_side())
    for c, value in enumerate((base, slope, zeroth, first, second, grown)):
        out[c] = value
    half = info.shape[0] // 2
    rows = by_owner(info[pl.ds(half, half)], their_info[pl.ds(0, half)], parts)
    lists[0:1] = jnp.concatenate(rows(2), axis=1) - (receiving_side() * base.shape[0]).astype(F32)
    lists[1:2] = jnp.concatenate(rows(4), axis=1)
    hot_place[...] = hot(base.shape[1], jnp.concatenate(rows(3), axis=1).astype(jnp.int32))


def second_substeps(beside, ready, late):
    base, slope, zeroth, first, second, grown = (ready[c] for c in range(6))
    now = base + slope * beside[0]
    for k in range(SUBS):
        now, first, second, grown = substep(now, zeroth, first, second, late[k], grown)
    return now, grown


def second_kernel(beside, ready, late, hot_place, lists, out, *, parts):
    _, grown = second_substeps(beside, ready, late)
    stacked = jnp.concatenate(pieces(grown), axis=0)
    found = picked_growth(stacked, hot_place[...], lists[0:1].astype(jnp.int32)) * lists[1:2]
    places = grown.shape[1]
    for i in range(2 * parts):
        out[i : i + 1] = found[:, i * places : (i + 1) * places]
    out[2 * parts :] = jnp.zeros((out.shape[0] - 2 * parts, places), F32)


def migrants_kernel(size, weight, cell, rows, count, out, *, places):
    side = receiving_side()
    table_rows = size.shape[0]
    slots = rows.shape[2]
    table, nothing = [], jnp.zeros(size.shape, BF16)
    for values in (size[...], weight[...]):
        stack, rest = [], values
        for _ in range(3):
            part = rest.astype(BF16)
            rest = rest - part.astype(F32)
            stack.append(part)
        table.append(jnp.concatenate(stack, axis=0))
    cells = cell[...]
    for values in (cells // places, cells % places):
        table.append(jnp.concatenate([values.astype(F32).astype(BF16), nothing, nothing], axis=0))
    table = jnp.concatenate(table, axis=1)
    slot = lax.broadcasted_iota(jnp.int32, (1, slots), 1)
    half = out.shape[0] // 2
    for block, j in ((0, side), (half, 1 - side)):
        row = jnp.where(j == 0, rows[0, 0:1, :], rows[0, 1:2, :])
        used = jnp.where(j == 0, count[0:1, 0:1], count[0:1, 1:2])
        valid = jnp.where(slot < used, 1.0, 0.0)
        hot_row = jnp.concatenate([hot(table_rows, row // LANES)] * 3, axis=0)
        picked = lax.dot_general(table, hot_row, TN, preferred_element_type=F32)
        hot_lane = hot(LANES, row % LANES).astype(F32)
        found = [jnp.sum(picked[c * LANES : (c + 1) * LANES] * hot_lane, axis=0, keepdims=True) for c in range(4)]
        sizes, weights = found[0] * valid, found[1] * valid
        at = block
        for value in (sizes, weights, found[2], found[3], valid):
            for start in range(0, slots, places):
                out[at : at + 1] = value[:, start : start + places]
                at += 1
        out[at : block + half] = jnp.zeros((block + half - at, places), F32)


def picked_growth(stacked, hot_place, line):
    lines = stacked.shape[0] // 2
    picked = lax.dot_general(stacked, hot_place, NN, preferred_element_type=F32)
    picked = picked[:lines] + picked[lines:]
    index = lax.broadcasted_iota(jnp.int32, picked.shape, 0)
    return jnp.sum(jnp.where(index == line, picked, 0.0), axis=0, keepdims=True)


def grown_at(stacked, line, place):
    return picked_growth(stacked, hot(stacked.shape[1], place), line)


def both_planes(mine, other):
    first = receiving_side() == 0
    low = jnp.where(first, mine, other)
    high = jnp.where(first, other, mine)
    return jnp.concatenate(pieces(jnp.concatenate([low, high], axis=0)), axis=0)


def by_owner(mine, partners, parts):
    first = lax.axis_index("grp") == 0
    blocks = [jnp.where(first, one, other) for one, other in ((mine, partners), (partners, mine))]
    return lambda c: [block[i : i + 1] for block in blocks for i in range(c * parts, (c + 1) * parts)]


def plane_growth(grown, rows, parts):
    lines, places = grown.shape
    stacked = jnp.concatenate(pieces(grown), axis=0)
    line = jnp.concatenate(rows(2), axis=1).astype(jnp.int32) - receiving_side() * lines
    found = grown_at(stacked, line, jnp.concatenate(rows(3), axis=1).astype(jnp.int32))
    valid = rows(4)
    return [found[:, i * places : (i + 1) * places] * valid[i] for i in range(2 * parts)]


def own_kernel(beside, ready, late, info, their_info, out, front, total, *, parts):
    front[0], total[0] = second_substeps(beside, ready, late)
    half = info.shape[0] // 2
    rows = by_owner(info[pl.ds(0, half)], their_info[pl.ds(half, half)], parts)
    found = plane_growth(total[0], rows, parts)
    sizes, weights = rows(0), rows(1)
    for i in range(2 * parts):
        at = (i // parts) * 2 * parts + i % parts
        out[at : at + 1] = sizes[i] + found[i]
        out[at + parts : at + parts + 1] = weights[i]


def leaving_kernel(front, own, theirs, out, *, parts):
    lines = front.shape[1]
    out[pl.ds(0, lines)] = front[0]
    for j in range(2):
        at = 2 * parts * j
        out[lines + at : lines + at + parts] = own[at : at + parts] + theirs[j * parts : (j + 1) * parts]
        out[lines + at + parts : lines + at + 2 * parts] = own[at + parts : at + 2 * parts]


def sizes_kernel(total, their_total, size, cell, active, out):
    places = total.shape[2]
    stacked = both_planes(total[0], their_total[0])
    cells = cell[...]
    line = cells // places
    place = cells % places
    group = 4
    found = []
    for start in range(0, size.shape[0], group):
        each = range(start, start + group)
        grown = grown_at(
            stacked,
            jnp.concatenate([line[r : r + 1] for r in each], axis=1),
            jnp.concatenate([place[r : r + 1] for r in each], axis=1),
        )
        found += [grown[:, i * LANES : (i + 1) * LANES] for i in range(group)]
    grown = jnp.concatenate(found, axis=0)
    out[...] = active[...] * (size[...] + grown)


def rest_kernel(front, their_front, inlet, out):
    other = receives_other()
    field = jnp.where(other, their_front[0], front[0])
    beyond = jnp.where(other, front[0], their_front[0])
    out[0], out[1] = split_transport(field, beyond, inlet[0].astype(F32), lax.axis_index("grp"))


def last_kernel(rest, received, relayed, field_out, arrivals_out, *, lines, parts):
    slab, grp = lax.axis_index("slab"), lax.axis_index("grp")
    here = pl.ds(0, lines)
    field_out[0] = rest[0] + rest[1] * jnp.where(sends_other(), relayed[here], received[here])
    rows = 2 * parts
    pick = lambda block: jnp.where(grp == 0, block[lines : lines + rows], block[lines + rows : lines + 2 * rows])
    mine, theirs = pick(received), pick(relayed)
    from_lower = sending_side() == 0
    lower = jnp.where(slab > 0, jnp.where(from_lower, mine, theirs), 0.0)
    upper = jnp.where(slab < lax.axis_size("slab") - 1, jnp.where(from_lower, theirs, mine), 0.0)
    places = mine.shape[1]
    for side, value in enumerate((lower, upper)):
        for v in range(2):
            for p in range(parts):
                at = v * parts + p
                arrivals_out[0, side, v : v + 1, pl.ds(p * places, places)] = value[at : at + 1]


VMEM = pl.BlockSpec(memory_space=pltpu.VMEM)
SMEM = pl.BlockSpec(memory_space=pltpu.SMEM)
HBM = pl.BlockSpec(memory_space=pltpu.HBM)


def shape(*dims):
    return jax.ShapeDtypeStruct(dims, F32)


def call(kernel, out_shape, *args, name, cost=0, limit=16, scratch=(), specs=None):
    return pl.pallas_call(
        kernel,
        out_shape=out_shape,
        in_specs=specs or [VMEM] * len(args),
        out_specs=jax.tree.map(lambda _: VMEM, out_shape),
        scratch_shapes=scratch,
        compiler_params=pltpu.CompilerParams(vmem_limit_bytes=limit << 20),
        cost_estimate=pl.CostEstimate(flops=cost, bytes_accessed=0, transcendentals=0) if cost else None,
        name=name,
    )(*args)


def local(
    saturation,
    inlet_mask,
    crystal_size,
    crystal_weight,
    crystal_cell,
    live_count,
    nucleus_cell,
    nucleus_count,
    migrant_rows,
    migrant_count,
):
    lines, places = saturation.shape[1:]
    slots = migrant_rows.shape[2]
    parts = slots // places
    swap = lambda value: lax.ppermute(value, "grp", [(0, 1), (1, 0)])
    slabs = lax.axis_size("slab")
    across = lambda value, second: lax.ppermute(value, ("slab", "grp"), across_pairs(slabs, second))

    hbm = lambda a: pltpu.with_memory_space_constraint(a, pltpu.HBM)
    like = lambda a: jax.ShapeDtypeStruct(a.shape, a.dtype)
    inputs = [a.reshape(-1, LANES) for a in (crystal_size, crystal_weight, crystal_cell)]
    inputs += [nucleus_cell, nucleus_count, saturation]
    others = [inlet_mask, migrant_rows, migrant_count]
    parcel_rows, events = inputs[0].shape[0], nucleus_cell.shape[1:]
    _, packed_rows = sections(parcel_rows, events[0] * events[1] // LANES, lines)
    packed, size, weight, cell, event_cell, event_count, field, active, counted = call(
        load_kernel,
        [shape(packed_rows, LANES)]
        + [like(a) for a in inputs]
        + [shape(*inputs[0].shape), shape(SUBS, lines, places)],
        *[hbm(a) for a in inputs],
        live_count,
        specs=[HBM] * 6 + [SMEM],
        scratch=[pltpu.SemaphoreType.DMA((len(inputs),))],
        name="load",
    )
    packed = swap(packed)
    home, counts, inlet, rows, count = call(
        home_kernel, [shape(3, lines, places), shape(SUBS, lines, places)] + [like(a) for a in others],
        size, weight, cell, event_cell, event_count, counted, *[hbm(a) for a in others],
        specs=[VMEM] * 6 + [HBM] * 3, scratch=[pltpu.SemaphoreType.DMA((3,))],
        cost=1 << 30, name="home",
    )
    front, state = call(
        functools.partial(front_kernel, parcel_rows=parcel_rows, events=events),
        (shape(1, lines, places), shape(5, lines, places)), field, home, counts, packed, name="front",
    )
    beside = across(front, False)
    _, state = lax.optimization_barrier((front, state))
    mine = call(pack_kernel, shape(6, lines, places), state, inlet, cost=1 << 28, name="pack")
    other = swap(mine)
    info = call(
        functools.partial(migrants_kernel, places=places), shape(32, places), size, weight, cell, rows, count,
        cost=1 << 33, name="migrants",
    )
    their_info = swap(info)
    late = call(
        functools.partial(late_kernel, parcel_rows=parcel_rows), shape(SUBS, lines, places),
        packed, event_cell, event_count, cost=1 << 28, name="late",
    )
    info, late = lax.optimization_barrier((info, late))
    ready, hot_place, lists = call(
        functools.partial(ready_kernel, parts=parts),
        (shape(6, lines, places), jax.ShapeDtypeStruct((places, 2 * slots), BF16), shape(8, 2 * slots)),
        mine, other, info, their_info, cost=1 << 26, name="ready",
    )
    given = call(
        functools.partial(second_kernel, parts=parts), shape(8, places), beside, ready, late, hot_place, lists,
        name="second",
    )
    theirs = swap(given)
    own, front, total = call(
        functools.partial(own_kernel, parts=parts),
        (shape(4 * parts, places), shape(1, lines, places), shape(1, lines, places)),
        beside, ready, late, info, their_info, cost=1 << 28, name="own",
    )
    leaving = call(
        functools.partial(leaving_kernel, parts=parts), shape(lines + 4 * parts, places), front, own, theirs, name="leaving"
    )
    received = across(leaving, True)
    _, later = lax.optimization_barrier((leaving, total))
    their_total, their_front = swap(later), swap(front)
    size_out = call(
        sizes_kernel, shape(*size.shape), total, their_total, size, cell, active, cost=1 << 26, name="sizes",
    )
    received, size_out = lax.optimization_barrier((received, size_out))
    relayed = swap(received)
    rest = call(rest_kernel, shape(2, lines, places), front, their_front, inlet, cost=1 << 28, name="rest")
    field_out, arrivals = call(
        functools.partial(last_kernel, lines=lines, parts=parts),
        (shape(1, lines, places), shape(1, 2, 2, slots)), rest, received, relayed, name="last",
    )
    return (field_out, size_out.reshape(-1), arrivals)


def solution(mesh):
    in_specs = (
        P(("slab", "grp"), None, None),
        P(("slab", "grp"), None, None),
        P(("slab", "grp")),
        P(("slab", "grp")),
        P(("slab", "grp")),
        P(("slab", "grp")),
        P(("slab", "grp"), None, None),
        P(("slab", "grp"), None, None),
        P(("slab", "grp"), None, None),
        P(("slab", "grp"), None),
    )
    out_specs = (
        P(("slab", "grp"), None, None),
        P(("slab", "grp")),
        P(("slab", "grp"), None, None, None),
    )
    return jax.shard_map(local, mesh=mesh, in_specs=in_specs, out_specs=out_specs, check_vma=False)
```

```python
import functools

import jax
import jax.numpy as jnp
from jax import lax
from jax.experimental import pallas as pl
from jax.experimental.pallas import tpu as pltpu
from jax.sharding import PartitionSpec as P

STEPS = 2
SUBS = 2

GROWTH = 0.08
NUCLEATE = 0.02
DIFFUSE = 0.12
INLET = 4.0

LANES = 128
F32 = jnp.float32
BF16 = jnp.bfloat16
NT = (((1,), (1,)), ((), ()))
NN = (((1,), (0,)), ((), ()))
TN = (((0,), (0,)), ((), ()))


def softplus(x):
    return jnp.maximum(x, 0.0) + jnp.log(1.0 + jnp.exp(-jnp.abs(x)))


def pieces(x):
    high = x.astype(BF16)
    return high, (x - high.astype(F32)).astype(BF16)


def hot(count, row):
    index = lax.broadcasted_iota(jnp.int32, (count, row.shape[1]), 0)
    return jnp.where(index == row, 1.0, 0.0).astype(BF16)


def row_numbers(shape):
    return lax.broadcasted_iota(jnp.int32, shape, 0) * LANES + lax.broadcasted_iota(jnp.int32, shape, 1)


def ends():
    slab = lax.axis_index("slab")
    return (slab == 0) | (slab == lax.axis_size("slab") - 1)


def sends_other():
    return ends() | (lax.axis_index("slab") % 2 == 0)


def receives_other():
    return (lax.axis_index("slab") % 2 == 0) & ~ends()


def sending_side():
    grp = lax.axis_index("grp")
    return jnp.where(sends_other(), 1 - grp, grp)


def receiving_side():
    grp = lax.axis_index("grp")
    return jnp.where(receives_other(), 1 - grp, grp)


def has_beside(side):
    slab = lax.axis_index("slab")
    return jnp.where(side == 0, slab > 0, slab < lax.axis_size("slab") - 1)


def across_pairs(slabs, second):
    last, first_out = slabs - 1, 1 if second else 0
    up_out = lambda s: first_out if s == 0 else s % 2
    up_in = lambda s: 1 - first_out if s == 0 else s % 2
    down_out = lambda s: 1 - first_out if s == last else 1 - s % 2
    down_in = lambda s: first_out if s == last else 1 - s % 2
    pairs = [(s * 2 + up_out(s), (s + 1) * 2 + down_in(s + 1)) for s in range(last)]
    pairs += [((s + 1) * 2 + down_out(s + 1), s * 2 + up_in(s)) for s in range(last)]
    closing = [(1 - first_out, first_out), (last * 2 + first_out, last * 2 + 1 - first_out)]
    return pairs + closing


def plane_moments(plane, sizes, weights, cells, plane_shape):
    lines, places = plane_shape
    first = weights * sizes
    parts = [part.astype(F32) for moment in (weights, first, first * sizes) for part in pieces(moment)]
    line = cells // places - plane * lines
    place = cells % places
    group = 4
    sums = jnp.zeros((len(parts) * lines, places), F32)
    for start in range(0, sizes.shape[0], group):
        left, right = [], []
        for r in range(start, start + group):
            hot_line = hot(lines, line[r : r + 1])
            left.append(jnp.concatenate([hot_line * part[r : r + 1].astype(BF16) for part in parts], axis=0))
            right.append(hot(places, place[r : r + 1]))
        left, right = jnp.concatenate(left, axis=1), jnp.concatenate(right, axis=1)
        sums = sums + lax.dot_general(left, right, NT, preferred_element_type=F32)
    return [sums[2 * c * lines : (2 * c + 1) * lines] + sums[(2 * c + 1) * lines : (2 * c + 2) * lines] for c in range(3)]


def plane_counts(plane, cells, counts, plane_shape):
    lines, places = plane_shape
    left = hot(lines, cells // places - plane * lines) * counts.astype(BF16)
    return lax.dot_general(left, hot(places, cells % places), NT, preferred_element_type=F32)


def own_events(event_cell, event_count, k):
    row = pl.ds(k, 1)
    return event_cell[0, row, :], event_count[0, row, :].astype(F32)


def own_counts(event_cell, event_count, out):
    for k in range(SUBS):
        out[k] = plane_counts(sending_side(), *own_events(event_cell, event_count, k), out.shape[1:])


def sections(parcel_rows, event_rows, field_rows):
    sizes = [parcel_rows] * 3 + [event_rows] * 2 + [field_rows] * 2
    starts = [sum(sizes[:i]) for i in range(len(sizes) + 1)]
    return [pl.ds(start, size) for start, size in zip(starts, sizes)], starts[-1]


def packed_events(packed, spans, k, width):
    per = width // LANES
    rows = [packed[pl.ds(span.start + k * per + j, 1)] for span in spans for j in range(per)]
    cells, counts = jnp.concatenate(rows[:per], axis=1), jnp.concatenate(rows[per:], axis=1)
    return cells.astype(jnp.int32), counts


def zeros_kernel(out):
    out[...] = jnp.zeros(out.shape, jnp.int32)


def live_kernel(live, zeros, out):
    out[...] = zeros[...] + live[0]


def load_kernel(*refs):
    size, all_weight, cell, event_cell, event_count, field, live, out, weight, active, counts = refs
    active[...] = jnp.where(row_numbers(size.shape) < live[0:1, 0:1], 1.0, 0.0)
    weight[...] = all_weight[...] * active[...]
    events, width = event_cell.shape[1:]
    per = width // LANES
    spans, _ = sections(size.shape[0], events * per, field.shape[1])
    out[spans[0]] = size[...]
    out[spans[1]] = weight[...]
    out[spans[2]] = cell[...].astype(F32)
    for span, array in ((spans[3], event_cell), (spans[4], event_count)):
        values = array[0].astype(F32)
        for k in range(events):
            for j in range(per):
                out[pl.ds(span.start + k * per + j, 1)] = values[k : k + 1, j * LANES : (j + 1) * LANES]
    for j in range(2):
        out[spans[5 + j]] = field[0, :, pl.ds(j * LANES, LANES)]

    @pl.when(lax.axis_index("grp") == 1)
    def _():
        own_counts(event_cell, event_count, counts)


def home_kernel(size, weight, cell, event_cell, event_count, counted, inlet, rows, count, out, counts, *rest):
    kept, sems = rest[:3], rest[3]
    copies = [pltpu.make_async_copy(src, dst, sems.at[i]) for i, (src, dst) in enumerate(zip((inlet, rows, count), kept))]
    for copy in copies:
        copy.start()
    grp = lax.axis_index("grp")

    def own_moments():
        for c, moment in enumerate(plane_moments(sending_side(), size[...], weight[...], cell[...], out.shape[1:])):
            out[c] = moment

    @pl.when(grp == 0)
    def _():
        own_moments()
        own_counts(event_cell, event_count, counts)

    @pl.when(grp == 1)
    def _():
        own_moments()
        counts[...] = counted[...]

    for copy in copies:
        copy.wait()


def substep(field, zeroth, first, second, counts, grown):
    rate = softplus(field - 1.0)
    growth = GROWTH * rate
    taken = growth * (3.0 * second + growth * (3.0 * first + growth * zeroth))
    field = field - (taken + counts * (NUCLEATE * rate))
    second = second + growth * (2.0 * first + growth * zeroth)
    first = first + growth * zeroth
    return field, first, second, grown + growth


def front_kernel(field, home, home_counts, packed, out, state, *, parcel_rows, events):
    plane_shape = out.shape[1:]
    plane = sending_side()
    spans, _ = sections(parcel_rows, events[0] * events[1] // LANES, plane_shape[0])
    cells = packed[spans[2]].astype(jnp.int32)
    zeroth, first, second = plane_moments(plane, packed[spans[0]], packed[spans[1]], cells, plane_shape)
    zeroth, first, second = zeroth + home[0], first + home[1], second + home[2]
    theirs = jnp.concatenate([packed[spans[5]], packed[spans[6]]], axis=1)
    now = jnp.where(sends_other(), theirs, field[0])
    grown = jnp.zeros_like(now)
    for k in range(SUBS):
        counts = home_counts[k] + plane_counts(plane, *packed_events(packed, spans[3:5], k, events[1]), plane_shape)
        now, first, second, grown = substep(now, zeroth, first, second, counts, grown)
    out[0] = now
    for c, value in enumerate((now, zeroth, first, second, grown)):
        state[c] = value


def pack_kernel(state, inlet, out):
    for c in range(5):
        out[c] = state[c]
    out[5] = inlet[0].astype(F32)


def late_kernel(packed, event_cell, event_count, late, *, parcel_rows):
    plane_shape = late.shape[1:]
    events, width = event_cell.shape[1:]
    spans, _ = sections(parcel_rows, events * width // LANES, plane_shape[0])
    for k in range(SUBS):
        mine = own_events(event_cell, event_count, SUBS + k)
        theirs = packed_events(packed, spans[3:5], SUBS + k, width)
        both = [jnp.concatenate(pair, axis=1) for pair in zip(mine, theirs)]
        late[k] = plane_counts(receiving_side(), *both, plane_shape)


def moved(field):
    lines, places = field.shape
    line = lax.broadcasted_iota(jnp.int32, field.shape, 0)
    place = lax.broadcasted_iota(jnp.int32, field.shape, 1)
    total = jnp.where(line == 0, 0.0, pltpu.roll(field, 1, 0))
    total += jnp.where(line == lines - 1, 0.0, pltpu.roll(field, lines - 1, 0))
    total += jnp.where(place == 0, 0.0, pltpu.roll(field, 1, 1))
    total += jnp.where(place == places - 1, 0.0, pltpu.roll(field, places - 1, 1))
    return total


def split_transport(field, other, inlet, side):
    keep = 1.0 - inlet
    field = field + DIFFUSE * (other + moved(field) - 6.0 * field)
    return keep * field + inlet * INLET, jnp.where(has_beside(side), DIFFUSE * keep, 0.0)


def ready_kernel(mine, other, info, their_info, out, hot_place, lists, *, parts):
    now, zeroth, first, second, grown = (jnp.where(ends(), other[c], mine[c]) for c in range(5))
    partner_field = jnp.where(ends(), mine[0], other[0])
    inlet = jnp.where(receives_other(), other[5], mine[5])
    base, slope = split_transport(now, partner_field, inlet, receiving_side())
    for c, value in enumerate((base, slope, zeroth, first, second, grown)):
        out[c] = value
    half = info.shape[0] // 2
    rows = by_owner(info[pl.ds(half, half)], their_info[pl.ds(0, half)], parts)
    lists[0:1] = jnp.concatenate(rows(2), axis=1) - (receiving_side() * base.shape[0]).astype(F32)
    lists[1:2] = jnp.concatenate(rows(4), axis=1)
    hot_place[...] = hot(base.shape[1], jnp.concatenate(rows(3), axis=1).astype(jnp.int32))


def second_substeps(beside, ready, late):
    base, slope, zeroth, first, second, grown = (ready[c] for c in range(6))
    now = base + slope * beside[0]
    for k in range(SUBS):
        now, first, second, grown = substep(now, zeroth, first, second, late[k], grown)
    return now, grown


def second_kernel(beside, ready, late, hot_place, lists, out, *, parts):
    _, grown = second_substeps(beside, ready, late)
    stacked = jnp.concatenate(pieces(grown), axis=0)
    found = picked_growth(stacked, hot_place[...], lists[0:1].astype(jnp.int32)) * lists[1:2]
    places = grown.shape[1]
    for i in range(2 * parts):
        out[i : i + 1] = found[:, i * places : (i + 1) * places]
    out[2 * parts :] = jnp.zeros((out.shape[0] - 2 * parts, places), F32)


def migrants_kernel(size, weight, cell, rows, count, out, *, places):
    side = receiving_side()
    table_rows = size.shape[0]
    slots = rows.shape[2]
    table, nothing = [], jnp.zeros(size.shape, BF16)
    for values in (size[...], weight[...]):
        stack, rest = [], values
        for _ in range(3):
            part = rest.astype(BF16)
            rest = rest - part.astype(F32)
            stack.append(part)
        table.append(jnp.concatenate(stack, axis=0))
    cells = cell[...]
    for values in (cells // places, cells % places):
        table.append(jnp.concatenate([values.astype(F32).astype(BF16), nothing, nothing], axis=0))
    table = jnp.concatenate(table, axis=1)
    slot = lax.broadcasted_iota(jnp.int32, (1, slots), 1)
    half = out.shape[0] // 2
    for block, j in ((0, side), (half, 1 - side)):
        row = jnp.where(j == 0, rows[0, 0:1, :], rows[0, 1:2, :])
        used = jnp.where(j == 0, count[0:1, 0:1], count[0:1, 1:2])
        valid = jnp.where(slot < used, 1.0, 0.0)
        hot_row = jnp.concatenate([hot(table_rows, row // LANES)] * 3, axis=0)
        picked = lax.dot_general(table, hot_row, TN, preferred_element_type=F32)
        hot_lane = hot(LANES, row % LANES).astype(F32)
        found = [jnp.sum(picked[c * LANES : (c + 1) * LANES] * hot_lane, axis=0, keepdims=True) for c in range(4)]
        sizes, weights = found[0] * valid, found[1] * valid
        at = block
        for value in (sizes, weights, found[2], found[3], valid):
            for start in range(0, slots, places):
                out[at : at + 1] = value[:, start : start + places]
                at += 1
        out[at : block + half] = jnp.zeros((block + half - at, places), F32)


def picked_growth(stacked, hot_place, line):
    lines = stacked.shape[0] // 2
    picked = lax.dot_general(stacked, hot_place, NN, preferred_element_type=F32)
    picked = picked[:lines] + picked[lines:]
    index = lax.broadcasted_iota(jnp.int32, picked.shape, 0)
    return jnp.sum(jnp.where(index == line, picked, 0.0), axis=0, keepdims=True)


def grown_at(stacked, line, place):
    return picked_growth(stacked, hot(stacked.shape[1], place), line)


def both_planes(mine, other):
    first = receiving_side() == 0
    low = jnp.where(first, mine, other)
    high = jnp.where(first, other, mine)
    return jnp.concatenate(pieces(jnp.concatenate([low, high], axis=0)), axis=0)


def by_owner(mine, partners, parts):
    first = lax.axis_index("grp") == 0
    blocks = [jnp.where(first, one, other) for one, other in ((mine, partners), (partners, mine))]
    return lambda c: [block[i : i + 1] for block in blocks for i in range(c * parts, (c + 1) * parts)]


def plane_growth(grown, rows, parts):
    lines, places = grown.shape
    stacked = jnp.concatenate(pieces(grown), axis=0)
    line = jnp.concatenate(rows(2), axis=1).astype(jnp.int32) - receiving_side() * lines
    found = grown_at(stacked, line, jnp.concatenate(rows(3), axis=1).astype(jnp.int32))
    valid = rows(4)
    return [found[:, i * places : (i + 1) * places] * valid[i] for i in range(2 * parts)]


def own_kernel(beside, ready, late, info, their_info, out, front, total, *, parts):
    front[0], total[0] = second_substeps(beside, ready, late)
    half = info.shape[0] // 2
    rows = by_owner(info[pl.ds(0, half)], their_info[pl.ds(half, half)], parts)
    found = plane_growth(total[0], rows, parts)
    sizes, weights = rows(0), rows(1)
    for i in range(2 * parts):
        at = (i // parts) * 2 * parts + i % parts
        out[at : at + 1] = sizes[i] + found[i]
        out[at + parts : at + parts + 1] = weights[i]


def leaving_kernel(front, own, theirs, out, *, parts):
    lines = front.shape[1]
    out[pl.ds(0, lines)] = front[0]
    for j in range(2):
        at = 2 * parts * j
        out[lines + at : lines + at + parts] = own[at : at + parts] + theirs[j * parts : (j + 1) * parts]
        out[lines + at + parts : lines + at + 2 * parts] = own[at + parts : at + 2 * parts]


def sizes_kernel(total, their_total, size, cell, active, out):
    places = total.shape[2]
    stacked = both_planes(total[0], their_total[0])
    cells = cell[...]
    line = cells // places
    place = cells % places
    group = 4
    found = []
    for start in range(0, size.shape[0], group):
        each = range(start, start + group)
        grown = grown_at(
            stacked,
            jnp.concatenate([line[r : r + 1] for r in each], axis=1),
            jnp.concatenate([place[r : r + 1] for r in each], axis=1),
        )
        found += [grown[:, i * LANES : (i + 1) * LANES] for i in range(group)]
    grown = jnp.concatenate(found, axis=0)
    out[...] = active[...] * (size[...] + grown)


def rest_kernel(front, their_front, inlet, out):
    other = receives_other()
    field = jnp.where(other, their_front[0], front[0])
    beyond = jnp.where(other, front[0], their_front[0])
    out[0], out[1] = split_transport(field, beyond, inlet[0].astype(F32), lax.axis_index("grp"))


def last_kernel(rest, received, relayed, field_out, arrivals_out, *, lines, parts):
    slab, grp = lax.axis_index("slab"), lax.axis_index("grp")
    here = pl.ds(0, lines)
    field_out[0] = rest[0] + rest[1] * jnp.where(sends_other(), relayed[here], received[here])
    rows = 2 * parts
    pick = lambda block: jnp.where(grp == 0, block[lines : lines + rows], block[lines + rows : lines + 2 * rows])
    mine, theirs = pick(received), pick(relayed)
    from_lower = sending_side() == 0
    lower = jnp.where(slab > 0, jnp.where(from_lower, mine, theirs), 0.0)
    upper = jnp.where(slab < lax.axis_size("slab") - 1, jnp.where(from_lower, theirs, mine), 0.0)
    places = mine.shape[1]
    for side, value in enumerate((lower, upper)):
        for v in range(2):
            for p in range(parts):
                at = v * parts + p
                arrivals_out[0, side, v : v + 1, pl.ds(p * places, places)] = value[at : at + 1]


VMEM = pl.BlockSpec(memory_space=pltpu.VMEM)
SMEM = pl.BlockSpec(memory_space=pltpu.SMEM)
HBM = pl.BlockSpec(memory_space=pltpu.HBM)


def shape(*dims):
    return jax.ShapeDtypeStruct(dims, F32)


def call(kernel, out_shape, *args, name, cost=0, limit=16, scratch=(), specs=None):
    return pl.pallas_call(
        kernel,
        out_shape=out_shape,
        in_specs=specs or [VMEM] * len(args),
        out_specs=jax.tree.map(lambda _: VMEM, out_shape),
        scratch_shapes=scratch,
        compiler_params=pltpu.CompilerParams(vmem_limit_bytes=limit << 20),
        cost_estimate=pl.CostEstimate(flops=cost, bytes_accessed=0, transcendentals=0) if cost else None,
        name=name,
    )(*args)


def local(
    saturation,
    inlet_mask,
    crystal_size,
    crystal_weight,
    crystal_cell,
    live_count,
    nucleus_cell,
    nucleus_count,
    migrant_rows,
    migrant_count,
):
    lines, places = saturation.shape[1:]
    slots = migrant_rows.shape[2]
    parts = slots // places
    swap = lambda value: lax.ppermute(value, "grp", [(0, 1), (1, 0)])
    slabs = lax.axis_size("slab")
    across = lambda value, second: lax.ppermute(value, ("slab", "grp"), across_pairs(slabs, second))

    hbm = lambda a: pltpu.with_memory_space_constraint(a, pltpu.HBM)
    like = lambda a: jax.ShapeDtypeStruct(a.shape, a.dtype)
    inputs = [a.reshape(-1, LANES) for a in (crystal_size, crystal_weight, crystal_cell)]
    inputs += [nucleus_cell, nucleus_count, saturation]
    others = [inlet_mask, migrant_rows, migrant_count]
    parcel_rows, events = inputs[0].shape[0], nucleus_cell.shape[1:]
    _, packed_rows = sections(parcel_rows, events[0] * events[1] // LANES, lines)
    tile = jax.ShapeDtypeStruct((8, LANES), jnp.int32)
    zeros = call(zeros_kernel, tile, cost=1 << 30, name="zeros")
    live = call(live_kernel, tile, live_count, zeros, specs=[SMEM, VMEM], name="live")
    size, _, cell, event_cell, event_count, field = inputs
    packed, weight, active, counted = call(
        load_kernel,
        [shape(packed_rows, LANES), shape(*size.shape), shape(*size.shape), shape(SUBS, lines, places)],
        *inputs, live, name="load",
    )
    packed = swap(packed)
    home, counts, inlet, rows, count = call(
        home_kernel, [shape(3, lines, places), shape(SUBS, lines, places)] + [like(a) for a in others],
        size, weight, cell, event_cell, event_count, counted, *[hbm(a) for a in others],
        specs=[VMEM] * 6 + [HBM] * 3, scratch=[pltpu.SemaphoreType.DMA((3,))],
        cost=1 << 30, name="home",
    )
    front, state = call(
        functools.partial(front_kernel, parcel_rows=parcel_rows, events=events),
        (shape(1, lines, places), shape(5, lines, places)), field, home, counts, packed, name="front",
    )
    beside = across(front, False)
    _, state = lax.optimization_barrier((front, state))
    mine = call(pack_kernel, shape(6, lines, places), state, inlet, cost=1 << 28, name="pack")
    other = swap(mine)
    info = call(
        functools.partial(migrants_kernel, places=places), shape(32, places), size, weight, cell, rows, count,
        cost=1 << 33, name="migrants",
    )
    their_info = swap(info)
    late = call(
        functools.partial(late_kernel, parcel_rows=parcel_rows), shape(SUBS, lines, places),
        packed, event_cell, event_count, cost=1 << 28, name="late",
    )
    info, late = lax.optimization_barrier((info, late))
    ready, hot_place, lists = call(
        functools.partial(ready_kernel, parts=parts),
        (shape(6, lines, places), jax.ShapeDtypeStruct((places, 2 * slots), BF16), shape(8, 2 * slots)),
        mine, other, info, their_info, cost=1 << 26, name="ready",
    )
    given = call(
        functools.partial(second_kernel, parts=parts), shape(8, places), beside, ready, late, hot_place, lists,
        name="second",
    )
    theirs = swap(given)
    own, front, total = call(
        functools.partial(own_kernel, parts=parts),
        (shape(4 * parts, places), shape(1, lines, places), shape(1, lines, places)),
        beside, ready, late, info, their_info, cost=1 << 28, name="own",
    )
    leaving = call(
        functools.partial(leaving_kernel, parts=parts), shape(lines + 4 * parts, places), front, own, theirs, name="leaving"
    )
    received = across(leaving, True)
    _, later = lax.optimization_barrier((leaving, total))
    their_total, their_front = swap(later), swap(front)
    size_out = call(
        sizes_kernel, shape(*size.shape), total, their_total, size, cell, active, cost=1 << 26, name="sizes",
    )
    received, size_out = lax.optimization_barrier((received, size_out))
    relayed = swap(received)
    rest = call(rest_kernel, shape(2, lines, places), front, their_front, inlet, cost=1 << 28, name="rest")
    field_out, arrivals = call(
        functools.partial(last_kernel, lines=lines, parts=parts),
        (shape(1, lines, places), shape(1, 2, 2, slots)), rest, received, relayed, name="last",
    )
    return (field_out, size_out.reshape(-1), arrivals)


def solution(mesh):
    in_specs = (
        P(("slab", "grp"), None, None),
        P(("slab", "grp"), None, None),
        P(("slab", "grp")),
        P(("slab", "grp")),
        P(("slab", "grp")),
        P(("slab", "grp")),
        P(("slab", "grp"), None, None),
        P(("slab", "grp"), None, None),
        P(("slab", "grp"), None, None),
        P(("slab", "grp"), None),
    )
    out_specs = (
        P(("slab", "grp"), None, None),
        P(("slab", "grp")),
        P(("slab", "grp"), None, None, None),
    )
    return jax.shard_map(local, mesh=mesh, in_specs=in_specs, out_specs=out_specs, check_vma=False)
```

```python
import functools

import jax
import jax.numpy as jnp
from jax import lax
from jax.experimental import pallas as pl
from jax.experimental.pallas import tpu as pltpu
from jax.sharding import PartitionSpec as P

STEPS = 2
SUBS = 2

GROWTH = 0.08
NUCLEATE = 0.02
DIFFUSE = 0.12
INLET = 4.0

LANES = 128
F32 = jnp.float32
BF16 = jnp.bfloat16
NT = (((1,), (1,)), ((), ()))
NN = (((1,), (0,)), ((), ()))
TN = (((0,), (0,)), ((), ()))


def softplus(x):
    return jnp.maximum(x, 0.0) + jnp.log(1.0 + jnp.exp(-jnp.abs(x)))


def pieces(x):
    high = x.astype(BF16)
    return high, (x - high.astype(F32)).astype(BF16)


def hot(count, row):
    index = lax.broadcasted_iota(jnp.int32, (count, row.shape[1]), 0)
    return jnp.where(index == row, 1.0, 0.0).astype(BF16)


def row_numbers(shape):
    return lax.broadcasted_iota(jnp.int32, shape, 0) * LANES + lax.broadcasted_iota(jnp.int32, shape, 1)


def ends():
    slab = lax.axis_index("slab")
    return (slab == 0) | (slab == lax.axis_size("slab") - 1)


def sends_other():
    return ends() | (lax.axis_index("slab") % 2 == 0)


def receives_other():
    return (lax.axis_index("slab") % 2 == 0) & ~ends()


def sending_side():
    grp = lax.axis_index("grp")
    return jnp.where(sends_other(), 1 - grp, grp)


def receiving_side():
    grp = lax.axis_index("grp")
    return jnp.where(receives_other(), 1 - grp, grp)


def has_beside(side):
    slab = lax.axis_index("slab")
    return jnp.where(side == 0, slab > 0, slab < lax.axis_size("slab") - 1)


def across_pairs(slabs, second):
    last, first_out = slabs - 1, 1 if second else 0
    up_out = lambda s: first_out if s == 0 else s % 2
    up_in = lambda s: 1 - first_out if s == 0 else s % 2
    down_out = lambda s: 1 - first_out if s == last else 1 - s % 2
    down_in = lambda s: first_out if s == last else 1 - s % 2
    pairs = [(s * 2 + up_out(s), (s + 1) * 2 + down_in(s + 1)) for s in range(last)]
    pairs += [((s + 1) * 2 + down_out(s + 1), s * 2 + up_in(s)) for s in range(last)]
    closing = [(1 - first_out, first_out), (last * 2 + first_out, last * 2 + 1 - first_out)]
    return pairs + closing


def plane_moments(plane, sizes, weights, cells, plane_shape):
    lines, places = plane_shape
    first = weights * sizes
    parts = [part.astype(F32) for moment in (weights, first, first * sizes) for part in pieces(moment)]
    line = cells // places - plane * lines
    place = cells % places
    group = 4
    sums = jnp.zeros((len(parts) * lines, places), F32)
    for start in range(0, sizes.shape[0], group):
        left, right = [], []
        for r in range(start, start + group):
            hot_line = hot(lines, line[r : r + 1])
            left.append(jnp.concatenate([hot_line * part[r : r + 1].astype(BF16) for part in parts], axis=0))
            right.append(hot(places, place[r : r + 1]))
        left, right = jnp.concatenate(left, axis=1), jnp.concatenate(right, axis=1)
        sums = sums + lax.dot_general(left, right, NT, preferred_element_type=F32)
    return [sums[2 * c * lines : (2 * c + 1) * lines] + sums[(2 * c + 1) * lines : (2 * c + 2) * lines] for c in range(3)]


def plane_counts(plane, cells, counts, plane_shape):
    lines, places = plane_shape
    left = hot(lines, cells // places - plane * lines) * counts.astype(BF16)
    return lax.dot_general(left, hot(places, cells % places), NT, preferred_element_type=F32)


def own_events(event_cell, event_count, k):
    row = pl.ds(k, 1)
    return event_cell[0, row, :], event_count[0, row, :].astype(F32)


def own_counts(event_cell, event_count, out):
    for k in range(SUBS):
        out[k] = plane_counts(sending_side(), *own_events(event_cell, event_count, k), out.shape[1:])


def sections(parcel_rows, event_rows, field_rows):
    sizes = [parcel_rows] * 3 + [event_rows] * 2 + [field_rows] * 2
    starts = [sum(sizes[:i]) for i in range(len(sizes) + 1)]
    return [pl.ds(start, size) for start, size in zip(starts, sizes)], starts[-1]


def packed_events(packed, spans, k, width):
    per = width // LANES
    events = spans[0].size // per
    rows = [packed[pl.ds(span.start + j * events + k, 1)] for span in spans for j in range(per)]
    cells, counts = jnp.concatenate(rows[:per], axis=1), jnp.concatenate(rows[per:], axis=1)
    return cells.astype(jnp.int32), counts


def zeros_kernel(out):
    out[...] = jnp.zeros(out.shape, jnp.int32)


def live_kernel(live, zeros, out):
    out[...] = zeros[...] + live[0]


def load_kernel(*refs):
    size, all_weight, cell, event_cell, event_count, field, live, out, weight, active, counts = refs
    active[...] = jnp.where(row_numbers(size.shape) < live[0:1, 0:1], 1.0, 0.0)
    weight[...] = all_weight[...] * active[...]
    events, width = event_cell.shape[1:]
    per = width // LANES
    spans, _ = sections(size.shape[0], events * per, field.shape[1])
    out[spans[0]] = size[...]
    out[spans[1]] = weight[...]
    out[spans[2]] = cell[...].astype(F32)
    for span, array in ((spans[3], event_cell), (spans[4], event_count)):
        values = array[0].astype(F32)
        for j in range(per):
            out[pl.ds(span.start + j * events, events)] = values[:, j * LANES : (j + 1) * LANES]
    for j in range(2):
        out[spans[5 + j]] = field[0, :, pl.ds(j * LANES, LANES)]

    @pl.when(lax.axis_index("grp") == 1)
    def _():
        own_counts(event_cell, event_count, counts)


def home_kernel(size, weight, cell, event_cell, event_count, counted, inlet, rows, count, out, counts, *rest):
    kept, sems = rest[:3], rest[3]
    copies = [pltpu.make_async_copy(src, dst, sems.at[i]) for i, (src, dst) in enumerate(zip((inlet, rows, count), kept))]
    for copy in copies:
        copy.start()
    grp = lax.axis_index("grp")

    def own_moments():
        for c, moment in enumerate(plane_moments(sending_side(), size[...], weight[...], cell[...], out.shape[1:])):
            out[c] = moment

    @pl.when(grp == 0)
    def _():
        own_moments()
        own_counts(event_cell, event_count, counts)

    @pl.when(grp == 1)
    def _():
        own_moments()
        counts[...] = counted[...]

    for copy in copies:
        copy.wait()


def substep(field, zeroth, first, second, counts, grown):
    rate = softplus(field - 1.0)
    growth = GROWTH * rate
    linear = growth * zeroth
    inner = first + linear
    field = field - (growth * (second + growth * inner) + counts * (NUCLEATE * rate))
    second = second + growth * (inner + inner + linear)
    return field, first + 3.0 * linear, second, grown + growth


def front_kernel(field, home, home_counts, packed, out, state, *, parcel_rows, events):
    plane_shape = out.shape[1:]
    plane = sending_side()
    spans, _ = sections(parcel_rows, events[0] * events[1] // LANES, plane_shape[0])
    cells = packed[spans[2]].astype(jnp.int32)
    zeroth, first, second = plane_moments(plane, packed[spans[0]], packed[spans[1]], cells, plane_shape)
    zeroth, first, second = zeroth + home[0], 3.0 * (first + home[1]), 3.0 * (second + home[2])
    theirs = jnp.concatenate([packed[spans[5]], packed[spans[6]]], axis=1)
    now = jnp.where(sends_other(), theirs, field[0])
    grown = jnp.zeros_like(now)
    for k in range(SUBS):
        counts = home_counts[k] + plane_counts(plane, *packed_events(packed, spans[3:5], k, events[1]), plane_shape)
        now, first, second, grown = substep(now, zeroth, first, second, counts, grown)
    out[0] = now
    for c, value in enumerate((now, zeroth, first, second, grown)):
        state[c] = value


def pack_kernel(state, inlet, out):
    for c in range(5):
        out[c] = state[c]
    out[5] = inlet[0].astype(F32)


def late_kernel(packed, event_cell, event_count, late, *, parcel_rows):
    plane_shape = late.shape[1:]
    events, width = event_cell.shape[1:]
    spans, _ = sections(parcel_rows, events * width // LANES, plane_shape[0])
    for k in range(SUBS):
        mine = own_events(event_cell, event_count, SUBS + k)
        theirs = packed_events(packed, spans[3:5], SUBS + k, width)
        both = [jnp.concatenate(pair, axis=1) for pair in zip(mine, theirs)]
        late[k] = plane_counts(receiving_side(), *both, plane_shape)


def moved(field):
    lines, places = field.shape
    line = lax.broadcasted_iota(jnp.int32, field.shape, 0)
    place = lax.broadcasted_iota(jnp.int32, field.shape, 1)
    total = jnp.where(line == 0, 0.0, pltpu.roll(field, 1, 0))
    total += jnp.where(line == lines - 1, 0.0, pltpu.roll(field, lines - 1, 0))
    total += jnp.where(place == 0, 0.0, pltpu.roll(field, 1, 1))
    total += jnp.where(place == places - 1, 0.0, pltpu.roll(field, places - 1, 1))
    return total


def split_transport(field, other, inlet, side):
    keep = 1.0 - inlet
    field = field + DIFFUSE * (other + moved(field) - 6.0 * field)
    return keep * field + inlet * INLET, jnp.where(has_beside(side), DIFFUSE * keep, 0.0)


def ready_kernel(mine, other, info, their_info, out, hot_place, lists, *, parts):
    now, zeroth, first, second, grown = (jnp.where(ends(), other[c], mine[c]) for c in range(5))
    partner_field = jnp.where(ends(), mine[0], other[0])
    inlet = jnp.where(receives_other(), other[5], mine[5])
    base, slope = split_transport(now, partner_field, inlet, receiving_side())
    for c, value in enumerate((base, slope, zeroth, first, second, grown)):
        out[c] = value
    half = info.shape[0] // 2
    rows = by_owner(info[pl.ds(half, half)], their_info[pl.ds(0, half)], parts)
    lists[0:1] = jnp.concatenate(rows(2), axis=1) - (receiving_side() * base.shape[0]).astype(F32)
    lists[1:2] = jnp.concatenate(rows(4), axis=1)
    hot_place[...] = hot(base.shape[1], jnp.concatenate(rows(3), axis=1).astype(jnp.int32))


def second_substeps(beside, ready, late):
    base, slope, zeroth, first, second, grown = (ready[c] for c in range(6))
    now = base + slope * beside[0]
    for k in range(SUBS):
        now, first, second, grown = substep(now, zeroth, first, second, late[k], grown)
    return now, grown


def second_kernel(beside, ready, late, hot_place, lists, out, *, parts):
    _, grown = second_substeps(beside, ready, late)
    stacked = jnp.concatenate(pieces(grown), axis=0)
    found = picked_growth(stacked, hot_place[...], lists[0:1].astype(jnp.int32)) * lists[1:2]
    places = grown.shape[1]
    for i in range(2 * parts):
        out[i : i + 1] = found[:, i * places : (i + 1) * places]
    out[2 * parts :] = jnp.zeros((out.shape[0] - 2 * parts, places), F32)


def migrants_kernel(size, weight, cell, rows, count, out, *, places):
    side = receiving_side()
    table_rows = size.shape[0]
    slots = rows.shape[2]
    table, nothing = [], jnp.zeros(size.shape, BF16)
    for values in (size[...], weight[...]):
        stack, rest = [], values
        for _ in range(3):
            part = rest.astype(BF16)
            rest = rest - part.astype(F32)
            stack.append(part)
        table.append(jnp.concatenate(stack, axis=0))
    cells = cell[...]
    for values in (cells // places, cells % places):
        table.append(jnp.concatenate([values.astype(F32).astype(BF16), nothing, nothing], axis=0))
    table = jnp.concatenate(table, axis=1)
    slot = lax.broadcasted_iota(jnp.int32, (1, slots), 1)
    half = out.shape[0] // 2
    for block, j in ((0, side), (half, 1 - side)):
        row = jnp.where(j == 0, rows[0, 0:1, :], rows[0, 1:2, :])
        used = jnp.where(j == 0, count[0:1, 0:1], count[0:1, 1:2])
        valid = jnp.where(slot < used, 1.0, 0.0)
        hot_row = jnp.concatenate([hot(table_rows, row // LANES)] * 3, axis=0)
        picked = lax.dot_general(table, hot_row, TN, preferred_element_type=F32)
        hot_lane = hot(LANES, row % LANES).astype(F32)
        found = [jnp.sum(picked[c * LANES : (c + 1) * LANES] * hot_lane, axis=0, keepdims=True) for c in range(4)]
        sizes, weights = found[0] * valid, found[1] * valid
        at = block
        for value in (sizes, weights, found[2], found[3], valid):
            for start in range(0, slots, places):
                out[at : at + 1] = value[:, start : start + places]
                at += 1
        out[at : block + half] = jnp.zeros((block + half - at, places), F32)


def picked_growth(stacked, hot_place, line):
    lines = stacked.shape[0] // 2
    picked = lax.dot_general(stacked, hot_place, NN, preferred_element_type=F32)
    picked = picked[:lines] + picked[lines:]
    index = lax.broadcasted_iota(jnp.int32, picked.shape, 0)
    return jnp.sum(jnp.where(index == line, picked, 0.0), axis=0, keepdims=True)


def grown_at(stacked, line, place):
    return picked_growth(stacked, hot(stacked.shape[1], place), line)


def both_planes(mine, other):
    first = receiving_side() == 0
    low = jnp.where(first, mine, other)
    high = jnp.where(first, other, mine)
    return jnp.concatenate(pieces(jnp.concatenate([low, high], axis=0)), axis=0)


def by_owner(mine, partners, parts):
    first = lax.axis_index("grp") == 0
    blocks = [jnp.where(first, one, other) for one, other in ((mine, partners), (partners, mine))]
    return lambda c: [block[i : i + 1] for block in blocks for i in range(c * parts, (c + 1) * parts)]


def plane_growth(grown, rows, parts):
    lines, places = grown.shape
    stacked = jnp.concatenate(pieces(grown), axis=0)
    line = jnp.concatenate(rows(2), axis=1).astype(jnp.int32) - receiving_side() * lines
    found = grown_at(stacked, line, jnp.concatenate(rows(3), axis=1).astype(jnp.int32))
    valid = rows(4)
    return [found[:, i * places : (i + 1) * places] * valid[i] for i in range(2 * parts)]


def own_kernel(beside, ready, late, info, their_info, out, front, total, *, parts):
    front[0], total[0] = second_substeps(beside, ready, late)
    half = info.shape[0] // 2
    rows = by_owner(info[pl.ds(0, half)], their_info[pl.ds(half, half)], parts)
    found = plane_growth(total[0], rows, parts)
    sizes, weights = rows(0), rows(1)
    for i in range(2 * parts):
        at = (i // parts) * 2 * parts + i % parts
        out[at : at + 1] = sizes[i] + found[i]
        out[at + parts : at + parts + 1] = weights[i]


def leaving_kernel(front, own, theirs, out, *, parts):
    lines = front.shape[1]
    out[pl.ds(0, lines)] = front[0]
    for j in range(2):
        at = 2 * parts * j
        out[lines + at : lines + at + parts] = own[at : at + parts] + theirs[j * parts : (j + 1) * parts]
        out[lines + at + parts : lines + at + 2 * parts] = own[at + parts : at + 2 * parts]


def sizes_kernel(total, their_total, size, cell, active, out):
    places = total.shape[2]
    stacked = both_planes(total[0], their_total[0])
    cells = cell[...]
    line = cells // places
    place = cells % places
    group = 4
    found = []
    for start in range(0, size.shape[0], group):
        each = range(start, start + group)
        grown = grown_at(
            stacked,
            jnp.concatenate([line[r : r + 1] for r in each], axis=1),
            jnp.concatenate([place[r : r + 1] for r in each], axis=1),
        )
        found += [grown[:, i * LANES : (i + 1) * LANES] for i in range(group)]
    grown = jnp.concatenate(found, axis=0)
    out[...] = active[...] * (size[...] + grown)


def rest_kernel(front, their_front, inlet, out):
    other = receives_other()
    field = jnp.where(other, their_front[0], front[0])
    beyond = jnp.where(other, front[0], their_front[0])
    out[0], out[1] = split_transport(field, beyond, inlet[0].astype(F32), lax.axis_index("grp"))


def last_kernel(rest, received, relayed, field_out, arrivals_out, *, lines, parts):
    slab, grp = lax.axis_index("slab"), lax.axis_index("grp")
    here = pl.ds(0, lines)
    field_out[0] = rest[0] + rest[1] * jnp.where(sends_other(), relayed[here], received[here])
    rows = 2 * parts
    pick = lambda block: jnp.where(grp == 0, block[lines : lines + rows], block[lines + rows : lines + 2 * rows])
    mine, theirs = pick(received), pick(relayed)
    from_lower = sending_side() == 0
    lower = jnp.where(slab > 0, jnp.where(from_lower, mine, theirs), 0.0)
    upper = jnp.where(slab < lax.axis_size("slab") - 1, jnp.where(from_lower, theirs, mine), 0.0)
    places = mine.shape[1]
    for side, value in enumerate((lower, upper)):
        for v in range(2):
            for p in range(parts):
                at = v * parts + p
                arrivals_out[0, side, v : v + 1, pl.ds(p * places, places)] = value[at : at + 1]


VMEM = pl.BlockSpec(memory_space=pltpu.VMEM)
SMEM = pl.BlockSpec(memory_space=pltpu.SMEM)
HBM = pl.BlockSpec(memory_space=pltpu.HBM)


def shape(*dims):
    return jax.ShapeDtypeStruct(dims, F32)


def call(kernel, out_shape, *args, name, cost=0, limit=16, scratch=(), specs=None):
    return pl.pallas_call(
        kernel,
        out_shape=out_shape,
        in_specs=specs or [VMEM] * len(args),
        out_specs=jax.tree.map(lambda _: VMEM, out_shape),
        scratch_shapes=scratch,
        compiler_params=pltpu.CompilerParams(vmem_limit_bytes=limit << 20),
        cost_estimate=pl.CostEstimate(flops=cost, bytes_accessed=0, transcendentals=0) if cost else None,
        name=name,
    )(*args)


def local(
    saturation,
    inlet_mask,
    crystal_size,
    crystal_weight,
    crystal_cell,
    live_count,
    nucleus_cell,
    nucleus_count,
    migrant_rows,
    migrant_count,
):
    lines, places = saturation.shape[1:]
    slots = migrant_rows.shape[2]
    parts = slots // places
    swap = lambda value: lax.ppermute(value, "grp", [(0, 1), (1, 0)])
    slabs = lax.axis_size("slab")
    across = lambda value, second: lax.ppermute(value, ("slab", "grp"), across_pairs(slabs, second))

    hbm = lambda a: pltpu.with_memory_space_constraint(a, pltpu.HBM)
    like = lambda a: jax.ShapeDtypeStruct(a.shape, a.dtype)
    inputs = [a.reshape(-1, LANES) for a in (crystal_size, crystal_weight, crystal_cell)]
    inputs += [nucleus_cell, nucleus_count, saturation]
    others = [inlet_mask, migrant_rows, migrant_count]
    parcel_rows, events = inputs[0].shape[0], nucleus_cell.shape[1:]
    _, packed_rows = sections(parcel_rows, events[0] * events[1] // LANES, lines)
    tile = jax.ShapeDtypeStruct((8, LANES), jnp.int32)
    zeros = call(zeros_kernel, tile, cost=1 << 30, name="zeros")
    live = call(live_kernel, tile, live_count, zeros, specs=[SMEM, VMEM], name="live")
    size, _, cell, event_cell, event_count, field = inputs
    packed, weight, active, counted = call(
        load_kernel,
        [shape(packed_rows, LANES), shape(*size.shape), shape(*size.shape), shape(SUBS, lines, places)],
        *inputs, live, name="load",
    )
    packed = swap(packed)
    home, counts, inlet, rows, count = call(
        home_kernel, [shape(3, lines, places), shape(SUBS, lines, places)] + [like(a) for a in others],
        size, weight, cell, event_cell, event_count, counted, *[hbm(a) for a in others],
        specs=[VMEM] * 6 + [HBM] * 3, scratch=[pltpu.SemaphoreType.DMA((3,))],
        cost=1 << 30, name="home",
    )
    front, state = call(
        functools.partial(front_kernel, parcel_rows=parcel_rows, events=events),
        (shape(1, lines, places), shape(5, lines, places)), field, home, counts, packed, name="front",
    )
    beside = across(front, False)
    _, state = lax.optimization_barrier((front, state))
    mine = call(pack_kernel, shape(6, lines, places), state, inlet, cost=1 << 28, name="pack")
    other = swap(mine)
    info = call(
        functools.partial(migrants_kernel, places=places), shape(32, places), size, weight, cell, rows, count,
        cost=1 << 33, name="migrants",
    )
    their_info = swap(info)
    late = call(
        functools.partial(late_kernel, parcel_rows=parcel_rows), shape(SUBS, lines, places),
        packed, event_cell, event_count, cost=1 << 28, name="late",
    )
    info, late = lax.optimization_barrier((info, late))
    ready, hot_place, lists = call(
        functools.partial(ready_kernel, parts=parts),
        (shape(6, lines, places), jax.ShapeDtypeStruct((places, 2 * slots), BF16), shape(8, 2 * slots)),
        mine, other, info, their_info, cost=1 << 26, name="ready",
    )
    given = call(
        functools.partial(second_kernel, parts=parts), shape(8, places), beside, ready, late, hot_place, lists,
        name="second",
    )
    theirs = swap(given)
    own, front, total = call(
        functools.partial(own_kernel, parts=parts),
        (shape(4 * parts, places), shape(1, lines, places), shape(1, lines, places)),
        beside, ready, late, info, their_info, cost=1 << 28, name="own",
    )
    leaving = call(
        functools.partial(leaving_kernel, parts=parts), shape(lines + 4 * parts, places), front, own, theirs, name="leaving"
    )
    received = across(leaving, True)
    _, later = lax.optimization_barrier((leaving, total))
    their_total, their_front = swap(later), swap(front)
    size_out = call(
        sizes_kernel, shape(*size.shape), total, their_total, size, cell, active, cost=1 << 26, name="sizes",
    )
    received, size_out = lax.optimization_barrier((received, size_out))
    relayed = swap(received)
    rest = call(rest_kernel, shape(2, lines, places), front, their_front, inlet, cost=1 << 28, name="rest")
    field_out, arrivals = call(
        functools.partial(last_kernel, lines=lines, parts=parts),
        (shape(1, lines, places), shape(1, 2, 2, slots)), rest, received, relayed, name="last",
    )
    return (field_out, size_out.reshape(-1), arrivals)


def solution(mesh):
    in_specs = (
        P(("slab", "grp"), None, None),
        P(("slab", "grp"), None, None),
        P(("slab", "grp")),
        P(("slab", "grp")),
        P(("slab", "grp")),
        P(("slab", "grp")),
        P(("slab", "grp"), None, None),
        P(("slab", "grp"), None, None),
        P(("slab", "grp"), None, None),
        P(("slab", "grp"), None),
    )
    out_specs = (
        P(("slab", "grp"), None, None),
        P(("slab", "grp")),
        P(("slab", "grp"), None, None, None),
    )
    return jax.shard_map(local, mesh=mesh, in_specs=in_specs, out_specs=out_specs, check_vma=False)
```
